32 devices in a mesh: sample: 2 (over x), depth: 16 (over z, y, core).
Axes of the slice: x: 2, y: 2, z: 4, core: 2. Of those that a mesh axis runs over, the one named last changes fastest.
Arguments:
- volume: bfloat16 [2, 16, 32, 2048], P('sample', 'depth'), may hold values from -6 to 6
- conv1_weight: bfloat16 [27, 64, 64], replicated, may hold values from -0.15625 to 0.15625
- conv2_weight: bfloat16 [27, 1024, 1024], P(None, 'depth'), may hold values from -0.0390625 to 0.0390625
- cotangent: bfloat16 [2, 16, 8, 8, 1024], P('sample', 'depth'), may hold values from -6 to 6
Outputs:
- features_out: bfloat16 [2, 16, 8, 8, 1024], P('sample', 'depth')
- grad_volume: bfloat16 [2, 16, 32, 2048], P('sample', 'depth')
- grad_conv1: float32 [27, 64, 64], replicated
- grad_conv2: float32 [27, 1024, 1024], P(None, 'depth')
The draws below stay inside these ranges and needn't reach their ends.
All inputs are finite; a program needn't handle non-finite values.
Results may differ from the reference program's by a relative error of at most 0.014.
Values may be sent and summed in bfloat16 or wider, within the bound.
No kernel may reach another device: no remote copies, remote signals or barrier semaphores. Data moves between devices by JAX's collectives and lax.ppermute only.
A program may use at most 256 MiB of HBM per device.

```python
import math
import jax
import jax.numpy as jnp
from jax import lax

C1 = 64
LAT = 32
BLOCK = 4
C2 = 1024
LS = 8
DEPTH = 16
SAMPLES = 2


def block_levels(rng, extent, cuts, least, high):
    def one(position, blocks):
        steps = jax.random.uniform(jax.random.fold_in(jax.random.fold_in(rng, 6), position), (blocks,), jnp.float32, least / len(cuts), high / len(cuts))
        return jnp.repeat(jnp.exp(steps), extent[position] // blocks).reshape((-1,) + (1,) * (len(extent) - position - 1))

    gain = one(*cuts[0])
    for cut in cuts[1:]:
        gain = gain * one(*cut)
    return gain


def normal_values(own_key, extent, scale, bound, shards=(), dtype=jnp.bfloat16):
    entries = jax.random.normal(own_key, extent, jnp.float32) * scale
    if len(shards) > 0:
        entries = block_levels(own_key, extent, shards, -0.22, 0.18) * entries
    return jnp.clip(entries, min=-bound, max=bound).astype(dtype)


def setup_inputs(seed: int = 0) -> dict:
    keys = jax.random.split(jax.random.key(seed), 5)
    volume = normal_values(keys[0], (SAMPLES, DEPTH, LAT, LAT * C1), 1.0, 6.0, ((0, 2), (1, 16)))
    conv1_weight = normal_values(keys[1], (27, C1, C1), (27 * C1) ** -0.5, 0.15625)
    conv2_weight = normal_values(keys[2], (27, C2, C2), (27 * C2) ** -0.5, 0.0390625, ((1, 16),))
    cotangent = normal_values(keys[3], (SAMPLES, DEPTH, LS, LS, C2), 1.0, 6.0, ((0, 2), (1, 16)))
    return dict(volume=volume, conv1_weight=conv1_weight, conv2_weight=conv2_weight, cotangent=cotangent)


root_coef = 0.7978845608028654
cubic_coef = 0.044715

def gelu_tanh(value):
    inner = root_coef * (value + cubic_coef * value * value * value)
    return 0.5 * value * (1.0 + jnp.tanh(inner))

def gelu_slope(value):
    inner = root_coef * (value + cubic_coef * value * value * value)
    tanh_val = jnp.tanh(inner)
    return 0.5 * (1.0 + tanh_val) + 0.5 * value * (1.0 - tanh_val * tanh_val) * root_coef * (1.0 + 3.0 * cubic_coef * value * value)

def patches(padded, planes):
    rows = padded.shape[1] - 2
    columns = padded.shape[2] - 2
    pieces = [padded[a:a + planes, b:b + rows, c:c + columns, :] for a in range(3) for b in range(3) for c in range(3)]
    return jnp.concatenate(pieces, axis=3).reshape(planes * rows * columns, -1)

def pad_all(field):
    return jnp.pad(field, ((1, 1), (1, 1), (1, 1), (0, 0)))

def adjoint_weight(weight, chans_in, chans_out):
    shaped = weight.reshape(3, 3, 3, chans_in, chans_out)[::-1, ::-1, ::-1]
    return jnp.swapaxes(shaped, 3, 4).reshape(27 * chans_out, chans_in)

def reference(volume, conv1_weight, conv2_weight, cotangent):
    flat_one = conv1_weight.reshape(27 * C1, C1)
    flat_two = conv2_weight.reshape(27 * C2, C2)
    back_one = adjoint_weight(conv1_weight, C1, C1)
    back_two = adjoint_weight(conv2_weight, C2, C2)

    def one_sample(carry, inputs):
        acc_one, acc_two = carry
        sample_vol, sample_cot = inputs
        field = sample_vol.reshape(DEPTH, LAT, LAT, C1)
        taps_one = patches(pad_all(field), DEPTH)
        pre = jnp.dot(taps_one, flat_one, preferred_element_type=jnp.float32)
        hidden = gelu_tanh(pre).astype(jnp.bfloat16)
        moved = hidden.reshape(DEPTH, LS, BLOCK, LS, BLOCK, C1).transpose(0, 1, 3, 2, 4, 5).reshape(DEPTH, LS, LS, C2)
        taps_two = patches(pad_all(moved), DEPTH)
        output = jnp.dot(taps_two, flat_two, preferred_element_type=jnp.float32).astype(jnp.bfloat16)
        output = output.reshape(DEPTH, LS, LS, C2)
        cot_flat = sample_cot.reshape(DEPTH * LS * LS, C2)
        acc_two = acc_two + jnp.dot(taps_two.T, cot_flat, preferred_element_type=jnp.float32)
        grad_moved = jnp.dot(patches(pad_all(sample_cot), DEPTH), back_two, preferred_element_type=jnp.float32).astype(jnp.bfloat16)
        spread = grad_moved.reshape(DEPTH, LS, LS, BLOCK, BLOCK, C1).transpose(0, 1, 3, 2, 4, 5).reshape(DEPTH * LAT * LAT, C1)
        grad_pre = (spread.astype(jnp.float32) * gelu_slope(pre)).astype(jnp.bfloat16)
        acc_one = acc_one + jnp.dot(taps_one.T, grad_pre, preferred_element_type=jnp.float32)
        grad_field = grad_pre.reshape(DEPTH, LAT, LAT, C1)
        grad_in = jnp.dot(patches(pad_all(grad_field), DEPTH), back_one, preferred_element_type=jnp.float32).astype(jnp.bfloat16)
        return ((acc_one, acc_two), (output, grad_in.reshape(DEPTH, LAT, LAT * C1)))
    start = (jnp.zeros((27 * C1, C1), jnp.float32), jnp.zeros((27 * C2, C2), jnp.float32))
    (acc_one, acc_two), (features_out, grad_volume) = lax.scan(one_sample, start, (volume, cotangent))
    scale_one = 1.0 / math.sqrt(SAMPLES * DEPTH * LAT * LAT)
    scale_two = 1.0 / math.sqrt(SAMPLES * DEPTH * LS * LS)
    grad_conv1 = (acc_one * scale_one).reshape(27, C1, C1)
    grad_conv2 = (acc_two * scale_two).reshape(27, C2, C2)
    return (features_out, grad_volume, grad_conv1, grad_conv2)
```

```python
import math

import jax
import jax.numpy as jnp
from jax import lax
from jax.experimental import pallas as pl
from jax.experimental.pallas import tpu as pltpu
from jax.sharding import PartitionSpec as P

C1 = 64
LAT = 32
BLOCK = 4
C2 = 1024
LS = 8
CELLS = LS * LS
GROUP = BLOCK * C1
WINDOW = GROUP + 2 * C1
TAPS = 27
PACK = 2 * C1

root_coef = 0.7978845608028654
cubic_coef = 0.044715

f32 = jnp.float32
bf16 = jnp.bfloat16


def params(mebibytes):
    return pltpu.CompilerParams(vmem_limit_bytes=mebibytes * 1024 * 1024)


def low_lanes(shape):
    return lax.broadcasted_iota(jnp.int32, shape, len(shape) - 1) < C1


def band_kernel(w_ref, out_ref):
    for lateral in range(9):
        for slot in range(BLOCK + 2):
            column = slot if slot <= BLOCK else -1
            for pair in range(BLOCK // 2):
                halves = []
                for own in (2 * pair, 2 * pair + 1):
                    c = column - own + 1
                    if 0 <= c <= 2:
                        halves.append(w_ref[3 * lateral + c])
                    else:
                        halves.append(jnp.zeros((C1, C1), bf16))
                start = lateral * WINDOW + slot * C1
                out_ref[start : start + C1, pair * PACK : (pair + 1) * PACK] = jnp.concatenate(halves, axis=1)


def banded(weight):
    return pl.pallas_call(
        band_kernel,
        out_shape=jax.ShapeDtypeStruct((9 * WINDOW, GROUP), bf16),
        compiler_params=params(16),
        cost_estimate=pl.CostEstimate(flops=0, bytes_accessed=4 << 20, transcendentals=0),
    )(weight)


def write_windows(lhs_ref, a, groups):
    field = jnp.concatenate(groups, axis=0)
    blank = jnp.zeros((LAT, PACK), f32)
    after = jnp.concatenate([g[:, :PACK] for g in groups[1:]] + [blank], axis=0)
    before = jnp.concatenate([blank] + [g[:, GROUP - PACK :] for g in groups[:-1]], axis=0)
    edge = jnp.where(low_lanes(after.shape), after, before)
    window = jnp.concatenate([field, edge], axis=1)
    rows = window.shape[0]
    row = lax.broadcasted_iota(jnp.int32, window.shape, 0) % LAT
    shifted = [
        jnp.where(row == 0, 0.0, pltpu.roll(window, 1, 0)),
        window,
        jnp.where(row == LAT - 1, 0.0, pltpu.roll(window, rows - 1, 0)),
    ]
    for b in range(3):
        start = (3 * a + b) * WINDOW
        lhs_ref[:, start : start + WINDOW] = shifted[b].astype(bf16)


def conv_one_kernel(before_ref, own_ref, after_ref, w_ref, moved_ref, slope_ref, lhs_ref, hid_ref):
    for a, ref in enumerate((before_ref, own_ref, after_ref)):
        write_windows(lhs_ref, a, [ref[:, g * GROUP : (g + 1) * GROUP].astype(f32) for g in range(LS)])
    pre = jnp.dot(lhs_ref[...], w_ref[...], preferred_element_type=f32)
    tanh_val = jnp.tanh(root_coef * (pre + cubic_coef * pre * pre * pre))
    hidden = 0.5 * pre * (1.0 + tanh_val)
    slope_ref[...] = 0.5 * (1.0 + tanh_val) + 0.5 * pre * (1.0 - tanh_val * tanh_val) * root_coef * (
        1.0 + 3.0 * cubic_coef * pre * pre
    )
    for u in range(BLOCK // 2):
        hid_ref[u] = hidden[:, u * PACK : (u + 1) * PACK]
    for r in range(BLOCK):
        for u in range(BLOCK // 2):
            cells = jnp.concatenate(
                [hid_ref[u, pl.ds(BLOCK * i + r, LS, stride=LAT), :] for i in range(LS)], axis=0
            )
            top, bottom = cells[: CELLS // 2], cells[CELLS // 2 :]
            low = low_lanes(top.shape)
            piece = r * BLOCK + 2 * u
            moved_ref[piece] = jnp.where(low, top, pltpu.roll(bottom, C1, 1)).astype(bf16)
            moved_ref[piece + 1] = jnp.where(low, pltpu.roll(top, C1, 1), bottom).astype(bf16)


def conv_one(before, own, after, band):
    rows = LS * LAT
    return pl.pallas_call(
        conv_one_kernel,
        out_shape=(
            jax.ShapeDtypeStruct((BLOCK * BLOCK, CELLS // 2, PACK), bf16),
            jax.ShapeDtypeStruct((rows, GROUP), f32),
            jax.ShapeDtypeStruct((rows, 9 * WINDOW), bf16),
        ),
        scratch_shapes=[pltpu.VMEM((BLOCK // 2, rows, PACK), f32)],
        compiler_params=params(24),
        cost_estimate=pl.CostEstimate(
            flops=2 * rows * 9 * WINDOW * GROUP, bytes_accessed=5 << 20, transcendentals=rows * GROUP
        ),
    )(before, own, after, band)


def shift_cells(field, step):
    if step == 0:
        return field
    column = lax.broadcasted_iota(jnp.int32, field.shape, 1)
    edge = LS - 1 if step > 0 else 0
    return jnp.where(column == edge, 0.0, pltpu.roll(field, (-step) % LS, 1))


def conv_two_kernel(planes, x_ref, w_ref, out_ref, lhs_ref, v_ref):
    @pl.when(pl.program_id(0) == 0)
    def _():
        def clear(p, carry):
            v_ref[:, :, p] = jnp.zeros((3, 2, LS + 2, LS, PACK), f32)
            return carry

        lax.fori_loop(0, planes + 2, clear, 0)

        def spread(p, carry):
            x = x_ref[p].astype(f32)
            turned = pltpu.roll(x, C1, 1)
            for half, parts in enumerate(((x, turned), (turned, x))):
                cells = jnp.concatenate(parts, axis=0).reshape(LS, LS, PACK)
                for c in range(3):
                    v_ref[c, half, p + 1, 1 : LS + 1] = shift_cells(cells, c - 1)
            return carry

        lax.fori_loop(0, planes, spread, 0)

        def gather(p, carry):
            rows = pl.ds(pl.multiple_of(p * CELLS, CELLS), CELLS)
            for m in range((TAPS + 1) // 2):
                t = 2 * m
                low = v_ref[t % 3, 0, p + t // 9, pl.ds((t // 3) % 3, LS)].reshape(CELLS, PACK)
                t = 2 * m + 1
                if t < TAPS:
                    high = v_ref[t % 3, 1, p + t // 9, pl.ds((t // 3) % 3, LS)].reshape(CELLS, PACK)
                    tile = jnp.where(low_lanes(low.shape), low, high)
                    lhs_ref[rows, m * PACK : (m + 1) * PACK] = tile.astype(bf16)
                else:
                    lhs_ref[rows, m * PACK : m * PACK + C1] = low[:, :C1].astype(bf16)
            return carry

        lax.fori_loop(0, planes, gather, 0)

    if w_ref is not None:
        chunk = 4 * CELLS
        for m in range(planes * CELLS // chunk):
            rows = slice(m * chunk, (m + 1) * chunk)
            out_ref[rows] = jnp.dot(lhs_ref[rows], w_ref[...], preferred_element_type=f32).astype(bf16)


def conv_two(pieces, weight):
    planes = pieces.shape[0]
    cells = planes * CELLS
    block = 256
    return pl.pallas_call(
        lambda *refs: conv_two_kernel(planes, *refs),
        grid=(C2 // block,),
        in_specs=[
            pl.BlockSpec(pieces.shape, lambda n: (0, 0, 0)),
            pl.BlockSpec((TAPS * C1, block), lambda n: (0, n)),
        ],
        out_specs=(
            pl.BlockSpec((cells, block), lambda n: (0, n)),
            pl.BlockSpec((cells, TAPS * C1), lambda n: (0, 0)),
        ),
        out_shape=(
            jax.ShapeDtypeStruct((cells, C2), bf16),
            jax.ShapeDtypeStruct((cells, TAPS * C1), bf16),
        ),
        scratch_shapes=[pltpu.VMEM((3, 2, planes + 2, LS + 2, LS, PACK), f32)],
        compiler_params=params(40),
        cost_estimate=pl.CostEstimate(
            flops=2 * cells * TAPS * C1 * C2, bytes_accessed=10 << 20, transcendentals=0
        ),
    )(pieces, weight)


def taps_of(pieces):
    planes = pieces.shape[0]
    cells = planes * CELLS
    return pl.pallas_call(
        lambda x_ref, lhs_ref, v_ref: conv_two_kernel(planes, x_ref, None, None, lhs_ref, v_ref),
        grid=(1,),
        in_specs=[pl.BlockSpec(pieces.shape, lambda n: (0, 0, 0))],
        out_specs=pl.BlockSpec((cells, TAPS * C1), lambda n: (0, 0)),
        out_shape=jax.ShapeDtypeStruct((cells, TAPS * C1), bf16),
        scratch_shapes=[pltpu.VMEM((3, 2, planes + 2, LS + 2, LS, PACK), f32)],
        compiler_params=params(24),
        cost_estimate=pl.CostEstimate(flops=0, bytes_accessed=8 << 20, transcendentals=0),
    )(pieces)


def back_two_kernel(planes, cot_ref, w_ref, out_ref, acc_ref):
    step = pl.program_id(0)

    @pl.when(step == 0)
    def _():
        def clear(p, carry):
            acc_ref[:, :, p] = jnp.zeros((3, 2, LS + 2, LS, PACK), f32)
            return carry

        lax.fori_loop(0, planes + 2, clear, 0)

    taps = w_ref.shape[0] // C1
    slab = 4
    for m in range(planes // slab):
        product = lax.dot_general(
            cot_ref[m * slab * CELLS : (m + 1) * slab * CELLS],
            w_ref[...],
            (((1,), (1,)), ((), ())),
            preferred_element_type=f32,
        )
        for u in range(taps):
            t = taps * step + u

            @pl.when(t < TAPS)
            def _():
                first = (u // 2) * PACK
                tile = product[:, first : first + PACK].reshape(slab, LS, LS, PACK)
                where = (t % 3, u % 2, pl.ds(m * slab + t // 9, slab), pl.ds((t // 3) % 3, LS))
                acc_ref[where] = acc_ref[where] + tile

    @pl.when(step == pl.num_programs(0) - 1)
    def _():
        def finish(p, carry):
            total = None
            for half in range(2):
                part = None
                for c in range(3):
                    term = shift_cells(acc_ref[c, half, p + 1, 1 : LS + 1], 1 - c)
                    part = term if part is None else part + term
                part = part.reshape(CELLS, PACK)
                total = part if half == 0 else total + pltpu.roll(part, C1, 1)
            top, bottom = total[: CELLS // 2], total[CELLS // 2 :]
            out_ref[p] = jnp.where(low_lanes(top.shape), top, pltpu.roll(bottom, C1, 1)).astype(bf16)
            return carry

        lax.fori_loop(0, planes, finish, 0)


def back_two(cot, weight):
    planes = cot.shape[0] // CELLS
    block = 256
    return pl.pallas_call(
        lambda *refs: back_two_kernel(planes, *refs),
        grid=(pl.cdiv(TAPS * C1, block),),
        in_specs=[
            pl.BlockSpec(cot.shape, lambda n: (0, 0)),
            pl.BlockSpec((block, C2), lambda n: (n, 0)),
        ],
        out_specs=pl.BlockSpec((planes, CELLS // 2, PACK), lambda n: (0, 0, 0)),
        out_shape=jax.ShapeDtypeStruct((planes, CELLS // 2, PACK), bf16),
        scratch_shapes=[pltpu.VMEM((3, 2, planes + 2, LS + 2, LS, PACK), f32)],
        compiler_params=params(32),
        cost_estimate=pl.CostEstimate(
            flops=2 * planes * CELLS * TAPS * C1 * C2, bytes_accessed=6 << 20, transcendentals=0
        ),
    )(cot, weight)


def weight_two_kernel(samples, scale, *refs):
    lhs_refs, cot_refs, out_ref = refs[:samples], refs[samples : 2 * samples], refs[2 * samples]
    total = None
    for lhs_ref, cot_ref in zip(lhs_refs, cot_refs):
        term = lax.dot_general(
            lhs_ref[...], cot_ref[...], (((0,), (0,)), ((), ())), preferred_element_type=f32
        )
        total = term if total is None else total + term
    out_ref[...] = total * scale


def weight_two(lhs, cots, scale):
    samples = len(lhs)
    cells = lhs[0].shape[0]
    block = 256
    return pl.pallas_call(
        lambda *refs: weight_two_kernel(samples, scale, *refs),
        grid=(pl.cdiv(TAPS * C1, block),),
        in_specs=[pl.BlockSpec((cells, block), lambda n: (0, n))] * samples
        + [pl.BlockSpec((cells, C2), lambda n: (0, 0))] * samples,
        out_specs=pl.BlockSpec((block, C2), lambda n: (n, 0)),
        out_shape=jax.ShapeDtypeStruct((TAPS * C1, C2), f32),
        compiler_params=params(56),
        cost_estimate=pl.CostEstimate(
            flops=2 * samples * cells * TAPS * C1 * C2, bytes_accessed=20 << 20, transcendentals=0
        ),
    )(*lhs, *cots)


def grad_pre_kernel(pieces_ref, slope_ref, lhs_ref, grad_ref, partial_ref, spread_ref, packed_ref):
    for r in range(BLOCK):
        for u in range(BLOCK // 2):
            piece = r * BLOCK + 2 * u
            first = pieces_ref[piece].astype(f32)
            second = pieces_ref[piece + 1].astype(f32)
            low = low_lanes(first.shape)
            top = jnp.where(low, first, pltpu.roll(second, C1, 1))
            bottom = jnp.where(low, pltpu.roll(first, C1, 1), second)
            for i in range(LS):
                source = top if i < LS // 2 else bottom
                start = (i % (LS // 2)) * LS
                spread_ref[u, pl.ds(BLOCK * i + r, LS, stride=LAT), :] = source[start : start + LS]
    grads = []
    for u in range(BLOCK // 2):
        lanes = slice(u * PACK, (u + 1) * PACK)
        value = (spread_ref[u] * slope_ref[:, lanes]).astype(bf16)
        grad_ref[:, lanes] = value
        grads.append(value)
    grad = jnp.concatenate(grads, axis=1)
    for lateral in range(9):
        window = lhs_ref[:, lateral * WINDOW : (lateral + 1) * WINDOW]
        product = lax.dot_general(window, grad, (((0,), (0,)), ((), ())), preferred_element_type=f32)
        for c in range(3):
            sums = []
            for parity in range(2):
                part = None
                for pair in range(BLOCK // 2):
                    column = 2 * pair + parity + c - 1
                    slot = column if column >= 0 else BLOCK + 1
                    term = product[slot * C1 : (slot + 1) * C1, pair * PACK : (pair + 1) * PACK]
                    part = term if part is None else part + term
                sums.append(part)
            total = sums[0] + pltpu.roll(sums[1], C1, 1)
            top, bottom = total[: C1 // 2], total[C1 // 2 :]
            t = 3 * lateral + c
            packed_ref[t * (C1 // 2) : (t + 1) * (C1 // 2)] = jnp.where(
                low_lanes(top.shape), top, pltpu.roll(bottom, C1, 1)
            )
    packed_ref[TAPS * (C1 // 2) :] = jnp.zeros(((32 - TAPS) * (C1 // 2), PACK), f32)
    for row in range(C1 // 2):
        entry = packed_ref[pl.ds(row, 32, stride=C1 // 2), :]
        partial_ref[row] = entry.astype(bf16)


def grad_pre_of(pieces, slope, lhs):
    rows = LS * LAT
    return pl.pallas_call(
        grad_pre_kernel,
        out_shape=(
            jax.ShapeDtypeStruct((rows, GROUP), bf16),
            jax.ShapeDtypeStruct((C1 // 2, 32, PACK), bf16),
        ),
        scratch_shapes=[
            pltpu.VMEM((BLOCK // 2, rows, PACK), f32),
            pltpu.VMEM((32 * (C1 // 2), PACK), f32),
        ],
        compiler_params=params(24),
        cost_estimate=pl.CostEstimate(
            flops=2 * rows * 9 * WINDOW * GROUP, bytes_accessed=3 << 20, transcendentals=0
        ),
    )(pieces, slope, lhs)


def back_one_kernel(before_ref, own_ref, after_ref, w_ref, out_ref, lhs_ref):
    for a, ref in enumerate((before_ref, own_ref, after_ref)):
        write_windows(lhs_ref, a, [ref[g * LAT : (g + 1) * LAT].astype(f32) for g in range(LS)])
    result = jnp.dot(lhs_ref[...], w_ref[...], preferred_element_type=f32)
    for g in range(LS):
        out_ref[:, g * GROUP : (g + 1) * GROUP] = result[g * LAT : (g + 1) * LAT].astype(bf16)


def back_one(before, own, after, band):
    rows = LS * LAT
    return pl.pallas_call(
        back_one_kernel,
        out_shape=jax.ShapeDtypeStruct((LAT, LAT * C1), bf16),
        scratch_shapes=[pltpu.VMEM((rows, 9 * WINDOW), bf16)],
        compiler_params=params(24),
        cost_estimate=pl.CostEstimate(
            flops=2 * rows * 9 * WINDOW * GROUP, bytes_accessed=3 << 20, transcendentals=0
        ),
    )(before, own, after, band)


def unpack_kernel(packed_ref, out_ref, wide_ref):
    wide_ref[...] = packed_ref[...].astype(f32).reshape(wide_ref.shape)
    for t in range(TAPS):
        entry = wide_ref[pl.ds(t, C1 // 2, stride=32), :]
        out_ref[t] = jnp.concatenate([entry[:, :C1], entry[:, C1:]], axis=0)


def unpack(packed):
    return pl.pallas_call(
        unpack_kernel,
        out_shape=jax.ShapeDtypeStruct((TAPS, C1, C1), f32),
        scratch_shapes=[pltpu.VMEM((32 * (C1 // 2), PACK), f32)],
        compiler_params=params(16),
        cost_estimate=pl.CostEstimate(flops=0, bytes_accessed=1 << 20, transcendentals=0),
    )(packed)


def neighbours(value, axis):
    count = lax.axis_size(axis)
    before = lax.ppermute(value, axis, [(i, i + 1) for i in range(count - 1)])
    after = lax.ppermute(value, axis, [(i + 1, i) for i in range(count - 1)])
    return before, after


def over_samples(value):
    count = lax.axis_size("sample")
    return [value] + [
        lax.ppermute(value, "sample", [(i, (i + shift) % count) for i in range(count)])
        for shift in range(1, count)
    ]


def on_device(volume, conv1_weight, conv2_weight, cotangent):
    samples = lax.axis_size("sample")
    shards = lax.axis_size("depth")
    flat_two = conv2_weight.reshape(TAPS * C1, C2)
    own = volume.reshape(LAT, LAT * C1)

    cots = lax.all_gather(cotangent.reshape(CELLS, C2), "depth", axis=0, tiled=True)
    before, after = neighbours(own, "depth")

    back_weight = jnp.swapaxes(conv1_weight[::-1], 1, 2)
    band = banded(conv1_weight)
    back_band = banded(back_weight)

    moved, slope, windows = conv_one(before, own, after, band)
    pieces = lax.all_to_all(moved, "depth", split_axis=0, concat_axis=0, tiled=True)

    partial, own_taps = conv_two(pieces, flat_two)
    features = lax.psum_scatter(partial, "depth", scatter_dimension=0, tiled=True)

    grad_pieces = back_two(cots, flat_two)
    grad_pieces = lax.all_to_all(grad_pieces, "depth", split_axis=0, concat_axis=0, tiled=True)
    grad_pre, partial_one = grad_pre_of(grad_pieces, slope, windows)
    grad_before, grad_after = neighbours(grad_pre, "depth")

    devices = samples * shards
    both = ("sample", "depth")
    scale_one = 1.0 / math.sqrt(samples * shards * LAT * LAT)
    shares = partial_one.reshape(devices, -1, PACK)
    shares = lax.all_to_all(shares, both, split_axis=0, concat_axis=0, tiled=True)
    summed = (jnp.sum(shares.astype(f32), axis=0) * scale_one).astype(bf16)
    summed = jnp.broadcast_to(summed[None], shares.shape)
    summed = lax.all_to_all(summed, both, split_axis=0, concat_axis=0, tiled=True)
    grad_conv1 = unpack(summed.reshape(C1 // 2, 32, PACK))

    grad_volume = back_one(grad_before, grad_pre, grad_after, back_band)

    scale_two = 1.0 / math.sqrt(samples * shards * CELLS)
    all_taps = [own_taps] + [taps_of(value) for value in over_samples(pieces)[1:]]
    grad_conv2 = weight_two(all_taps, over_samples(cots), scale_two)

    return (
        features.reshape(cotangent.shape),
        grad_volume.reshape(volume.shape),
        grad_conv1,
        grad_conv2.reshape(conv2_weight.shape),
    )


def solution(mesh):
    return jax.shard_map(
        on_device,
        mesh=mesh,
        in_specs=(
            P("sample", "depth", None, None),
            P(),
            P(None, "depth", None),
            P("sample", "depth", None, None, None),
        ),
        out_specs=(
            P("sample", "depth", None, None, None),
            P("sample", "depth", None, None),
            P(),
            P(None, "depth", None),
        ),
        check_vma=False,
    )
```

```python
import math

import jax
import jax.numpy as jnp
from jax import lax
from jax.experimental import pallas as pl
from jax.experimental.pallas import tpu as pltpu
from jax.sharding import PartitionSpec as P

C1 = 64
LAT = 32
BLOCK = 4
C2 = 1024
LS = 8
CELLS = LS * LS
GROUP = BLOCK * C1
WINDOW = GROUP + 2 * C1
TAPS = 27
PACK = 2 * C1

root_coef = 0.7978845608028654
cubic_coef = 0.044715

f32 = jnp.float32
bf16 = jnp.bfloat16


def params(mebibytes):
    return pltpu.CompilerParams(vmem_limit_bytes=mebibytes * 1024 * 1024)


def low_lanes(shape):
    return lax.broadcasted_iota(jnp.int32, shape, len(shape) - 1) < C1


def band_kernel(w_ref, out_ref):
    for lateral in range(9):
        for slot in range(BLOCK + 2):
            column = slot if slot <= BLOCK else -1
            for pair in range(BLOCK // 2):
                halves = []
                for own in (2 * pair, 2 * pair + 1):
                    c = column - own + 1
                    if 0 <= c <= 2:
                        halves.append(w_ref[3 * lateral + c])
                    else:
                        halves.append(jnp.zeros((C1, C1), bf16))
                start = lateral * WINDOW + slot * C1
                out_ref[start : start + C1, pair * PACK : (pair + 1) * PACK] = jnp.concatenate(halves, axis=1)


def banded(weight):
    return pl.pallas_call(
        band_kernel,
        out_shape=jax.ShapeDtypeStruct((9 * WINDOW, GROUP), bf16),
        compiler_params=params(16),
        cost_estimate=pl.CostEstimate(flops=0, bytes_accessed=4 << 20, transcendentals=0),
    )(weight)


def write_windows(lhs_ref, a, groups):
    field = jnp.concatenate(groups, axis=0)
    blank = jnp.zeros((LAT, PACK), f32)
    after = jnp.concatenate([g[:, :PACK] for g in groups[1:]] + [blank], axis=0)
    before = jnp.concatenate([blank] + [g[:, GROUP - PACK :] for g in groups[:-1]], axis=0)
    edge = jnp.where(low_lanes(after.shape), after, before)
    window = jnp.concatenate([field, edge], axis=1)
    rows = window.shape[0]
    row = lax.broadcasted_iota(jnp.int32, window.shape, 0) % LAT
    shifted = [
        jnp.where(row == 0, 0.0, pltpu.roll(window, 1, 0)),
        window,
        jnp.where(row == LAT - 1, 0.0, pltpu.roll(window, rows - 1, 0)),
    ]
    for b in range(3):
        start = (3 * a + b) * WINDOW
        lhs_ref[:, start : start + WINDOW] = shifted[b].astype(bf16)


def conv_one_kernel(before_ref, own_ref, after_ref, w_ref, moved_ref, slope_ref, lhs_ref, hid_ref):
    for a, ref in enumerate((before_ref, own_ref, after_ref)):
        write_windows(lhs_ref, a, [ref[:, g * GROUP : (g + 1) * GROUP].astype(f32) for g in range(LS)])
    pre = jnp.dot(lhs_ref[...], w_ref[...], preferred_element_type=f32)
    tanh_val = jnp.tanh(root_coef * (pre + cubic_coef * pre * pre * pre))
    hidden = 0.5 * pre * (1.0 + tanh_val)
    slope_ref[...] = 0.5 * (1.0 + tanh_val) + 0.5 * pre * (1.0 - tanh_val * tanh_val) * root_coef * (
        1.0 + 3.0 * cubic_coef * pre * pre
    )
    for u in range(BLOCK // 2):
        hid_ref[u] = hidden[:, u * PACK : (u + 1) * PACK]
    for r in range(BLOCK):
        for u in range(BLOCK // 2):
            cells = jnp.concatenate(
                [hid_ref[u, pl.ds(BLOCK * i + r, LS, stride=LAT), :] for i in range(LS)], axis=0
            )
            top, bottom = cells[: CELLS // 2], cells[CELLS // 2 :]
            low = low_lanes(top.shape)
            piece = r * BLOCK + 2 * u
            moved_ref[piece] = jnp.where(low, top, pltpu.roll(bottom, C1, 1)).astype(bf16)
            moved_ref[piece + 1] = jnp.where(low, pltpu.roll(top, C1, 1), bottom).astype(bf16)


def conv_one(before, own, after, band):
    rows = LS * LAT
    return pl.pallas_call(
        conv_one_kernel,
        out_shape=(
            jax.ShapeDtypeStruct((BLOCK * BLOCK, CELLS // 2, PACK), bf16),
            jax.ShapeDtypeStruct((rows, GROUP), f32),
            jax.ShapeDtypeStruct((rows, 9 * WINDOW), bf16),
        ),
        scratch_shapes=[pltpu.VMEM((BLOCK // 2, rows, PACK), f32)],
        compiler_params=params(24),
        cost_estimate=pl.CostEstimate(
            flops=2 * rows * 9 * WINDOW * GROUP, bytes_accessed=5 << 20, transcendentals=rows * GROUP
        ),
    )(before, own, after, band)


def shift_cells(field, step):
    if step == 0:
        return field
    column = lax.broadcasted_iota(jnp.int32, field.shape, 1)
    edge = LS - 1 if step > 0 else 0
    return jnp.where(column == edge, 0.0, pltpu.roll(field, (-step) % LS, 1))


def turn_kernel(x_ref, out_ref):
    out_ref[...] = x_ref[...].T


def turned(value, block):
    rows, columns = value.shape
    return pl.pallas_call(
        turn_kernel,
        grid=(columns // block,),
        in_specs=[pl.BlockSpec((rows, block), lambda n: (0, n))],
        out_specs=pl.BlockSpec((block, rows), lambda n: (n, 0)),
        out_shape=jax.ShapeDtypeStruct((columns, rows), value.dtype),
        compiler_params=params(12),
        cost_estimate=pl.CostEstimate(flops=0, bytes_accessed=8 * rows * columns, transcendentals=0),
    )(value)


def turn_weight_kernel(rows, x_ref, out_ref):
    block = x_ref.shape[0]
    row = lax.broadcasted_iota(jnp.int32, x_ref.shape, 0) + block * pl.program_id(0)
    out_ref[...] = jnp.where(row < rows, x_ref[...].astype(f32), 0.0).astype(bf16).T


def turned_weight(weight, block=256):
    rows, columns = weight.shape
    steps = pl.cdiv(rows, block)
    return pl.pallas_call(
        lambda *refs: turn_weight_kernel(rows, *refs),
        grid=(steps,),
        in_specs=[pl.BlockSpec((block, columns), lambda n: (n, 0))],
        out_specs=pl.BlockSpec((columns, block), lambda n: (0, n)),
        out_shape=jax.ShapeDtypeStruct((columns, steps * block), weight.dtype),
        compiler_params=params(12),
        cost_estimate=pl.CostEstimate(flops=0, bytes_accessed=16 << 20, transcendentals=0),
    )(weight)


def conv_send_kernel(planes, parity_ref, x_ref, w_ref, out_ref, lhs_ref, v_ref):
    half_planes = planes // 2

    @pl.when(pl.program_id(0) == 0)
    def _():
        v_ref[:, :, 0] = jnp.zeros((3, 2, LS + 2, LS, PACK), f32)
        v_ref[:, :, planes + 1] = jnp.zeros((3, 2, LS + 2, LS, PACK), f32)
        edge = jnp.zeros((LS, PACK), f32)

        def spread(p, carry):
            x = x_ref[p].astype(f32)
            turn = pltpu.roll(x, C1, 1)
            for half, parts in enumerate(((x, turn), (turn, x))):
                cells = jnp.concatenate(parts, axis=0).reshape(LS, LS, PACK)
                for c in range(3):
                    v_ref[c, half, p + 1, 0] = edge
                    v_ref[c, half, p + 1, 1 : LS + 1] = shift_cells(cells, c - 1)
                    v_ref[c, half, p + 1, LS + 1] = edge
            return carry

        lax.fori_loop(0, planes, spread, 0)

        def gather(p, carry):
            group = jnp.where(p % 2 == parity_ref[0], 0, half_planes)
            rows = pl.ds(pl.multiple_of((group + p // 2) * CELLS, CELLS), CELLS)
            for m in range((TAPS + 1) // 2):
                t = 2 * m
                low = v_ref[t % 3, 0, p + t // 9, pl.ds((t // 3) % 3, LS)].reshape(CELLS, PACK)
                t = 2 * m + 1
                if t < TAPS:
                    high = v_ref[t % 3, 1, p + t // 9, pl.ds((t // 3) % 3, LS)].reshape(CELLS, PACK)
                    tile = jnp.where(low_lanes(low.shape), low, high)
                    lhs_ref[rows, m * PACK : (m + 1) * PACK] = tile.astype(bf16)
                else:
                    lhs_ref[rows, m * PACK : m * PACK + C1] = low[:, :C1].astype(bf16)
            return carry

        lax.fori_loop(0, planes, gather, 0)

    first = half_planes * CELLS
    out_ref[...] = jnp.dot(lhs_ref[first:], w_ref[...], preferred_element_type=f32).astype(bf16)


def conv_send(parity, pieces, weight):
    planes = pieces.shape[0]
    cells = planes * CELLS
    block = 256
    return pl.pallas_call(
        lambda *refs: conv_send_kernel(planes, *refs),
        grid_spec=pltpu.PrefetchScalarGridSpec(
            num_scalar_prefetch=1,
            grid=(C2 // block,),
            in_specs=[
                pl.BlockSpec(pieces.shape, lambda n, s: (0, 0, 0)),
                pl.BlockSpec((TAPS * C1, block), lambda n, s: (0, n)),
            ],
            out_specs=(
                pl.BlockSpec((cells // 2, block), lambda n, s: (0, n)),
                pl.BlockSpec((cells, TAPS * C1), lambda n, s: (0, 0)),
            ),
            scratch_shapes=[pltpu.VMEM((3, 2, planes + 2, LS + 2, LS, PACK), f32)],
        ),
        out_shape=(
            jax.ShapeDtypeStruct((cells // 2, C2), bf16),
            jax.ShapeDtypeStruct((cells, TAPS * C1), bf16),
        ),
        compiler_params=params(24),
        cost_estimate=pl.CostEstimate(
            flops=2 * cells * TAPS * C1 * C2, bytes_accessed=10 << 20, transcendentals=0
        ),
    )(parity, pieces, weight)


def conv_keep_kernel(lhs_ref, w_ref, more_ref, out_ref):
    product = jnp.dot(lhs_ref[...], w_ref[...], preferred_element_type=f32)
    out_ref[...] = (product + more_ref[...].astype(f32)).astype(bf16)


def conv_keep(lhs, weight, more):
    cells = more.shape[0]
    block = 256
    return pl.pallas_call(
        conv_keep_kernel,
        grid=(C2 // block,),
        in_specs=[
            pl.BlockSpec((cells, TAPS * C1), lambda n: (0, 0)),
            pl.BlockSpec((TAPS * C1, block), lambda n: (0, n)),
            pl.BlockSpec((cells, block), lambda n: (0, n)),
        ],
        out_specs=pl.BlockSpec((cells, block), lambda n: (0, n)),
        out_shape=jax.ShapeDtypeStruct((cells, C2), bf16),
        compiler_params=params(16),
        cost_estimate=pl.CostEstimate(
            flops=2 * cells * TAPS * C1 * C2, bytes_accessed=8 << 20, transcendentals=0
        ),
    )(lhs, weight, more)


def taps_kernel(planes, x_ref, out_ref, flat_ref):
    half_cells = planes // 2 * CELLS

    def cells_of(p):
        x = x_ref[p].astype(f32)
        return jnp.concatenate([x, pltpu.roll(x, C1, 1)], axis=0)

    for s in range(2):
        for j in range(planes // 4):
            pair = jnp.concatenate([cells_of(4 * j + s), cells_of(4 * j + 2 + s)], axis=0)
            flat_ref[s, :, j * PACK : (j + 1) * PACK] = pair.T[:C1]

    lane = lax.broadcasted_iota(jnp.int32, (C1, half_cells), 1)
    row, column = (lane // LS) % LS, lane % LS
    for b in range(3):
        for c in range(3):
            inside = (row + b >= 1) & (row + b <= LS) & (column + c >= 1) & (column + c <= LS)
            step = LS * (b - 1) + c - 1
            even, odd = (
                jnp.where(inside, pltpu.roll(flat_ref[s], (-step) % half_cells, 1), 0.0) for s in range(2)
            )
            odd_before = jnp.where(lane < CELLS, 0.0, pltpu.roll(odd, CELLS, 1))
            even_after = jnp.where(
                lane >= half_cells - CELLS, 0.0, pltpu.roll(even, half_cells - CELLS, 1)
            )
            for s, sources in enumerate(((odd_before, even, odd), (even, odd, even_after))):
                for a in range(3):
                    t = 9 * a + 3 * b + c
                    out_ref[s, t * C1 : (t + 1) * C1] = sources[a].astype(bf16)


def taps_of(pieces):
    planes = pieces.shape[0]
    half_cells = planes // 2 * CELLS
    return pl.pallas_call(
        lambda *refs: taps_kernel(planes, *refs),
        out_shape=jax.ShapeDtypeStruct((2, TAPS * C1, half_cells), bf16),
        scratch_shapes=[pltpu.VMEM((2, C1, half_cells), f32)],
        compiler_params=params(16),
        cost_estimate=pl.CostEstimate(flops=0, bytes_accessed=8 << 20, transcendentals=0),
    )(pieces)


def back_two_kernel(planes, parity_ref, own_ref, other_ref, w_ref, out_ref, acc_ref):
    step = pl.program_id(0)

    @pl.when(step == 0)
    def _():
        def clear(p, carry):
            acc_ref[:, :, p] = jnp.zeros((3, 2, LS + 2, LS, PACK), f32)
            return carry

        lax.fori_loop(0, planes + 3, clear, 0)

    taps = w_ref.shape[1] // C1
    slab = 4
    for s, cot_ref in enumerate((own_ref, other_ref)):
        for m in range(planes // 2 // slab):
            product = jnp.dot(
                cot_ref[m * slab * CELLS : (m + 1) * slab * CELLS], w_ref[...], preferred_element_type=f32
            )
            for u in range(taps):
                t = taps * step + u
                lanes = slice((u // 2) * PACK, (u // 2 + 1) * PACK)
                for k in range(slab):
                    plane = 2 * (m * slab + k) + (parity_ref[0] if s == 0 else 1 - parity_ref[0])
                    tile = product[k * CELLS : (k + 1) * CELLS, lanes].reshape(LS, LS, PACK)
                    where = (t % 3, u % 2, plane + t // 9, pl.ds((t // 3) % 3, LS))
                    acc_ref[where] = acc_ref[where] + tile

    @pl.when(step == pl.num_programs(0) - 1)
    def _():
        def finish(p, carry):
            total = None
            for half in range(2):
                part = None
                for c in range(3):
                    term = shift_cells(acc_ref[c, half, p + 1, 1 : LS + 1], 1 - c)
                    part = term if part is None else part + term
                part = part.reshape(CELLS, PACK)
                total = part if half == 0 else total + pltpu.roll(part, C1, 1)
            top, bottom = total[: CELLS // 2], total[CELLS // 2 :]
            out_ref[p] = jnp.where(low_lanes(top.shape), top, pltpu.roll(bottom, C1, 1)).astype(bf16)
            return carry

        lax.fori_loop(0, planes, finish, 0)


def back_two(parity, own, other, weight):
    planes = 2 * own.shape[0] // CELLS
    block = 256
    return pl.pallas_call(
        lambda *refs: back_two_kernel(planes, *refs),
        grid_spec=pltpu.PrefetchScalarGridSpec(
            num_scalar_prefetch=1,
            grid=(weight.shape[1] // block,),
            in_specs=[
                pl.BlockSpec(own.shape, lambda n, s: (0, 0)),
                pl.BlockSpec(own.shape, lambda n, s: (0, 0)),
                pl.BlockSpec((C2, block), lambda n, s: (0, n)),
            ],
            out_specs=pl.BlockSpec((planes, CELLS // 2, PACK), lambda n, s: (0, 0, 0)),
            scratch_shapes=[pltpu.VMEM((3, 2, planes + 3, LS + 2, LS, PACK), f32)],
        ),
        out_shape=jax.ShapeDtypeStruct((planes, CELLS // 2, PACK), bf16),
        compiler_params=params(20),
        cost_estimate=pl.CostEstimate(
            flops=2 * planes * CELLS * TAPS * C1 * C2, bytes_accessed=6 << 20, transcendentals=0
        ),
    )(parity, own, other, weight)


def weight_two_kernel(count, scale, *refs):
    lhs_refs, cot_refs, out_ref = refs[1 : count + 1], refs[count + 1 : 2 * count + 1], refs[2 * count + 1]
    total = None
    for lhs_ref, cot_ref in zip(lhs_refs, cot_refs):
        term = jnp.dot(lhs_ref[0], cot_ref[...], preferred_element_type=f32)
        total = term if total is None else total + term
    out_ref[...] = total * scale


def weight_two(parity, taps, cots, scale):
    lhs = [value for value in taps for _ in range(2)]
    flat = [value for pair in cots for value in pair]
    count = len(flat)
    cells = flat[0].shape[0]
    block = 3 * 3 * C1
    specs = [
        pl.BlockSpec((1, block, cells), lambda n, s: (s[0], n, 0)),
        pl.BlockSpec((1, block, cells), lambda n, s: (1 - s[0], n, 0)),
    ] * (count // 2)
    return pl.pallas_call(
        lambda *refs: weight_two_kernel(count, scale, *refs),
        grid_spec=pltpu.PrefetchScalarGridSpec(
            num_scalar_prefetch=1,
            grid=(TAPS * C1 // block,),
            in_specs=specs + [pl.BlockSpec((cells, C2), lambda n, s: (0, 0))] * count,
            out_specs=pl.BlockSpec((block, C2), lambda n, s: (n, 0)),
        ),
        out_shape=jax.ShapeDtypeStruct((TAPS * C1, C2), f32),
        compiler_params=params(32 if count <= 4 else 56),
        cost_estimate=pl.CostEstimate(
            flops=2 * count * cells * TAPS * C1 * C2, bytes_accessed=18 << 20, transcendentals=0
        ),
    )(parity, *lhs, *flat)


def grad_pre_kernel(pieces_ref, slope_ref, lhs_ref, grad_ref, partial_ref, spread_ref, packed_ref):
    for r in range(BLOCK):
        for u in range(BLOCK // 2):
            piece = r * BLOCK + 2 * u
            first = pieces_ref[piece].astype(f32)
            second = pieces_ref[piece + 1].astype(f32)
            low = low_lanes(first.shape)
            top = jnp.where(low, first, pltpu.roll(second, C1, 1))
            bottom = jnp.where(low, pltpu.roll(first, C1, 1), second)
            for i in range(LS):
                source = top if i < LS // 2 else bottom
                start = (i % (LS // 2)) * LS
                spread_ref[u, pl.ds(BLOCK * i + r, LS, stride=LAT), :] = source[start : start + LS]
    grads = []
    for u in range(BLOCK // 2):
        lanes = slice(u * PACK, (u + 1) * PACK)
        value = (spread_ref[u] * slope_ref[:, lanes]).astype(bf16)
        grad_ref[:, lanes] = value
        grads.append(value)
    grad = jnp.concatenate(grads, axis=1)
    for lateral in range(9):
        window = lhs_ref[lateral * WINDOW : (lateral + 1) * WINDOW]
        product = jnp.dot(window, grad, preferred_element_type=f32)
        for c in range(3):
            sums = []
            for parity in range(2):
                part = None
                for pair in range(BLOCK // 2):
                    column = 2 * pair + parity + c - 1
                    slot = column if column >= 0 else BLOCK + 1
                    term = product[slot * C1 : (slot + 1) * C1, pair * PACK : (pair + 1) * PACK]
                    part = term if part is None else part + term
                sums.append(part)
            total = sums[0] + pltpu.roll(sums[1], C1, 1)
            top, bottom = total[: C1 // 2], total[C1 // 2 :]
            t = 3 * lateral + c
            packed_ref[t * (C1 // 2) : (t + 1) * (C1 // 2)] = jnp.where(
                low_lanes(top.shape), top, pltpu.roll(bottom, C1, 1)
            )
    packed_ref[TAPS * (C1 // 2) :] = jnp.zeros(((32 - TAPS) * (C1 // 2), PACK), f32)
    for row in range(C1 // 2):
        entry = packed_ref[pl.ds(row, 32, stride=C1 // 2), :]
        partial_ref[row] = entry.astype(bf16)


def grad_pre_of(pieces, slope, lhs):
    rows = LS * LAT
    return pl.pallas_call(
        grad_pre_kernel,
        out_shape=(
            jax.ShapeDtypeStruct((rows, GROUP), bf16),
            jax.ShapeDtypeStruct((C1 // 2, 32, PACK), bf16),
        ),
        scratch_shapes=[
            pltpu.VMEM((BLOCK // 2, rows, PACK), f32),
            pltpu.VMEM((32 * (C1 // 2), PACK), f32),
        ],
        compiler_params=params(24),
        cost_estimate=pl.CostEstimate(
            flops=2 * rows * 9 * WINDOW * GROUP, bytes_accessed=3 << 20, transcendentals=0
        ),
    )(pieces, slope, lhs)


def back_one_kernel(before_ref, own_ref, after_ref, w_ref, out_ref, lhs_ref):
    for a, ref in enumerate((before_ref, own_ref, after_ref)):
        write_windows(lhs_ref, a, [ref[g * LAT : (g + 1) * LAT].astype(f32) for g in range(LS)])
    result = jnp.dot(lhs_ref[...], w_ref[...], preferred_element_type=f32)
    for g in range(LS):
        out_ref[:, g * GROUP : (g + 1) * GROUP] = result[g * LAT : (g + 1) * LAT].astype(bf16)


def back_one(before, own, after, band):
    rows = LS * LAT
    return pl.pallas_call(
        back_one_kernel,
        out_shape=jax.ShapeDtypeStruct((LAT, LAT * C1), bf16),
        scratch_shapes=[pltpu.VMEM((rows, 9 * WINDOW), bf16)],
        compiler_params=params(24),
        cost_estimate=pl.CostEstimate(
            flops=2 * rows * 9 * WINDOW * GROUP, bytes_accessed=3 << 20, transcendentals=0
        ),
    )(before, own, after, band)


def unpack_kernel(packed_ref, out_ref, wide_ref):
    wide_ref[...] = packed_ref[...].astype(f32).reshape(wide_ref.shape)
    for t in range(TAPS):
        entry = wide_ref[pl.ds(t, C1 // 2, stride=32), :]
        out_ref[t] = jnp.concatenate([entry[:, :C1], entry[:, C1:]], axis=0)


def unpack(packed):
    return pl.pallas_call(
        unpack_kernel,
        out_shape=jax.ShapeDtypeStruct((TAPS, C1, C1), f32),
        scratch_shapes=[pltpu.VMEM((32 * (C1 // 2), PACK), f32)],
        compiler_params=params(16),
        cost_estimate=pl.CostEstimate(flops=0, bytes_accessed=1 << 20, transcendentals=0),
    )(packed)


def neighbours(value, axis):
    count = lax.axis_size(axis)
    before = lax.ppermute(value, axis, [(i, i + 1) for i in range(count - 1)])
    after = lax.ppermute(value, axis, [(i + 1, i) for i in range(count - 1)])
    return before, after


def swap_cores(value):
    count = lax.axis_size("depth")
    return lax.ppermute(value, "depth", [(i, i ^ 1) for i in range(count)])


def over_samples(value):
    count = lax.axis_size("sample")
    return [value] + [
        lax.ppermute(value, "sample", [(i, (i + shift) % count) for i in range(count)])
        for shift in range(1, count)
    ]


def on_device(volume, conv1_weight, conv2_weight, cotangent):
    samples = lax.axis_size("sample")
    shards = lax.axis_size("depth")
    flat_two = conv2_weight.reshape(TAPS * C1, C2)
    own = volume.reshape(LAT, LAT * C1)
    parity = (lax.axis_index("depth") % 2).astype(jnp.int32).reshape(1)
    groups = [list(range(core, shards, 2)) for core in range(2)]

    cot_own = lax.all_gather(
        cotangent.reshape(CELLS, C2), "depth", axis=0, tiled=True, axis_index_groups=groups
    )
    before, after = neighbours(own, "depth")

    back_weight = jnp.swapaxes(conv1_weight[::-1], 1, 2)
    band = banded(conv1_weight)
    back_band = banded(back_weight)
    turned_two = turned_weight(flat_two)

    moved, slope, windows = conv_one(before, own, after, band)
    pieces = lax.all_to_all(moved, "depth", split_axis=0, concat_axis=0, tiled=True)

    send, own_lhs = conv_send(parity, pieces, flat_two)
    received = swap_cores(send)
    kept = conv_keep(own_lhs, flat_two, received)
    features = lax.all_to_all(kept, "depth", split_axis=0, concat_axis=0, tiled=True, axis_index_groups=groups)
    features = jnp.sum(features.reshape(-1, CELLS, C2).astype(f32), axis=0).astype(bf16)

    cot_other = swap_cores(cot_own)
    grad_pieces = back_two(parity, cot_own, cot_other, turned_two)
    grad_pieces = lax.all_to_all(grad_pieces, "depth", split_axis=0, concat_axis=0, tiled=True)
    grad_pre, partial_one = grad_pre_of(grad_pieces, slope, turned(windows, WINDOW))
    grad_before, grad_after = neighbours(grad_pre, "depth")

    devices = samples * shards
    both = ("sample", "depth")
    scale_one = 1.0 / math.sqrt(samples * shards * LAT * LAT)
    shares = partial_one.reshape(devices, -1, PACK)
    shares = lax.all_to_all(shares, both, split_axis=0, concat_axis=0, tiled=True)
    summed = (jnp.sum(shares.astype(f32), axis=0) * scale_one).astype(bf16)
    summed = jnp.broadcast_to(summed[None], shares.shape)
    summed = lax.all_to_all(summed, both, split_axis=0, concat_axis=0, tiled=True)
    grad_conv1 = unpack(summed.reshape(C1 // 2, 32, PACK))

    grad_volume = back_one(grad_before, grad_pre, grad_after, back_band)

    scale_two = 1.0 / math.sqrt(samples * shards * CELLS)
    all_taps = [taps_of(value) for value in over_samples(pieces)]
    all_cots = [(cot_own, cot_other)] + [(value, swap_cores(value)) for value in over_samples(cot_own)[1:]]
    grad_conv2 = weight_two(parity, all_taps, all_cots, scale_two)

    return (
        features.reshape(cotangent.shape),
        grad_volume.reshape(volume.shape),
        grad_conv1,
        grad_conv2.reshape(conv2_weight.shape),
    )


def solution(mesh):
    return jax.shard_map(
        on_device,
        mesh=mesh,
        in_specs=(
            P("sample", "depth", None, None),
            P(),
            P(None, "depth", None),
            P("sample", "depth", None, None, None),
        ),
        out_specs=(
            P("sample", "depth", None, None, None),
            P("sample", "depth", None, None),
            P(),
            P(None, "depth", None),
        ),
        check_vma=False,
    )
```

```python
import math

import jax
import jax.numpy as jnp
from jax import lax
from jax.experimental import pallas as pl
from jax.experimental.pallas import tpu as pltpu
from jax.sharding import PartitionSpec as P

C1 = 64
LAT = 32
BLOCK = 4
C2 = 1024
LS = 8
CELLS = LS * LS
GROUP = BLOCK * C1
WINDOW = GROUP + 2 * C1
TAPS = 27
PACK = 2 * C1

root_coef = 0.7978845608028654
cubic_coef = 0.044715

f32 = jnp.float32
bf16 = jnp.bfloat16


def params(mebibytes):
    return pltpu.CompilerParams(vmem_limit_bytes=mebibytes * 1024 * 1024)


def low_lanes(shape):
    return lax.broadcasted_iota(jnp.int32, shape, len(shape) - 1) < C1


def band_kernel(w_ref, out_ref):
    for lateral in range(9):
        for slot in range(BLOCK + 2):
            column = slot if slot <= BLOCK else -1
            for pair in range(BLOCK // 2):
                halves = []
                for own in (2 * pair, 2 * pair + 1):
                    c = column - own + 1
                    if 0 <= c <= 2:
                        halves.append(w_ref[3 * lateral + c])
                    else:
                        halves.append(jnp.zeros((C1, C1), bf16))
                start = lateral * WINDOW + slot * C1
                out_ref[start : start + C1, pair * PACK : (pair + 1) * PACK] = jnp.concatenate(halves, axis=1)


def banded(weight):
    return pl.pallas_call(
        band_kernel,
        out_shape=jax.ShapeDtypeStruct((9 * WINDOW, GROUP), bf16),
        compiler_params=params(16),
        cost_estimate=pl.CostEstimate(flops=0, bytes_accessed=4 << 20, transcendentals=0),
    )(weight)


def write_windows(lhs_ref, a, groups):
    field = jnp.concatenate(groups, axis=0)
    blank = jnp.zeros((LAT, PACK), f32)
    after = jnp.concatenate([g[:, :PACK] for g in groups[1:]] + [blank], axis=0)
    before = jnp.concatenate([blank] + [g[:, GROUP - PACK :] for g in groups[:-1]], axis=0)
    edge = jnp.where(low_lanes(after.shape), after, before)
    window = jnp.concatenate([field, edge], axis=1)
    rows = window.shape[0]
    row = lax.broadcasted_iota(jnp.int32, window.shape, 0) % LAT
    shifted = [
        jnp.where(row == 0, 0.0, pltpu.roll(window, 1, 0)),
        window,
        jnp.where(row == LAT - 1, 0.0, pltpu.roll(window, rows - 1, 0)),
    ]
    for b in range(3):
        start = (3 * a + b) * WINDOW
        lhs_ref[:, start : start + WINDOW] = shifted[b].astype(bf16)


def conv_one_kernel(before_ref, own_ref, after_ref, w_ref, moved_ref, slope_ref, lhs_ref, hid_ref):
    for a, ref in enumerate((before_ref, own_ref, after_ref)):
        write_windows(lhs_ref, a, [ref[:, g * GROUP : (g + 1) * GROUP].astype(f32) for g in range(LS)])
    pre = jnp.dot(lhs_ref[...], w_ref[...], preferred_element_type=f32)
    tanh_val = jnp.tanh(root_coef * (pre + cubic_coef * pre * pre * pre))
    hidden = 0.5 * pre * (1.0 + tanh_val)
    slope_ref[...] = 0.5 * (1.0 + tanh_val) + 0.5 * pre * (1.0 - tanh_val * tanh_val) * root_coef * (
        1.0 + 3.0 * cubic_coef * pre * pre
    )
    for u in range(BLOCK // 2):
        hid_ref[u] = hidden[:, u * PACK : (u + 1) * PACK]
    for r in range(BLOCK):
        for u in range(BLOCK // 2):
            cells = jnp.concatenate(
                [hid_ref[u, pl.ds(BLOCK * i + r, LS, stride=LAT), :] for i in range(LS)], axis=0
            )
            top, bottom = cells[: CELLS // 2], cells[CELLS // 2 :]
            low = low_lanes(top.shape)
            piece = r * BLOCK + 2 * u
            moved_ref[piece] = jnp.where(low, top, pltpu.roll(bottom, C1, 1)).astype(bf16)
            moved_ref[piece + 1] = jnp.where(low, pltpu.roll(top, C1, 1), bottom).astype(bf16)


def conv_one(before, own, after, band):
    rows = LS * LAT
    return pl.pallas_call(
        conv_one_kernel,
        out_shape=(
            jax.ShapeDtypeStruct((BLOCK * BLOCK, CELLS // 2, PACK), bf16),
            jax.ShapeDtypeStruct((rows, GROUP), f32),
            jax.ShapeDtypeStruct((rows, 9 * WINDOW), bf16),
        ),
        scratch_shapes=[pltpu.VMEM((BLOCK // 2, rows, PACK), f32)],
        compiler_params=params(24),
        cost_estimate=pl.CostEstimate(
            flops=2 * rows * 9 * WINDOW * GROUP, bytes_accessed=5 << 20, transcendentals=rows * GROUP
        ),
    )(before, own, after, band)


def shift_cells(field, step):
    if step == 0:
        return field
    column = lax.broadcasted_iota(jnp.int32, field.shape, 1)
    edge = LS - 1 if step > 0 else 0
    return jnp.where(column == edge, 0.0, pltpu.roll(field, (-step) % LS, 1))


def turn_weight_kernel(rows, x_ref, out_ref):
    block = x_ref.shape[0]
    row = lax.broadcasted_iota(jnp.int32, x_ref.shape, 0) + block * pl.program_id(0)
    out_ref[...] = jnp.where(row < rows, x_ref[...].astype(f32), 0.0).astype(bf16).T


def turned_weight(weight, block=256):
    rows, columns = weight.shape
    steps = pl.cdiv(rows, block)
    return pl.pallas_call(
        lambda *refs: turn_weight_kernel(rows, *refs),
        grid=(steps,),
        in_specs=[pl.BlockSpec((block, columns), lambda n: (n, 0))],
        out_specs=pl.BlockSpec((columns, block), lambda n: (0, n)),
        out_shape=jax.ShapeDtypeStruct((columns, steps * block), weight.dtype),
        compiler_params=params(56),
        cost_estimate=pl.CostEstimate(flops=0, bytes_accessed=16 << 20, transcendentals=0),
    )(weight)


def conv_two_kernel(planes, x_ref, w_ref, out_ref, lhs_ref, v_ref):
    @pl.when(pl.program_id(0) == 0)
    def _():
        v_ref[:, :, 0] = jnp.zeros((3, 2, LS + 2, LS, PACK), f32)
        v_ref[:, :, planes + 1] = jnp.zeros((3, 2, LS + 2, LS, PACK), f32)
        edge = jnp.zeros((LS, PACK), f32)

        def spread(p, carry):
            x = x_ref[p].astype(f32)
            turned = pltpu.roll(x, C1, 1)
            for half, parts in enumerate(((x, turned), (turned, x))):
                cells = jnp.concatenate(parts, axis=0).reshape(LS, LS, PACK)
                for c in range(3):
                    v_ref[c, half, p + 1, 0] = edge
                    v_ref[c, half, p + 1, 1 : LS + 1] = shift_cells(cells, c - 1)
                    v_ref[c, half, p + 1, LS + 1] = edge
            return carry

        lax.fori_loop(0, planes, spread, 0)

        def gather(p, carry):
            rows = pl.ds(pl.multiple_of(p * CELLS, CELLS), CELLS)
            for m in range((TAPS + 1) // 2):
                t = 2 * m
                low = v_ref[t % 3, 0, p + t // 9, pl.ds((t // 3) % 3, LS)].reshape(CELLS, PACK)
                t = 2 * m + 1
                if t < TAPS:
                    high = v_ref[t % 3, 1, p + t // 9, pl.ds((t // 3) % 3, LS)].reshape(CELLS, PACK)
                    tile = jnp.where(low_lanes(low.shape), low, high)
                    lhs_ref[rows, m * PACK : (m + 1) * PACK] = tile.astype(bf16)
                else:
                    lhs_ref[rows, m * PACK : m * PACK + C1] = low[:, :C1].astype(bf16)
            return carry

        lax.fori_loop(0, planes, gather, 0)

    chunk = 4 * CELLS
    for m in range(planes * CELLS // chunk):
        rows = slice(m * chunk, (m + 1) * chunk)
        out_ref[rows] = jnp.dot(lhs_ref[rows], w_ref[...], preferred_element_type=f32).astype(bf16)


def conv_two(pieces, weight):
    planes = pieces.shape[0]
    cells = planes * CELLS
    block = 256
    return pl.pallas_call(
        lambda *refs: conv_two_kernel(planes, *refs),
        grid=(C2 // block,),
        in_specs=[
            pl.BlockSpec(pieces.shape, lambda n: (0, 0, 0)),
            pl.BlockSpec((TAPS * C1, block), lambda n: (0, n)),
        ],
        out_specs=pl.BlockSpec((cells, block), lambda n: (0, n)),
        out_shape=jax.ShapeDtypeStruct((cells, C2), bf16),
        scratch_shapes=[
            pltpu.VMEM((cells, TAPS * C1), bf16),
            pltpu.VMEM((3, 2, planes + 2, LS + 2, LS, PACK), f32),
        ],
        compiler_params=params(56),
        cost_estimate=pl.CostEstimate(
            flops=2 * cells * TAPS * C1 * C2, bytes_accessed=10 << 20, transcendentals=0
        ),
    )(pieces, weight)


def plane_copies(device, pieces, refs, target_ref, base, sems):
    copies = []
    for differences, ref in zip(pieces, refs):
        for k, difference in enumerate(differences):
            row = pl.multiple_of(base + (device ^ difference) * CELLS, CELLS)
            source = ref.at[pl.ds(k * CELLS, CELLS), :]
            target = target_ref.at[pl.ds(row, CELLS), :]
            copies.append(pltpu.make_async_copy(source, target, sems.at[base // CELLS + len(copies)]))
    return copies


def back_two_kernel(planes, pieces, device_ref, *refs):
    cot_refs = refs[: len(pieces)]
    w_ref, out_ref, cot_ref, product_ref, sems = refs[len(pieces)], *refs[-4:]
    step = pl.program_id(0)
    tiles = product_ref.shape[0]

    @pl.when(step == 0)
    def _():
        copies = plane_copies(device_ref[0], pieces, cot_refs, cot_ref, 0, sems)
        for copy in copies:
            copy.start()
        empty_plane = jnp.zeros((LS + 2, LS, PACK), f32)
        empty_row = jnp.zeros((planes, LS, PACK), f32)
        for m in range(tiles):
            product_ref[m, 0] = empty_plane
            product_ref[m, planes + 1] = empty_plane
            product_ref[m, 1 : planes + 1, 0] = empty_row
            product_ref[m, 1 : planes + 1, LS + 1] = empty_row
        for copy in copies:
            copy.wait()

    wide = w_ref.shape[1] // PACK
    slab = planes // 4
    for m in range(4):
        product = jnp.dot(
            cot_ref[m * slab * CELLS : (m + 1) * slab * CELLS], w_ref[...], preferred_element_type=f32
        )
        for u in range(wide):
            tile = product[:, u * PACK : (u + 1) * PACK].reshape(slab, LS, LS, PACK)
            product_ref[wide * step + u, 1 + m * slab : 1 + (m + 1) * slab, 1 : LS + 1] = tile

    @pl.when(step == pl.num_programs(0) - 1)
    def _():
        def finish(p, carry):
            sums = {}
            for m in range(tiles):
                taps = [t for t in (2 * m, 2 * m + 1) if t < TAPS]
                for k, t in enumerate(taps):
                    a, b = t // 9, (t // 3) % 3
                    same = len(taps) == 2 and taps[0] // 3 == taps[1] // 3
                    if same and k == 1:
                        continue
                    key = (t % 3, t % 3 + 1) if same else ((t % 3, None) if k == 0 else (None, t % 3))
                    tile = product_ref[m, p + 2 - a, 2 - b : 2 - b + LS]
                    sums[key] = tile if key not in sums else sums[key] + tile
            total = None
            for half in range(2):
                part = None
                for c in range(3):
                    found = [value for key, value in sums.items() if key[half] == c]
                    for value in found:
                        term = shift_cells(value, 1 - c)
                        part = term if part is None else part + term
                part = part.reshape(CELLS, PACK)
                total = part if half == 0 else total + pltpu.roll(part, C1, 1)
            top, bottom = total[: CELLS // 2], total[CELLS // 2 :]
            out_ref[p] = jnp.where(low_lanes(top.shape), top, pltpu.roll(bottom, C1, 1)).astype(bf16)
            return carry

        lax.fori_loop(0, planes, finish, 0)


def back_two(device, pieces, cots, weight, after):
    planes = sum(len(piece) for piece in pieces)
    block = 256
    tiles = weight.shape[1] // PACK
    return pl.pallas_call(
        lambda *refs: back_two_kernel(planes, pieces, *refs),
        grid_spec=pltpu.PrefetchScalarGridSpec(
            num_scalar_prefetch=1,
            grid=(weight.shape[1] // block,),
            in_specs=[pl.BlockSpec(memory_space=pl.ANY)] * len(cots)
            + [pl.BlockSpec((C2, block), lambda n, s: (0, n))]
            + [pl.BlockSpec(memory_space=pl.ANY)] * len(after),
            out_specs=pl.BlockSpec((planes, CELLS // 2, PACK), lambda n, s: (0, 0, 0)),
            scratch_shapes=[
                pltpu.VMEM((planes * CELLS, C2), bf16),
                pltpu.VMEM((tiles, planes + 2, LS + 2, LS, PACK), f32),
                pltpu.SemaphoreType.DMA((planes,)),
            ],
        ),
        out_shape=jax.ShapeDtypeStruct((planes, CELLS // 2, PACK), bf16),
        compiler_params=params(56),
        cost_estimate=pl.CostEstimate(
            flops=2 * planes * CELLS * TAPS * C1 * C2, bytes_accessed=6 << 20, transcendentals=0
        ),
    )(device, *cots, weight, *after)


def weight_two_kernel(planes, pieces, scale, device_ref, *refs):
    samples = len(pieces)
    field_refs, cot_refs = refs[:samples], refs[samples:]
    out_ref, cot_ref, flat_ref, lhs_ref, sems = refs[-5:]
    cells = planes * CELLS
    a = pl.program_id(0)

    def all_copies():
        copies, first = [], 0
        for s in range(samples):
            refs_here = cot_refs[first : first + len(pieces[s])]
            copies += plane_copies(device_ref[0], pieces[s], refs_here, cot_ref, s * cells, sems)
            first += len(pieces[s])
        return copies

    @pl.when(a == 0)
    def _():
        for copy in all_copies():
            copy.start()
        for s in range(samples):

            def cells_of(p):
                x = field_refs[s][p].astype(f32)
                return jnp.concatenate([x, pltpu.roll(x, C1, 1)], axis=0)

            for j in range(planes // 2):
                pair = jnp.concatenate([cells_of(2 * j), cells_of(2 * j + 1)], axis=0)
                flat_ref[s, :, j * PACK : (j + 1) * PACK] = pair.T[:C1]

    lane = lax.broadcasted_iota(jnp.int32, (C1, cells), 1)
    plane, row, column = lane // CELLS, (lane // LS) % LS, lane % LS
    deep = (plane + a >= 1) & (plane + a <= planes)
    for b in range(3):
        for c in range(3):
            inside = deep & (row + b >= 1) & (row + b <= LS) & (column + c >= 1) & (column + c <= LS)
            shift = lax.rem(2 * cells - (CELLS * (a - 1) + LS * (b - 1) + c - 1), cells)
            t = 3 * b + c
            for s in range(samples):
                value = jnp.where(inside, pltpu.roll(flat_ref[s], shift, 1), 0.0)
                lhs_ref[t * C1 : (t + 1) * C1, s * cells : (s + 1) * cells] = value.astype(bf16)

    @pl.when(a == 0)
    def _():
        for copy in all_copies():
            copy.wait()

    out_ref[...] = jnp.dot(lhs_ref[...], cot_ref[...], preferred_element_type=f32) * scale


def weight_two(device, fields, pieces, cots, scale, after):
    samples = len(fields)
    planes = fields[0].shape[0]
    cells = planes * CELLS
    block = 9 * C1
    flat = [value for sample in cots for value in sample]
    return pl.pallas_call(
        lambda *refs: weight_two_kernel(planes, pieces, scale, *refs),
        grid_spec=pltpu.PrefetchScalarGridSpec(
            num_scalar_prefetch=1,
            grid=(3,),
            in_specs=[pl.BlockSpec(field.shape, lambda n, s: (0, 0, 0)) for field in fields]
            + [pl.BlockSpec(memory_space=pl.ANY)] * (len(flat) + len(after)),
            out_specs=pl.BlockSpec((block, C2), lambda n, s: (n, 0)),
            scratch_shapes=[
                pltpu.VMEM((samples * cells, C2), bf16),
                pltpu.VMEM((samples, C1, cells), f32),
                pltpu.VMEM((block, samples * cells), bf16),
                pltpu.SemaphoreType.DMA((samples * planes,)),
            ],
        ),
        out_shape=jax.ShapeDtypeStruct((TAPS * C1, C2), f32),
        compiler_params=params(60),
        cost_estimate=pl.CostEstimate(
            flops=2 * samples * cells * TAPS * C1 * C2, bytes_accessed=18 << 20, transcendentals=0
        ),
    )(device, *fields, *flat, *after)


def grad_pre_kernel(pieces_ref, slope_ref, lhs_ref, grad_ref, partial_ref, spread_ref, packed_ref):
    for r in range(BLOCK):
        for u in range(BLOCK // 2):
            piece = r * BLOCK + 2 * u
            first = pieces_ref[piece].astype(f32)
            second = pieces_ref[piece + 1].astype(f32)
            low = low_lanes(first.shape)
            top = jnp.where(low, first, pltpu.roll(second, C1, 1))
            bottom = jnp.where(low, pltpu.roll(first, C1, 1), second)
            for i in range(LS):
                source = top if i < LS // 2 else bottom
                start = (i % (LS // 2)) * LS
                spread_ref[u, pl.ds(BLOCK * i + r, LS, stride=LAT), :] = source[start : start + LS]
    grads = []
    for u in range(BLOCK // 2):
        lanes = slice(u * PACK, (u + 1) * PACK)
        value = (spread_ref[u] * slope_ref[:, lanes]).astype(bf16)
        grad_ref[:, lanes] = value
        grads.append(value)
    grad = jnp.concatenate(grads, axis=1)
    for lateral in range(9):
        window = lhs_ref[:, lateral * WINDOW : (lateral + 1) * WINDOW]
        product = lax.dot_general(window, grad, (((0,), (0,)), ((), ())), preferred_element_type=f32)
        for c in range(3):
            sums = []
            for parity in range(2):
                part = None
                for pair in range(BLOCK // 2):
                    column = 2 * pair + parity + c - 1
                    slot = column if column >= 0 else BLOCK + 1
                    term = product[slot * C1 : (slot + 1) * C1, pair * PACK : (pair + 1) * PACK]
                    part = term if part is None else part + term
                sums.append(part)
            total = sums[0] + pltpu.roll(sums[1], C1, 1)
            top, bottom = total[: C1 // 2], total[C1 // 2 :]
            t = 3 * lateral + c
            packed_ref[t * (C1 // 2) : (t + 1) * (C1 // 2)] = jnp.where(
                low_lanes(top.shape), top, pltpu.roll(bottom, C1, 1)
            )
    packed_ref[TAPS * (C1 // 2) :] = jnp.zeros(((32 - TAPS) * (C1 // 2), PACK), f32)
    for row in range(C1 // 2):
        entry = packed_ref[pl.ds(row, 32, stride=C1 // 2), :]
        partial_ref[row] = entry.astype(bf16)


def grad_pre_of(pieces, slope, lhs):
    rows = LS * LAT
    return pl.pallas_call(
        grad_pre_kernel,
        out_shape=(
            jax.ShapeDtypeStruct((rows, GROUP), bf16),
            jax.ShapeDtypeStruct((C1 // 2, 32, PACK), bf16),
        ),
        scratch_shapes=[
            pltpu.VMEM((BLOCK // 2, rows, PACK), f32),
            pltpu.VMEM((32 * (C1 // 2), PACK), f32),
        ],
        compiler_params=params(24),
        cost_estimate=pl.CostEstimate(
            flops=2 * rows * 9 * WINDOW * GROUP, bytes_accessed=3 << 20, transcendentals=0
        ),
    )(pieces, slope, lhs)


def back_one_kernel(before_ref, own_ref, after_ref, w_ref, out_ref, lhs_ref):
    for a, ref in enumerate((before_ref, own_ref, after_ref)):
        write_windows(lhs_ref, a, [ref[g * LAT : (g + 1) * LAT].astype(f32) for g in range(LS)])
    result = jnp.dot(lhs_ref[...], w_ref[...], preferred_element_type=f32)
    for g in range(LS):
        out_ref[:, g * GROUP : (g + 1) * GROUP] = result[g * LAT : (g + 1) * LAT].astype(bf16)


def back_one(before, own, after, band):
    rows = LS * LAT
    return pl.pallas_call(
        back_one_kernel,
        out_shape=jax.ShapeDtypeStruct((LAT, LAT * C1), bf16),
        scratch_shapes=[pltpu.VMEM((rows, 9 * WINDOW), bf16)],
        compiler_params=params(24),
        cost_estimate=pl.CostEstimate(
            flops=2 * rows * 9 * WINDOW * GROUP, bytes_accessed=3 << 20, transcendentals=0
        ),
    )(before, own, after, band)


def unpack_kernel(packed_ref, out_ref, wide_ref):
    wide_ref[...] = packed_ref[...].astype(f32).reshape(wide_ref.shape)
    for t in range(TAPS):
        entry = wide_ref[pl.ds(t, C1 // 2, stride=32), :]
        out_ref[t] = jnp.concatenate([entry[:, :C1], entry[:, C1:]], axis=0)


def unpack(packed):
    return pl.pallas_call(
        unpack_kernel,
        out_shape=jax.ShapeDtypeStruct((TAPS, C1, C1), f32),
        scratch_shapes=[pltpu.VMEM((32 * (C1 // 2), PACK), f32)],
        compiler_params=params(16),
        cost_estimate=pl.CostEstimate(flops=0, bytes_accessed=1 << 20, transcendentals=0),
    )(packed)


def neighbours(value, axis):
    count = lax.axis_size(axis)
    before = lax.ppermute(value, axis, [(i, i + 1) for i in range(count - 1)])
    after = lax.ppermute(value, axis, [(i + 1, i) for i in range(count - 1)])
    return before, after


def flipped(value, difference):
    count = lax.axis_size("depth")
    return lax.ppermute(value, "depth", [(i, i ^ difference) for i in range(count)])


def over_samples(value):
    count = lax.axis_size("sample")
    return [value] + [
        lax.ppermute(value, "sample", [(i, (i + shift) % count) for i in range(count)])
        for shift in range(1, count)
    ]


def on_device(volume, conv1_weight, conv2_weight, cotangent):
    samples = lax.axis_size("sample")
    shards = lax.axis_size("depth")
    flat_two = conv2_weight.reshape(TAPS * C1, C2)
    own = volume.reshape(LAT, LAT * C1)
    device = lax.axis_index("depth").astype(jnp.int32).reshape(1)
    cot = cotangent.reshape(CELLS, C2)

    core, chip = 1, 2
    outer = list(range(4, shards, 4))
    far = [flipped(cot, difference) for difference in outer]
    before, after = neighbours(own, "depth")
    cot_chip = flipped(cot, chip)

    back_weight = jnp.swapaxes(conv1_weight[::-1], 1, 2)
    band = banded(conv1_weight)
    back_band = banded(back_weight)
    turned_two = turned_weight(flat_two)

    moved, slope, windows = conv_one(before, own, after, band)
    fields = lax.all_to_all(moved, "depth", split_axis=0, concat_axis=0, tiled=True)

    near = jnp.concatenate([cot, cot_chip], axis=0)
    far = jnp.concatenate(far, axis=0)
    far_chip = flipped(far, chip)
    cots = [near, far, far_chip]
    pieces = [[0, chip], outer, [difference + chip for difference in outer]]
    pieces = pieces + [[difference + core for difference in piece] for piece in pieces]

    partial = conv_two(fields, flat_two)
    features = lax.psum_scatter(partial, "depth", scatter_dimension=0, tiled=True)

    own_cots = cots + [flipped(value, core) for value in cots]
    grad_pieces = back_two(device, pieces, own_cots, turned_two, [partial])
    grad_pieces = lax.all_to_all(grad_pieces, "depth", split_axis=0, concat_axis=0, tiled=True)
    grad_pre, partial_one = grad_pre_of(grad_pieces, slope, windows)
    grad_before, grad_after = neighbours(grad_pre, "depth")

    devices = samples * shards
    both = ("sample", "depth")
    scale_one = 1.0 / math.sqrt(samples * shards * LAT * LAT)
    shares = partial_one.reshape(devices, -1, PACK)
    shares = lax.all_to_all(shares, both, split_axis=0, concat_axis=0, tiled=True)
    summed = (jnp.sum(shares.astype(f32), axis=0) * scale_one).astype(bf16)
    summed = jnp.broadcast_to(summed[None], shares.shape)
    summed = lax.all_to_all(summed, both, split_axis=0, concat_axis=0, tiled=True)
    grad_conv1 = unpack(summed.reshape(C1 // 2, 32, PACK))

    grad_volume = back_one(grad_before, grad_pre, grad_after, back_band)

    scale_two = 1.0 / math.sqrt(samples * shards * CELLS)
    half = jnp.concatenate(cots, axis=0)
    halves = [[difference for piece in group for difference in piece] for group in (pieces[:3], pieces[3:])]
    all_pieces, all_cots = [pieces], [own_cots]
    for value in over_samples(half)[1:]:
        all_pieces.append(halves)
        all_cots.append([value, flipped(value, core)])
    grad_conv2 = weight_two(device, over_samples(fields), all_pieces, all_cots, scale_two, [grad_pre])

    return (
        features.reshape(cotangent.shape),
        grad_volume.reshape(volume.shape),
        grad_conv1,
        grad_conv2.reshape(conv2_weight.shape),
    )


def solution(mesh):
    return jax.shard_map(
        on_device,
        mesh=mesh,
        in_specs=(
            P("sample", "depth", None, None),
            P(),
            P(None, "depth", None),
            P("sample", "depth", None, None, None),
        ),
        out_specs=(
            P("sample", "depth", None, None, None),
            P("sample", "depth", None, None),
            P(),
            P(None, "depth", None),
        ),
        check_vma=False,
    )
```

```python
import math

import jax
import jax.numpy as jnp
from jax import lax
from jax.experimental import pallas as pl
from jax.experimental.pallas import tpu as pltpu
from jax.sharding import PartitionSpec as P

C1 = 64
LAT = 32
BLOCK = 4
C2 = 1024
LS = 8
CELLS = LS * LS
GROUP = BLOCK * C1
WINDOW = GROUP + 2 * C1
TAPS = 27
PACK = 2 * C1

root_coef = 0.7978845608028654
cubic_coef = 0.044715

f32 = jnp.float32
bf16 = jnp.bfloat16


def params(mebibytes):
    return pltpu.CompilerParams(vmem_limit_bytes=mebibytes * 1024 * 1024)


def low_lanes(shape):
    return lax.broadcasted_iota(jnp.int32, shape, len(shape) - 1) < C1


def band_kernel(w_ref, out_ref):
    for lateral in range(9):
        for slot in range(BLOCK + 2):
            column = slot if slot <= BLOCK else -1
            for pair in range(BLOCK // 2):
                halves = []
                for own in (2 * pair, 2 * pair + 1):
                    c = column - own + 1
                    if 0 <= c <= 2:
                        halves.append(w_ref[3 * lateral + c])
                    else:
                        halves.append(jnp.zeros((C1, C1), bf16))
                start = lateral * WINDOW + slot * C1
                out_ref[start : start + C1, pair * PACK : (pair + 1) * PACK] = jnp.concatenate(halves, axis=1)


def banded(weight):
    return pl.pallas_call(
        band_kernel,
        out_shape=jax.ShapeDtypeStruct((9 * WINDOW, GROUP), bf16),
        compiler_params=params(16),
        cost_estimate=pl.CostEstimate(flops=0, bytes_accessed=4 << 20, transcendentals=0),
    )(weight)


def write_windows(lhs_ref, a, groups):
    field = jnp.concatenate(groups, axis=0)
    blank = jnp.zeros((LAT, PACK), f32)
    after = jnp.concatenate([g[:, :PACK] for g in groups[1:]] + [blank], axis=0)
    before = jnp.concatenate([blank] + [g[:, GROUP - PACK :] for g in groups[:-1]], axis=0)
    edge = jnp.where(low_lanes(after.shape), after, before)
    window = jnp.concatenate([field, edge], axis=1)
    rows = window.shape[0]
    row = lax.broadcasted_iota(jnp.int32, window.shape, 0) % LAT
    shifted = [
        jnp.where(row == 0, 0.0, pltpu.roll(window, 1, 0)),
        window,
        jnp.where(row == LAT - 1, 0.0, pltpu.roll(window, rows - 1, 0)),
    ]
    for b in range(3):
        start = (3 * a + b) * WINDOW
        lhs_ref[:, start : start + WINDOW] = shifted[b].astype(bf16)


def conv_one_kernel(before_ref, own_ref, after_ref, w_ref, moved_ref, slope_ref, lhs_ref, hid_ref):
    for a, ref in enumerate((before_ref, own_ref, after_ref)):
        write_windows(lhs_ref, a, [ref[:, g * GROUP : (g + 1) * GROUP].astype(f32) for g in range(LS)])
    pre = jnp.dot(lhs_ref[...], w_ref[...], preferred_element_type=f32)
    tanh_val = jnp.tanh(root_coef * (pre + cubic_coef * pre * pre * pre))
    hidden = 0.5 * pre * (1.0 + tanh_val)
    slope_ref[...] = 0.5 * (1.0 + tanh_val) + 0.5 * pre * (1.0 - tanh_val * tanh_val) * root_coef * (
        1.0 + 3.0 * cubic_coef * pre * pre
    )
    for u in range(BLOCK // 2):
        hid_ref[u] = hidden[:, u * PACK : (u + 1) * PACK]
    for r in range(BLOCK):
        for u in range(BLOCK // 2):
            cells = jnp.concatenate(
                [hid_ref[u, pl.ds(BLOCK * i + r, LS, stride=LAT), :] for i in range(LS)], axis=0
            )
            top, bottom = cells[: CELLS // 2], cells[CELLS // 2 :]
            low = low_lanes(top.shape)
            piece = r * BLOCK + 2 * u
            moved_ref[piece] = jnp.where(low, top, pltpu.roll(bottom, C1, 1)).astype(bf16)
            moved_ref[piece + 1] = jnp.where(low, pltpu.roll(top, C1, 1), bottom).astype(bf16)


def conv_one(before, own, after, band):
    rows = LS * LAT
    return pl.pallas_call(
        conv_one_kernel,
        out_shape=(
            jax.ShapeDtypeStruct((BLOCK * BLOCK, CELLS // 2, PACK), bf16),
            jax.ShapeDtypeStruct((rows, GROUP), f32),
            jax.ShapeDtypeStruct((rows, 9 * WINDOW), bf16),
        ),
        scratch_shapes=[pltpu.VMEM((BLOCK // 2, rows, PACK), f32)],
        compiler_params=params(24),
        cost_estimate=pl.CostEstimate(
            flops=2 * rows * 9 * WINDOW * GROUP, bytes_accessed=5 << 20, transcendentals=rows * GROUP
        ),
    )(before, own, after, band)


def shift_cells(field, step):
    if step == 0:
        return field
    column = lax.broadcasted_iota(jnp.int32, field.shape, 1)
    edge = LS - 1 if step > 0 else 0
    return jnp.where(column == edge, 0.0, pltpu.roll(field, (-step) % LS, 1))


def conv_two_kernel(planes, device_ref, x_ref, w_ref, send_ref, keep_ref, lhs_ref, v_ref):
    @pl.when(pl.program_id(0) == 0)
    def _():
        v_ref[:, :, 0] = jnp.zeros((3, 2, LS + 2, LS, PACK), f32)
        v_ref[:, :, planes + 1] = jnp.zeros((3, 2, LS + 2, LS, PACK), f32)
        edge = jnp.zeros((LS, PACK), f32)

        def spread(p, carry):
            x = x_ref[p].astype(f32)
            turned = pltpu.roll(x, C1, 1)
            for half, parts in enumerate(((x, turned), (turned, x))):
                cells = jnp.concatenate(parts, axis=0).reshape(LS, LS, PACK)
                for c in range(3):
                    v_ref[c, half, p + 1, 0] = edge
                    v_ref[c, half, p + 1, 1 : LS + 1] = shift_cells(cells, c - 1)
                    v_ref[c, half, p + 1, LS + 1] = edge
            return carry

        lax.fori_loop(0, planes, spread, 0)

        def gather(p, carry):
            difference = p ^ device_ref[0]
            place = (
                (1 - (difference & 1)) * (planes // 2)
                + ((difference >> 1) & 1) * (planes // 4)
                + (difference >> 2)
            )
            rows = pl.ds(pl.multiple_of(place * CELLS, CELLS), CELLS)
            for m in range((TAPS + 1) // 2):
                t = 2 * m
                low = v_ref[t % 3, 0, p + t // 9, pl.ds((t // 3) % 3, LS)].reshape(CELLS, PACK)
                t = 2 * m + 1
                if t < TAPS:
                    high = v_ref[t % 3, 1, p + t // 9, pl.ds((t // 3) % 3, LS)].reshape(CELLS, PACK)
                    tile = jnp.where(low_lanes(low.shape), low, high)
                    lhs_ref[rows, m * PACK : (m + 1) * PACK] = tile.astype(bf16)
                else:
                    lhs_ref[rows, m * PACK : m * PACK + C1] = low[:, :C1].astype(bf16)
            return carry

        lax.fori_loop(0, planes, gather, 0)

    product = jnp.dot(lhs_ref[...], w_ref[...], preferred_element_type=f32).astype(bf16)
    half = planes // 2 * CELLS
    send_ref[...] = product[:half]
    keep_ref[...] = product[half:]


def conv_two(device, fields, weight):
    planes = fields.shape[0]
    cells = planes * CELLS
    block = 512
    return pl.pallas_call(
        lambda *refs: conv_two_kernel(planes, *refs),
        grid_spec=pltpu.PrefetchScalarGridSpec(
            num_scalar_prefetch=1,
            grid=(C2 // block,),
            in_specs=[
                pl.BlockSpec(fields.shape, lambda n, s: (0, 0, 0)),
                pl.BlockSpec((TAPS * C1, block), lambda n, s: (0, n)),
            ],
            out_specs=(
                pl.BlockSpec((cells // 2, block), lambda n, s: (0, n)),
                pl.BlockSpec((cells // 2, block), lambda n, s: (0, n)),
            ),
            scratch_shapes=[
                pltpu.VMEM((cells, TAPS * C1), bf16),
                pltpu.VMEM((3, 2, planes + 2, LS + 2, LS, PACK), f32),
            ],
        ),
        out_shape=(jax.ShapeDtypeStruct((cells // 2, C2), bf16),) * 2,
        compiler_params=params(56),
        cost_estimate=pl.CostEstimate(
            flops=2 * cells * TAPS * C1 * C2, bytes_accessed=10 << 20, transcendentals=0
        ),
    )(device, fields, weight)


def join_kernel(count, *refs):
    out_ref, sems = refs[count], refs[count + 1]
    copies, first = [], 0
    for k in range(count):
        rows = refs[k].shape[0]
        copies.append(pltpu.make_async_copy(refs[k], out_ref.at[pl.ds(first, rows), :], sems.at[k]))
        first += rows
    for copy in copies:
        copy.start()
    for copy in copies:
        copy.wait()


def joined(values):
    rows = sum(value.shape[0] for value in values)
    columns = values[0].shape[1]
    return pl.pallas_call(
        lambda *refs: join_kernel(len(values), *refs),
        in_specs=[pl.BlockSpec(memory_space=pl.ANY)] * len(values),
        out_specs=pl.BlockSpec(memory_space=pl.ANY),
        out_shape=jax.ShapeDtypeStruct((rows, columns), values[0].dtype),
        scratch_shapes=[pltpu.SemaphoreType.DMA((len(values),))],
        compiler_params=params(56),
        cost_estimate=pl.CostEstimate(flops=0, bytes_accessed=4 * rows * columns, transcendentals=0),
    )(*values)


def plane_copies(device, pieces, refs, target_ref, base, sems):
    copies = []
    for differences, ref in zip(pieces, refs):
        for k, difference in enumerate(differences):
            row = pl.multiple_of(base + (device ^ difference) * CELLS, CELLS)
            source = ref.at[pl.ds(k * CELLS, CELLS), :]
            target = target_ref.at[pl.ds(row, CELLS), :]
            copies.append(pltpu.make_async_copy(source, target, sems.at[base // CELLS + len(copies)]))
    return copies


def back_two_kernel(planes, pieces, device_ref, *refs):
    cot_refs = refs[: len(pieces)]
    w_ref, out_ref, cot_ref, product_ref, sems = refs[len(pieces)], *refs[-4:]
    step = pl.program_id(0)
    tiles = product_ref.shape[0]

    @pl.when(step == 0)
    def _():
        copies = plane_copies(device_ref[0], pieces, cot_refs, cot_ref, 0, sems)
        for copy in copies:
            copy.start()
        empty_plane = jnp.zeros((LS + 2, LS, PACK), f32)
        empty_row = jnp.zeros((planes, LS, PACK), f32)
        for m in range(tiles):
            product_ref[m, 0] = empty_plane
            product_ref[m, planes + 1] = empty_plane
            product_ref[m, 1 : planes + 1, 0] = empty_row
            product_ref[m, 1 : planes + 1, LS + 1] = empty_row
        for copy in copies:
            copy.wait()

    wide = w_ref.shape[0] // PACK
    product = lax.dot_general(
        cot_ref[...], w_ref[...], (((1,), (1,)), ((), ())), preferred_element_type=f32
    )
    for u in range(wide):
        tile = product[:, u * PACK : (u + 1) * PACK].reshape(planes, LS, LS, PACK)
        product_ref[wide * step + u, 1 : planes + 1, 1 : LS + 1] = tile

    @pl.when(step == pl.num_programs(0) - 1)
    def _():
        def finish(p, carry):
            sums = {}
            for m in range(tiles):
                taps = [t for t in (2 * m, 2 * m + 1) if t < TAPS]
                for k, t in enumerate(taps):
                    a, b = t // 9, (t // 3) % 3
                    same = len(taps) == 2 and taps[0] // 3 == taps[1] // 3
                    if same and k == 1:
                        continue
                    key = (t % 3, t % 3 + 1) if same else ((t % 3, None) if k == 0 else (None, t % 3))
                    tile = product_ref[m, p + 2 - a, 2 - b : 2 - b + LS]
                    sums[key] = tile if key not in sums else sums[key] + tile
            total = None
            for half in range(2):
                part = None
                for c in range(3):
                    found = [value for key, value in sums.items() if key[half] == c]
                    for value in found:
                        term = shift_cells(value, 1 - c)
                        part = term if part is None else part + term
                part = part.reshape(CELLS, PACK)
                total = part if half == 0 else total + pltpu.roll(part, C1, 1)
            top, bottom = total[: CELLS // 2], total[CELLS // 2 :]
            out_ref[p] = jnp.where(low_lanes(top.shape), top, pltpu.roll(bottom, C1, 1)).astype(bf16)
            return carry

        lax.fori_loop(0, planes, finish, 0)


def back_two(device, pieces, cots, weight, after):
    planes = sum(len(piece) for piece in pieces)
    block = 256
    steps = pl.cdiv(TAPS * C1, block)
    tiles = steps * block // PACK
    return pl.pallas_call(
        lambda *refs: back_two_kernel(planes, pieces, *refs),
        grid_spec=pltpu.PrefetchScalarGridSpec(
            num_scalar_prefetch=1,
            grid=(steps,),
            in_specs=[pl.BlockSpec(memory_space=pl.ANY)] * len(cots)
            + [pl.BlockSpec((block, C2), lambda n, s: (n, 0))]
            + [pl.BlockSpec(memory_space=pl.ANY)] * len(after),
            out_specs=pl.BlockSpec((planes, CELLS // 2, PACK), lambda n, s: (0, 0, 0)),
            scratch_shapes=[
                pltpu.VMEM((planes * CELLS, C2), bf16),
                pltpu.VMEM((tiles, planes + 2, LS + 2, LS, PACK), f32),
                pltpu.SemaphoreType.DMA((planes,)),
            ],
        ),
        out_shape=jax.ShapeDtypeStruct((planes, CELLS // 2, PACK), bf16),
        compiler_params=params(56),
        cost_estimate=pl.CostEstimate(
            flops=2 * planes * CELLS * TAPS * C1 * C2, bytes_accessed=6 << 20, transcendentals=0
        ),
    )(device, *cots, weight, *after)


def weight_two_kernel(a, planes, pieces, scale, device_ref, *refs):
    samples = len(pieces)
    field_refs, cot_refs = refs[:samples], refs[samples:]
    out_ref, cot_ref, flat_ref, lhs_ref, sems = refs[-5:]
    cells = planes * CELLS
    copies, first = [], 0
    for s in range(samples):
        refs_here = cot_refs[first : first + len(pieces[s])]
        copies += plane_copies(device_ref[0], pieces[s], refs_here, cot_ref, s * cells, sems)
        first += len(pieces[s])
    for copy in copies:
        copy.start()

    for s in range(samples):

        def cells_of(p):
            x = field_refs[s][p].astype(f32)
            return jnp.concatenate([x, pltpu.roll(x, C1, 1)], axis=0)

        for j in range(planes // 2):
            pair = jnp.concatenate([cells_of(2 * j), cells_of(2 * j + 1)], axis=0)
            flat_ref[s, :, j * PACK : (j + 1) * PACK] = pair.T[:C1]

    lane = lax.broadcasted_iota(jnp.int32, (1, cells), 1)
    plane, row, column = lane // CELLS, (lane // LS) % LS, lane % LS
    for b in range(3):
        for c in range(3):
            inside = (row + b >= 1) & (row + b <= LS) & (column + c >= 1) & (column + c <= LS)
            if a == 0:
                inside = inside & (plane > 0)
            elif a == 2:
                inside = inside & (plane < planes - 1)
            mask = inside.astype(f32)
            shift = (-(CELLS * (a - 1) + LS * (b - 1) + c - 1)) % cells
            t = 3 * b + c
            for s in range(samples):
                value = flat_ref[s]
                if shift:
                    value = pltpu.roll(value, shift, 1) * mask
                lhs_ref[t * C1 : (t + 1) * C1, s * cells : (s + 1) * cells] = value.astype(bf16)

    for copy in copies:
        copy.wait()
    out_ref[...] = jnp.dot(lhs_ref[...], cot_ref[...], preferred_element_type=f32) * scale


def weight_two(a, total, device, fields, pieces, cots, scale, after):
    samples = len(fields)
    planes = fields[0].shape[0]
    cells = planes * CELLS
    block = 9 * C1
    flat = [value for sample in cots for value in sample]
    extra = list(after) + ([] if total is None else [total])
    count = 1 + samples + len(flat) + len(extra)
    return pl.pallas_call(
        lambda *refs: weight_two_kernel(a, planes, pieces, scale, *refs),
        grid_spec=pltpu.PrefetchScalarGridSpec(
            num_scalar_prefetch=1,
            grid=(1,),
            in_specs=[pl.BlockSpec(field.shape, lambda n, s: (0, 0, 0)) for field in fields]
            + [pl.BlockSpec(memory_space=pl.ANY)] * (len(flat) + len(extra)),
            out_specs=pl.BlockSpec((block, C2), lambda n, s: (a, 0)),
            scratch_shapes=[
                pltpu.VMEM((samples * cells, C2), bf16),
                pltpu.VMEM((samples, C1, cells), f32),
                pltpu.VMEM((block, samples * cells), bf16),
                pltpu.SemaphoreType.DMA((samples * planes,)),
            ],
        ),
        out_shape=jax.ShapeDtypeStruct((TAPS * C1, C2), f32),
        input_output_aliases={} if total is None else {count - 1: 0},
        compiler_params=params(60),
        cost_estimate=pl.CostEstimate(
            flops=2 * samples * cells * 9 * C1 * C2, bytes_accessed=8 << 20, transcendentals=0
        ),
    )(device, *fields, *flat, *extra)


def grad_pre_kernel(pieces_ref, slope_ref, lhs_ref, *refs):
    grad_ref, partial_ref, spread_ref, packed_ref = refs[-4:]
    for r in range(BLOCK):
        for u in range(BLOCK // 2):
            piece = r * BLOCK + 2 * u
            first = pieces_ref[piece].astype(f32)
            second = pieces_ref[piece + 1].astype(f32)
            low = low_lanes(first.shape)
            top = jnp.where(low, first, pltpu.roll(second, C1, 1))
            bottom = jnp.where(low, pltpu.roll(first, C1, 1), second)
            for i in range(LS):
                source = top if i < LS // 2 else bottom
                start = (i % (LS // 2)) * LS
                spread_ref[u, pl.ds(BLOCK * i + r, LS, stride=LAT), :] = source[start : start + LS]
    grads = []
    for u in range(BLOCK // 2):
        lanes = slice(u * PACK, (u + 1) * PACK)
        value = (spread_ref[u] * slope_ref[:, lanes]).astype(bf16)
        grad_ref[:, lanes] = value
        grads.append(value)
    grad = jnp.concatenate(grads, axis=1)
    for lateral in range(9):
        window = lhs_ref[:, lateral * WINDOW : (lateral + 1) * WINDOW]
        product = lax.dot_general(window, grad, (((0,), (0,)), ((), ())), preferred_element_type=f32)
        for c in range(3):
            sums = []
            for parity in range(2):
                part = None
                for pair in range(BLOCK // 2):
                    column = 2 * pair + parity + c - 1
                    slot = column if column >= 0 else BLOCK + 1
                    term = product[slot * C1 : (slot + 1) * C1, pair * PACK : (pair + 1) * PACK]
                    part = term if part is None else part + term
                sums.append(part)
            total = sums[0] + pltpu.roll(sums[1], C1, 1)
            top, bottom = total[: C1 // 2], total[C1 // 2 :]
            t = 3 * lateral + c
            packed_ref[t * (C1 // 2) : (t + 1) * (C1 // 2)] = jnp.where(
                low_lanes(top.shape), top, pltpu.roll(bottom, C1, 1)
            )
    packed_ref[TAPS * (C1 // 2) :] = jnp.zeros(((32 - TAPS) * (C1 // 2), PACK), f32)
    for row in range(C1 // 2):
        entry = packed_ref[pl.ds(row, 32, stride=C1 // 2), :]
        partial_ref[row] = entry.astype(bf16)


def grad_pre_of(pieces, slope, lhs, after):
    rows = LS * LAT
    whole = pl.BlockSpec(memory_space=pltpu.VMEM)
    return pl.pallas_call(
        grad_pre_kernel,
        in_specs=[whole] * 3 + [pl.BlockSpec(memory_space=pl.ANY)] * len(after),
        out_shape=(
            jax.ShapeDtypeStruct((rows, GROUP), bf16),
            jax.ShapeDtypeStruct((C1 // 2, 32, PACK), bf16),
        ),
        scratch_shapes=[
            pltpu.VMEM((BLOCK // 2, rows, PACK), f32),
            pltpu.VMEM((32 * (C1 // 2), PACK), f32),
        ],
        compiler_params=params(24),
        cost_estimate=pl.CostEstimate(
            flops=2 * rows * 9 * WINDOW * GROUP, bytes_accessed=3 << 20, transcendentals=0
        ),
    )(pieces, slope, lhs, *after)


def back_one_kernel(before_ref, own_ref, after_ref, w_ref, out_ref, lhs_ref):
    for a, ref in enumerate((before_ref, own_ref, after_ref)):
        write_windows(lhs_ref, a, [ref[g * LAT : (g + 1) * LAT].astype(f32) for g in range(LS)])
    result = jnp.dot(lhs_ref[...], w_ref[...], preferred_element_type=f32)
    for g in range(LS):
        out_ref[:, g * GROUP : (g + 1) * GROUP] = result[g * LAT : (g + 1) * LAT].astype(bf16)


def back_one(before, own, after, band):
    rows = LS * LAT
    return pl.pallas_call(
        back_one_kernel,
        out_shape=jax.ShapeDtypeStruct((LAT, LAT * C1), bf16),
        scratch_shapes=[pltpu.VMEM((rows, 9 * WINDOW), bf16)],
        compiler_params=params(24),
        cost_estimate=pl.CostEstimate(
            flops=2 * rows * 9 * WINDOW * GROUP, bytes_accessed=3 << 20, transcendentals=0
        ),
    )(before, own, after, band)


def sum_kernel(scale, shares_ref, *refs):
    out_ref = refs[-1]
    total = jnp.sum(shares_ref[...].astype(f32), axis=0) * scale
    out_ref[...] = jnp.broadcast_to(total.astype(bf16)[None], out_ref.shape)


def sum_shares(shares, scale, after):
    whole = pl.BlockSpec(memory_space=pltpu.VMEM)
    return pl.pallas_call(
        lambda *refs: sum_kernel(scale, *refs),
        in_specs=[whole] + [pl.BlockSpec(memory_space=pl.ANY)] * len(after),
        out_shape=jax.ShapeDtypeStruct(shares.shape, bf16),
        compiler_params=params(16),
        cost_estimate=pl.CostEstimate(flops=0, bytes_accessed=1 << 20, transcendentals=0),
    )(shares, *after)


def unpack_kernel(packed_ref, *refs):
    out_ref, wide_ref = refs[-2:]
    wide_ref[...] = packed_ref[...].astype(f32).reshape(wide_ref.shape)
    for t in range(TAPS):
        entry = wide_ref[pl.ds(t, C1 // 2, stride=32), :]
        out_ref[t] = jnp.concatenate([entry[:, :C1], entry[:, C1:]], axis=0)


def unpack(packed, after):
    whole = pl.BlockSpec(memory_space=pltpu.VMEM)
    return pl.pallas_call(
        unpack_kernel,
        in_specs=[whole] + [pl.BlockSpec(memory_space=pl.ANY)] * len(after),
        out_shape=jax.ShapeDtypeStruct((TAPS, C1, C1), f32),
        scratch_shapes=[pltpu.VMEM((32 * (C1 // 2), PACK), f32)],
        compiler_params=params(16),
        cost_estimate=pl.CostEstimate(flops=0, bytes_accessed=1 << 20, transcendentals=0),
    )(packed, *after)


def neighbours(value, axis):
    count = lax.axis_size(axis)
    before = lax.ppermute(value, axis, [(i, i + 1) for i in range(count - 1)])
    after = lax.ppermute(value, axis, [(i + 1, i) for i in range(count - 1)])
    return before, after


def flipped(value, difference):
    count = lax.axis_size("depth")
    return lax.ppermute(value, "depth", [(i, i ^ difference) for i in range(count)])


def over_samples(value):
    count = lax.axis_size("sample")
    return [value] + [
        lax.ppermute(value, "sample", [(i, (i + shift) % count) for i in range(count)])
        for shift in range(1, count)
    ]


def on_device(volume, conv1_weight, conv2_weight, cotangent):
    samples = lax.axis_size("sample")
    shards = lax.axis_size("depth")
    flat_two = conv2_weight.reshape(TAPS * C1, C2)
    own = volume.reshape(LAT, LAT * C1)
    device = lax.axis_index("depth").astype(jnp.int32).reshape(1)
    cot = cotangent.reshape(CELLS, C2)

    core, chip = 1, 2
    outer = list(range(4, shards, 4))
    before, after = neighbours(own, "depth")
    far = [flipped(cot, difference) for difference in outer]
    cot_chip = flipped(cot, chip)

    back_weight = jnp.swapaxes(conv1_weight[::-1], 1, 2)
    band = banded(conv1_weight)
    back_band = banded(back_weight)

    moved, slope, windows = conv_one(before, own, after, band)
    fields = lax.all_to_all(moved, "depth", split_axis=0, concat_axis=0, tiled=True)

    first = joined([cot, cot_chip] + far)
    last = flipped(joined(far), chip)
    pieces = [[0, chip] + outer, [difference + chip for difference in outer]]
    pieces = pieces + [[difference + core for difference in piece] for piece in pieces]
    all_cots, all_fields = [], over_samples(fields)
    for value in zip(over_samples(first), over_samples(last)):
        all_cots.append(list(value) + [flipped(part, core) for part in value])
    all_pieces = [pieces] * samples

    send, keep = conv_two(device, fields, flat_two)
    grad_pieces = back_two(device, pieces, all_cots[0], flat_two, [keep])

    received = flipped(send, core)
    half = keep.shape[0] // 2
    partial = keep.astype(f32) + received.astype(f32)
    received = flipped(partial[half:].astype(bf16), chip)
    partial = partial[:half] + received.astype(f32)
    features = partial[:CELLS]
    for k, difference in enumerate(outer):
        block = partial[(k + 1) * CELLS : (k + 2) * CELLS].astype(bf16)
        features = features + flipped(block, difference).astype(f32)
    features = features.astype(bf16)

    scale_two = 1.0 / math.sqrt(samples * shards * CELLS)

    def weight_part(a, total, after):
        return weight_two(a, total, device, all_fields, all_pieces, all_cots, scale_two, after)

    returned = lax.all_to_all(grad_pieces, "depth", split_axis=0, concat_axis=0, tiled=True)
    grad_two = weight_part(0, None, [grad_pieces])
    grad_pre, partial_one = grad_pre_of(returned, slope, windows, [grad_two])
    grad_before, grad_after = neighbours(grad_pre, "depth")

    devices = samples * shards
    both = ("sample", "depth")
    scale_one = 1.0 / math.sqrt(samples * shards * LAT * LAT)
    shares = partial_one.reshape(devices, -1, PACK)
    shares = lax.all_to_all(shares, both, split_axis=0, concat_axis=0, tiled=True)
    grad_two = weight_part(1, grad_two, [grad_pre])
    summed = sum_shares(shares, scale_one, [grad_two])
    shares = lax.all_to_all(summed, both, split_axis=0, concat_axis=0, tiled=True)
    grad_two = weight_part(2, grad_two, [summed])
    grad_volume = back_one(grad_before, grad_pre, grad_after, back_band)
    grad_conv1 = unpack(shares.reshape(C1 // 2, 32, PACK), [grad_two])
    grad_conv2 = grad_two

    return (
        features.reshape(cotangent.shape),
        grad_volume.reshape(volume.shape),
        grad_conv1,
        grad_conv2.reshape(conv2_weight.shape),
    )


def solution(mesh):
    return jax.shard_map(
        on_device,
        mesh=mesh,
        in_specs=(
            P("sample", "depth", None, None),
            P(),
            P(None, "depth", None),
            P("sample", "depth", None, None, None),
        ),
        out_specs=(
            P("sample", "depth", None, None, None),
            P("sample", "depth", None, None),
            P(),
            P(None, "depth", None),
        ),
        check_vma=False,
    )
```

```python
import math

import jax
import jax.numpy as jnp
from jax import lax
from jax.experimental import pallas as pl
from jax.experimental.pallas import tpu as pltpu
from jax.sharding import PartitionSpec as P

C1 = 64
LAT = 32
BLOCK = 4
C2 = 1024
LS = 8
CELLS = LS * LS
GROUP = BLOCK * C1
WINDOW = GROUP + 2 * C1
TAPS = 27
PACK = 2 * C1

root_coef = 0.7978845608028654
cubic_coef = 0.044715

f32 = jnp.float32
bf16 = jnp.bfloat16


def params(mebibytes):
    return pltpu.CompilerParams(vmem_limit_bytes=mebibytes * 1024 * 1024)


def low_lanes(shape):
    return lax.broadcasted_iota(jnp.int32, shape, len(shape) - 1) < C1


def band_kernel(w_ref, out_ref):
    for lateral in range(9):
        for slot in range(BLOCK + 2):
            column = slot if slot <= BLOCK else -1
            for pair in range(BLOCK // 2):
                halves = []
                for own in (2 * pair, 2 * pair + 1):
                    c = column - own + 1
                    if 0 <= c <= 2:
                        halves.append(w_ref[3 * lateral + c])
                    else:
                        halves.append(jnp.zeros((C1, C1), bf16))
                start = lateral * WINDOW + slot * C1
                out_ref[start : start + C1, pair * PACK : (pair + 1) * PACK] = jnp.concatenate(halves, axis=1)


def banded(weight):
    return pl.pallas_call(
        band_kernel,
        out_shape=jax.ShapeDtypeStruct((9 * WINDOW, GROUP), bf16),
        compiler_params=params(16),
        cost_estimate=pl.CostEstimate(flops=0, bytes_accessed=4 << 20, transcendentals=0),
    )(weight)


def write_windows(lhs_ref, a, groups):
    field = jnp.concatenate(groups, axis=0)
    blank = jnp.zeros((LAT, PACK), f32)
    after = jnp.concatenate([g[:, :PACK] for g in groups[1:]] + [blank], axis=0)
    before = jnp.concatenate([blank] + [g[:, GROUP - PACK :] for g in groups[:-1]], axis=0)
    edge = jnp.where(low_lanes(after.shape), after, before)
    window = jnp.concatenate([field, edge], axis=1)
    rows = window.shape[0]
    row = lax.broadcasted_iota(jnp.int32, window.shape, 0) % LAT
    shifted = [
        jnp.where(row == 0, 0.0, pltpu.roll(window, 1, 0)),
        window,
        jnp.where(row == LAT - 1, 0.0, pltpu.roll(window, rows - 1, 0)),
    ]
    for b in range(3):
        start = (3 * a + b) * WINDOW
        lhs_ref[:, start : start + WINDOW] = shifted[b].astype(bf16)


def conv_one_kernel(before_ref, own_ref, after_ref, w_ref, moved_ref, slope_ref, lhs_ref, hid_ref):
    for a, ref in enumerate((before_ref, own_ref, after_ref)):
        write_windows(lhs_ref, a, [ref[:, g * GROUP : (g + 1) * GROUP].astype(f32) for g in range(LS)])
    pre = jnp.dot(lhs_ref[...], w_ref[...], preferred_element_type=f32)
    tanh_val = jnp.tanh(root_coef * (pre + cubic_coef * pre * pre * pre))
    hidden = 0.5 * pre * (1.0 + tanh_val)
    slope_ref[...] = 0.5 * (1.0 + tanh_val) + 0.5 * pre * (1.0 - tanh_val * tanh_val) * root_coef * (
        1.0 + 3.0 * cubic_coef * pre * pre
    )
    for u in range(BLOCK // 2):
        hid_ref[u] = hidden[:, u * PACK : (u + 1) * PACK]
    for r in range(BLOCK):
        for u in range(BLOCK // 2):
            cells = jnp.concatenate(
                [hid_ref[u, pl.ds(BLOCK * i + r, LS, stride=LAT), :] for i in range(LS)], axis=0
            )
            top, bottom = cells[: CELLS // 2], cells[CELLS // 2 :]
            low = low_lanes(top.shape)
            piece = r * BLOCK + 2 * u
            moved_ref[piece] = jnp.where(low, top, pltpu.roll(bottom, C1, 1)).astype(bf16)
            moved_ref[piece + 1] = jnp.where(low, pltpu.roll(top, C1, 1), bottom).astype(bf16)


def conv_one(before, own, after, band):
    rows = LS * LAT
    return pl.pallas_call(
        conv_one_kernel,
        out_shape=(
            jax.ShapeDtypeStruct((BLOCK * BLOCK, CELLS // 2, PACK), bf16),
            jax.ShapeDtypeStruct((rows, GROUP), f32),
            jax.ShapeDtypeStruct((rows, 9 * WINDOW), bf16),
        ),
        scratch_shapes=[pltpu.VMEM((BLOCK // 2, rows, PACK), f32)],
        compiler_params=params(24),
        cost_estimate=pl.CostEstimate(
            flops=2 * rows * 9 * WINDOW * GROUP, bytes_accessed=5 << 20, transcendentals=rows * GROUP
        ),
    )(before, own, after, band)


def shift_cells(field, step):
    if step == 0:
        return field
    column = lax.broadcasted_iota(jnp.int32, field.shape, 1)
    edge = LS - 1 if step > 0 else 0
    return jnp.where(column == edge, 0.0, pltpu.roll(field, (-step) % LS, 1))


def shift_rows(field, step):
    if step == 0:
        return field
    blank = jnp.zeros((1,) + field.shape[1:], field.dtype)
    parts = [field[1:], blank] if step > 0 else [blank, field[:-1]]
    return jnp.concatenate(parts, axis=0)


def conv_two_kernel(planes, x_ref, w_ref, out_ref, lhs_ref):
    cells = planes * CELLS
    lateral = 9 * C1

    @pl.when(pl.program_id(0) == 0)
    def _():
        lhs_ref[:CELLS] = jnp.zeros((CELLS, lateral), bf16)
        lhs_ref[cells + CELLS :] = jnp.zeros((CELLS, lateral), bf16)

        def gather(p, carry):
            x = x_ref[p].astype(f32)
            turned = pltpu.roll(x, C1, 1)
            halves = []
            for parts in ((x, turned), (turned, x)):
                field = jnp.concatenate(parts, axis=0).reshape(LS, LS, PACK)
                halves.append([shift_cells(field, c - 1) for c in range(3)])
            rows = pl.ds(pl.multiple_of((p + 1) * CELLS, CELLS), CELLS)
            for m in range(5):
                t = 2 * m
                low = shift_rows(halves[0][t % 3], t // 3 - 1).reshape(CELLS, PACK)
                t = 2 * m + 1
                if t < 9:
                    high = shift_rows(halves[1][t % 3], t // 3 - 1).reshape(CELLS, PACK)
                    tile = jnp.where(low_lanes(low.shape), low, high)
                    lhs_ref[rows, m * PACK : (m + 1) * PACK] = tile.astype(bf16)
                else:
                    lhs_ref[rows, m * PACK : m * PACK + C1] = low[:, :C1].astype(bf16)
            return carry

        lax.fori_loop(0, planes, gather, 0)

    total = None
    for a in range(3):
        window = lhs_ref[a * CELLS : a * CELLS + cells]
        term = jnp.dot(window, w_ref[a * lateral : (a + 1) * lateral], preferred_element_type=f32)
        total = term if total is None else total + term
    out_ref[...] = total.astype(bf16)


def conv_two(fields, weight):
    planes = fields.shape[0]
    cells = planes * CELLS
    block = 512
    return pl.pallas_call(
        lambda *refs: conv_two_kernel(planes, *refs),
        grid=(C2 // block,),
        in_specs=[
            pl.BlockSpec(fields.shape, lambda n: (0, 0, 0)),
            pl.BlockSpec((TAPS * C1, block), lambda n: (0, n)),
        ],
        out_specs=pl.BlockSpec((cells, block), lambda n: (0, n)),
        out_shape=jax.ShapeDtypeStruct((cells, C2), bf16),
        scratch_shapes=[pltpu.VMEM((cells + 2 * CELLS, 9 * C1), bf16)],
        compiler_params=params(56),
        cost_estimate=pl.CostEstimate(
            flops=2 * cells * TAPS * C1 * C2, bytes_accessed=10 << 20, transcendentals=0
        ),
    )(fields, weight)


def plane_copies(device, pieces, refs, target_ref, base, sems):
    copies = []
    for differences, ref in zip(pieces, refs):
        for k, difference in enumerate(differences):
            row = pl.multiple_of(base + (device ^ difference) * CELLS, CELLS)
            source = ref.at[pl.ds(k * CELLS, CELLS), :]
            target = target_ref.at[pl.ds(row, CELLS), :]
            copies.append(pltpu.make_async_copy(source, target, sems.at[len(copies)]))
    return copies


def back_two_kernel(planes, pieces, device_ref, *refs):
    cot_refs = refs[: len(pieces)]
    w_ref, out_ref, cot_ref, sum_ref, sems = refs[len(pieces)], *refs[-4:]
    b = pl.program_id(0)
    cells = planes * CELLS

    @pl.when(b == 0)
    def _():
        copies = plane_copies(device_ref[0], pieces, cot_refs, cot_ref, CELLS, sems)
        for copy in copies:
            copy.start()
        cot_ref[:CELLS] = jnp.zeros((CELLS, C2), bf16)
        cot_ref[cells + CELLS :] = jnp.zeros((CELLS, C2), bf16)
        sum_ref[...] = jnp.zeros(sum_ref.shape, f32)
        for copy in copies:
            copy.wait()

    total = None
    for a in range(3):
        term = lax.dot_general(
            cot_ref[(2 - a) * CELLS : (2 - a) * CELLS + cells],
            w_ref[a],
            (((1,), (1,)), ((), ())),
            preferred_element_type=f32,
        )
        total = term if total is None else total + term
    rows = pl.ds(b, LS)
    first = total[:, :PACK].reshape(planes, LS, LS, PACK)
    sum_ref[0, :, rows] = sum_ref[0, :, rows] + first
    last = jnp.concatenate([total[:, PACK:], jnp.zeros((cells, C1), f32)], axis=1)
    sum_ref[1, :, rows] = sum_ref[1, :, rows] + last.reshape(planes, LS, LS, PACK)

    @pl.when(b == 2)
    def _():
        def finish(p, carry):
            pair = sum_ref[0, p, 1 : LS + 1]
            single = sum_ref[1, p, 1 : LS + 1]
            total = shift_cells(pair, 1) + shift_cells(single, -1)
            total = total.reshape(CELLS, PACK) + pltpu.roll(pair.reshape(CELLS, PACK), C1, 1)
            top, bottom = total[: CELLS // 2], total[CELLS // 2 :]
            out_ref[p] = jnp.where(low_lanes(top.shape), top, pltpu.roll(bottom, C1, 1)).astype(bf16)
            return carry

        lax.fori_loop(0, planes, finish, 0)


def back_two(device, pieces, cots, weight, after):
    planes = sum(len(piece) for piece in pieces)
    return pl.pallas_call(
        lambda *refs: back_two_kernel(planes, pieces, *refs),
        grid_spec=pltpu.PrefetchScalarGridSpec(
            num_scalar_prefetch=1,
            grid=(3,),
            in_specs=[pl.BlockSpec(memory_space=pl.ANY)] * len(cots)
            + [pl.BlockSpec((3, 3 * C1, C2), lambda n, s: (0, n, 0))]
            + [pl.BlockSpec(memory_space=pl.ANY)] * len(after),
            out_specs=pl.BlockSpec((planes, CELLS // 2, PACK), lambda n, s: (0, 0, 0)),
            scratch_shapes=[
                pltpu.VMEM(((planes + 2) * CELLS, C2), bf16),
                pltpu.VMEM((2, planes, LS + 2, LS, PACK), f32),
                pltpu.SemaphoreType.DMA((planes,)),
            ],
        ),
        out_shape=jax.ShapeDtypeStruct((planes, CELLS // 2, PACK), bf16),
        compiler_params=params(56),
        cost_estimate=pl.CostEstimate(
            flops=2 * planes * CELLS * TAPS * C1 * C2, bytes_accessed=6 << 20, transcendentals=0
        ),
    )(device, *cots, weight.reshape(3, 9 * C1, C2), *after)


def weight_two_kernel(planes, pieces, scale, device_ref, *refs):
    samples = len(pieces)
    field_refs, cot_refs = refs[:samples], refs[samples:]
    out_ref, cot_ref, flat_ref, lhs_ref, sems = refs[-5:]
    cells = planes * CELLS
    a = pl.program_id(0)

    @pl.when(a == 0)
    def _():
        copies, first = [], 0
        for s in range(samples):
            refs_here = cot_refs[first : first + len(pieces[s])]
            copies += plane_copies(device_ref[0], pieces[s], refs_here, cot_ref.at[s], CELLS, sems.at[s])
            first += len(pieces[s])
        for copy in copies:
            copy.start()
        for s in range(samples):
            cot_ref[s, :CELLS] = jnp.zeros((CELLS, C2), bf16)
            cot_ref[s, cells + CELLS :] = jnp.zeros((CELLS, C2), bf16)

            def cells_of(p):
                x = field_refs[s][p].astype(f32)
                return jnp.concatenate([x, pltpu.roll(x, C1, 1)], axis=0)

            for j in range(planes // 2):
                pair = jnp.concatenate([cells_of(2 * j), cells_of(2 * j + 1)], axis=0)
                flat_ref[s, :, j * PACK : (j + 1) * PACK] = pair.T[:C1]

        lane = lax.broadcasted_iota(jnp.int32, (1, cells), 1)
        row, column = (lane // LS) % LS, lane % LS
        for b in range(3):
            for c in range(3):
                inside = (row + b >= 1) & (row + b <= LS) & (column + c >= 1) & (column + c <= LS)
                mask = inside.astype(f32)
                shift = (-(LS * (b - 1) + c - 1)) % cells
                t = 3 * b + c
                for s in range(samples):
                    value = flat_ref[s]
                    if shift:
                        value = pltpu.roll(value, shift, 1) * mask
                    lhs_ref[s, t * C1 : (t + 1) * C1] = value.astype(bf16)
        for copy in copies:
            copy.wait()

    rows = pl.ds(pl.multiple_of((2 - a) * CELLS, CELLS), cells)
    total = None
    for s in range(samples):
        term = jnp.dot(lhs_ref[s], cot_ref[s, rows], preferred_element_type=f32)
        total = term if total is None else total + term
    out_ref[...] = total * scale


def weight_two(device, fields, pieces, cots, scale, after):
    samples = len(fields)
    planes = fields[0].shape[0]
    cells = planes * CELLS
    block = 9 * C1
    flat = [value for sample in cots for value in sample]
    return pl.pallas_call(
        lambda *refs: weight_two_kernel(planes, pieces, scale, *refs),
        grid_spec=pltpu.PrefetchScalarGridSpec(
            num_scalar_prefetch=1,
            grid=(3,),
            in_specs=[pl.BlockSpec(field.shape, lambda n, s: (0, 0, 0)) for field in fields]
            + [pl.BlockSpec(memory_space=pl.ANY)] * (len(flat) + len(after)),
            out_specs=pl.BlockSpec((block, C2), lambda n, s: (n, 0)),
            scratch_shapes=[
                pltpu.VMEM((samples, (planes + 2) * CELLS, C2), bf16),
                pltpu.VMEM((samples, C1, cells), f32),
                pltpu.VMEM((samples, block, cells), bf16),
                pltpu.SemaphoreType.DMA((samples, planes)),
            ],
        ),
        out_shape=jax.ShapeDtypeStruct((TAPS * C1, C2), f32),
        compiler_params=params(40 if samples <= 2 else 58),
        cost_estimate=pl.CostEstimate(
            flops=2 * samples * cells * TAPS * C1 * C2, bytes_accessed=18 << 20, transcendentals=0
        ),
    )(device, *fields, *flat, *after)


def grad_pre_kernel(pieces_ref, slope_ref, lhs_ref, *refs):
    grad_ref, partial_ref, spread_ref, packed_ref = refs[-4:]
    for r in range(BLOCK):
        for u in range(BLOCK // 2):
            piece = r * BLOCK + 2 * u
            first = pieces_ref[piece].astype(f32)
            second = pieces_ref[piece + 1].astype(f32)
            low = low_lanes(first.shape)
            top = jnp.where(low, first, pltpu.roll(second, C1, 1))
            bottom = jnp.where(low, pltpu.roll(first, C1, 1), second)
            for i in range(LS):
                source = top if i < LS // 2 else bottom
                start = (i % (LS // 2)) * LS
                spread_ref[u, pl.ds(BLOCK * i + r, LS, stride=LAT), :] = source[start : start + LS]
    grads = []
    for u in range(BLOCK // 2):
        lanes = slice(u * PACK, (u + 1) * PACK)
        value = (spread_ref[u] * slope_ref[:, lanes]).astype(bf16)
        grad_ref[:, lanes] = value
        grads.append(value)
    grad = jnp.concatenate(grads, axis=1)
    for lateral in range(9):
        window = lhs_ref[:, lateral * WINDOW : (lateral + 1) * WINDOW]
        product = lax.dot_general(window, grad, (((0,), (0,)), ((), ())), preferred_element_type=f32)
        for c in range(3):
            sums = []
            for parity in range(2):
                part = None
                for pair in range(BLOCK // 2):
                    column = 2 * pair + parity + c - 1
                    slot = column if column >= 0 else BLOCK + 1
                    term = product[slot * C1 : (slot + 1) * C1, pair * PACK : (pair + 1) * PACK]
                    part = term if part is None else part + term
                sums.append(part)
            total = sums[0] + pltpu.roll(sums[1], C1, 1)
            top, bottom = total[: C1 // 2], total[C1 // 2 :]
            t = 3 * lateral + c
            packed_ref[t * (C1 // 2) : (t + 1) * (C1 // 2)] = jnp.where(
                low_lanes(top.shape), top, pltpu.roll(bottom, C1, 1)
            )
    packed_ref[TAPS * (C1 // 2) :] = jnp.zeros(((32 - TAPS) * (C1 // 2), PACK), f32)
    for row in range(C1 // 2):
        entry = packed_ref[pl.ds(row, 32, stride=C1 // 2), :]
        partial_ref[row] = entry.astype(bf16)


def grad_pre_of(pieces, slope, lhs, after):
    rows = LS * LAT
    whole = pl.BlockSpec(memory_space=pltpu.VMEM)
    return pl.pallas_call(
        grad_pre_kernel,
        in_specs=[whole] * 3 + [pl.BlockSpec(memory_space=pl.ANY)] * len(after),
        out_shape=(
            jax.ShapeDtypeStruct((rows, GROUP), bf16),
            jax.ShapeDtypeStruct((C1 // 2, 32, PACK), bf16),
        ),
        scratch_shapes=[
            pltpu.VMEM((BLOCK // 2, rows, PACK), f32),
            pltpu.VMEM((32 * (C1 // 2), PACK), f32),
        ],
        compiler_params=params(24),
        cost_estimate=pl.CostEstimate(
            flops=2 * rows * 9 * WINDOW * GROUP, bytes_accessed=3 << 20, transcendentals=0
        ),
    )(pieces, slope, lhs, *after)


def back_one_kernel(before_ref, own_ref, after_ref, w_ref, out_ref, lhs_ref):
    for a, ref in enumerate((before_ref, own_ref, after_ref)):
        write_windows(lhs_ref, a, [ref[g * LAT : (g + 1) * LAT].astype(f32) for g in range(LS)])
    result = jnp.dot(lhs_ref[...], w_ref[...], preferred_element_type=f32)
    for g in range(LS):
        out_ref[:, g * GROUP : (g + 1) * GROUP] = result[g * LAT : (g + 1) * LAT].astype(bf16)


def back_one(before, own, after, band):
    rows = LS * LAT
    return pl.pallas_call(
        back_one_kernel,
        out_shape=jax.ShapeDtypeStruct((LAT, LAT * C1), bf16),
        scratch_shapes=[pltpu.VMEM((rows, 9 * WINDOW), bf16)],
        compiler_params=params(24),
        cost_estimate=pl.CostEstimate(
            flops=2 * rows * 9 * WINDOW * GROUP, bytes_accessed=3 << 20, transcendentals=0
        ),
    )(before, own, after, band)


def sum_kernel(scale, shares_ref, *refs):
    out_ref = refs[-1]
    total = jnp.sum(shares_ref[...].astype(f32), axis=0) * scale
    out_ref[...] = jnp.broadcast_to(total.astype(bf16)[None], out_ref.shape)


def sum_shares(shares, scale, after):
    whole = pl.BlockSpec(memory_space=pltpu.VMEM)
    return pl.pallas_call(
        lambda *refs: sum_kernel(scale, *refs),
        in_specs=[whole] + [pl.BlockSpec(memory_space=pl.ANY)] * len(after),
        out_shape=jax.ShapeDtypeStruct(shares.shape, bf16),
        compiler_params=params(16),
        cost_estimate=pl.CostEstimate(flops=0, bytes_accessed=1 << 20, transcendentals=0),
    )(shares, *after)


def unpack_kernel(packed_ref, *refs):
    out_ref, wide_ref = refs[-2:]
    wide_ref[...] = packed_ref[...].astype(f32).reshape(wide_ref.shape)
    for t in range(TAPS):
        entry = wide_ref[pl.ds(t, C1 // 2, stride=32), :]
        out_ref[t] = jnp.concatenate([entry[:, :C1], entry[:, C1:]], axis=0)


def unpack(packed, after):
    whole = pl.BlockSpec(memory_space=pltpu.VMEM)
    return pl.pallas_call(
        unpack_kernel,
        in_specs=[whole] + [pl.BlockSpec(memory_space=pl.ANY)] * len(after),
        out_shape=jax.ShapeDtypeStruct((TAPS, C1, C1), f32),
        scratch_shapes=[pltpu.VMEM((32 * (C1 // 2), PACK), f32)],
        compiler_params=params(16),
        cost_estimate=pl.CostEstimate(flops=0, bytes_accessed=1 << 20, transcendentals=0),
    )(packed, *after)


def neighbours(value, axis):
    count = lax.axis_size(axis)
    before = lax.ppermute(value, axis, [(i, i + 1) for i in range(count - 1)])
    after = lax.ppermute(value, axis, [(i + 1, i) for i in range(count - 1)])
    return before, after


def flipped(value, difference):
    count = lax.axis_size("depth")
    return lax.ppermute(value, "depth", [(i, i ^ difference) for i in range(count)])


def over_samples(value):
    count = lax.axis_size("sample")
    return [value] + [
        lax.ppermute(value, "sample", [(i, (i + shift) % count) for i in range(count)])
        for shift in range(1, count)
    ]


def on_device(volume, conv1_weight, conv2_weight, cotangent):
    samples = lax.axis_size("sample")
    shards = lax.axis_size("depth")
    flat_two = conv2_weight.reshape(TAPS * C1, C2)
    own = volume.reshape(LAT, LAT * C1)
    device = lax.axis_index("depth").astype(jnp.int32).reshape(1)
    cot = cotangent.reshape(CELLS, C2)

    core, chip = 1, 2
    outer = list(range(4, shards, 4))
    before, after = neighbours(own, "depth")
    far = [flipped(cot, difference) for difference in outer]
    cot_chip = flipped(cot, chip)

    back_weight = jnp.swapaxes(conv1_weight[::-1], 1, 2)
    band = banded(conv1_weight)
    back_band = banded(back_weight)

    moved, slope, windows = conv_one(before, own, after, band)
    fields = lax.all_to_all(moved, "depth", split_axis=0, concat_axis=0, tiled=True)

    cots = [cot, cot_chip] + far + [flipped(value, chip) for value in far]
    pieces = [0, chip] + outer + [difference + chip for difference in outer]
    pieces = [[difference] for difference in pieces + [difference + core for difference in pieces]]
    all_cots = []
    for value in zip(*[over_samples(value) for value in cots]):
        all_cots.append(list(value) + [flipped(part, core) for part in value])
    all_pieces = [pieces] * samples

    partial = conv_two(fields, flat_two)
    features = lax.psum_scatter(partial, "depth", scatter_dimension=0, tiled=True)

    grad_pieces = back_two(device, pieces, all_cots[0], flat_two, [partial])
    grad_pieces = lax.all_to_all(grad_pieces, "depth", split_axis=0, concat_axis=0, tiled=True)
    grad_pre, partial_one = grad_pre_of(grad_pieces, slope, windows, [])
    grad_before, grad_after = neighbours(grad_pre, "depth")

    devices = samples * shards
    both = ("sample", "depth")
    scale_one = 1.0 / math.sqrt(samples * shards * LAT * LAT)
    shares = partial_one.reshape(devices, -1, PACK)
    shares = lax.all_to_all(shares, both, split_axis=0, concat_axis=0, tiled=True)
    scale_two = 1.0 / math.sqrt(samples * shards * CELLS)
    grad_conv2 = weight_two(
        device, over_samples(fields), all_pieces, all_cots, scale_two, [grad_pre]
    )
    summed = sum_shares(shares, scale_one, [grad_conv2])
    shares = lax.all_to_all(summed, both, split_axis=0, concat_axis=0, tiled=True)
    grad_volume = back_one(grad_before, grad_pre, grad_after, back_band)
    grad_conv1 = unpack(shares.reshape(C1 // 2, 32, PACK), [])

    return (
        features.reshape(cotangent.shape),
        grad_volume.reshape(volume.shape),
        grad_conv1,
        grad_conv2.reshape(conv2_weight.shape),
    )


def solution(mesh):
    return jax.shard_map(
        on_device,
        mesh=mesh,
        in_specs=(
            P("sample", "depth", None, None),
            P(),
            P(None, "depth", None),
            P("sample", "depth", None, None, None),
        ),
        out_specs=(
            P("sample", "depth", None, None, None),
            P("sample", "depth", None, None),
            P(),
            P(None, "depth", None),
        ),
        check_vma=False,
    )
```

```python
import math

import jax
import jax.numpy as jnp
from jax import lax
from jax.experimental import pallas as pl
from jax.experimental.pallas import tpu as pltpu
from jax.sharding import PartitionSpec as P

C1 = 64
LAT = 32
BLOCK = 4
C2 = 1024
LS = 8
CELLS = LS * LS
GROUP = BLOCK * C1
WINDOW = GROUP + 2 * C1
TAPS = 27
PACK = 2 * C1

root_coef = 0.7978845608028654
cubic_coef = 0.044715

f32 = jnp.float32
bf16 = jnp.bfloat16


def params(mebibytes):
    return pltpu.CompilerParams(vmem_limit_bytes=mebibytes * 1024 * 1024)


def low_lanes(shape):
    return lax.broadcasted_iota(jnp.int32, shape, len(shape) - 1) < C1


def band_kernel(w_ref, out_ref):
    for lateral in range(9):
        for slot in range(BLOCK + 2):
            column = slot if slot <= BLOCK else -1
            for pair in range(BLOCK // 2):
                halves = []
                for own in (2 * pair, 2 * pair + 1):
                    c = column - own + 1
                    if 0 <= c <= 2:
                        halves.append(w_ref[3 * lateral + c])
                    else:
                        halves.append(jnp.zeros((C1, C1), bf16))
                start = lateral * WINDOW + slot * C1
                out_ref[start : start + C1, pair * PACK : (pair + 1) * PACK] = jnp.concatenate(halves, axis=1)


def banded(weight):
    return pl.pallas_call(
        band_kernel,
        out_shape=jax.ShapeDtypeStruct((9 * WINDOW, GROUP), bf16),
        compiler_params=params(16),
        cost_estimate=pl.CostEstimate(flops=0, bytes_accessed=4 << 20, transcendentals=0),
    )(weight)


def write_windows(lhs_ref, a, groups):
    field = jnp.concatenate(groups, axis=0)
    blank = jnp.zeros((LAT, PACK), f32)
    after = jnp.concatenate([g[:, :PACK] for g in groups[1:]] + [blank], axis=0)
    before = jnp.concatenate([blank] + [g[:, GROUP - PACK :] for g in groups[:-1]], axis=0)
    edge = jnp.where(low_lanes(after.shape), after, before)
    window = jnp.concatenate([field, edge], axis=1)
    rows = window.shape[0]
    row = lax.broadcasted_iota(jnp.int32, window.shape, 0) % LAT
    shifted = [
        jnp.where(row == 0, 0.0, pltpu.roll(window, 1, 0)),
        window,
        jnp.where(row == LAT - 1, 0.0, pltpu.roll(window, rows - 1, 0)),
    ]
    for b in range(3):
        start = (3 * a + b) * WINDOW
        lhs_ref[:, start : start + WINDOW] = shifted[b].astype(bf16)


def conv_one_kernel(before_ref, own_ref, after_ref, w_ref, *refs):
    moved_ref, slope_ref, lhs_ref, hid_ref = refs[-4:]
    for a, ref in enumerate((before_ref, own_ref, after_ref)):
        write_windows(lhs_ref, a, [ref[:, g * GROUP : (g + 1) * GROUP].astype(f32) for g in range(LS)])
    pre = jnp.dot(lhs_ref[...], w_ref[...], preferred_element_type=f32)
    tanh_val = jnp.tanh(root_coef * (pre + cubic_coef * pre * pre * pre))
    hidden = 0.5 * pre * (1.0 + tanh_val)
    slope_ref[...] = 0.5 * (1.0 + tanh_val) + 0.5 * pre * (1.0 - tanh_val * tanh_val) * root_coef * (
        1.0 + 3.0 * cubic_coef * pre * pre
    )
    for u in range(BLOCK // 2):
        hid_ref[u] = hidden[:, u * PACK : (u + 1) * PACK]
    for r in range(BLOCK):
        for u in range(BLOCK // 2):
            cells = jnp.concatenate(
                [hid_ref[u, pl.ds(BLOCK * i + r, LS, stride=LAT), :] for i in range(LS)], axis=0
            )
            top, bottom = cells[: CELLS // 2], cells[CELLS // 2 :]
            low = low_lanes(top.shape)
            piece = r * BLOCK + 2 * u
            moved_ref[piece] = jnp.where(low, top, pltpu.roll(bottom, C1, 1)).astype(bf16)
            moved_ref[piece + 1] = jnp.where(low, pltpu.roll(top, C1, 1), bottom).astype(bf16)


def conv_one(before, own, after, band, waits):
    rows = LS * LAT
    whole = pl.BlockSpec(memory_space=pltpu.VMEM)
    return pl.pallas_call(
        conv_one_kernel,
        in_specs=[whole] * 4 + [pl.BlockSpec(memory_space=pltpu.HBM)] * len(waits),
        out_shape=(
            jax.ShapeDtypeStruct((BLOCK * BLOCK, CELLS // 2, PACK), bf16),
            jax.ShapeDtypeStruct((rows, GROUP), f32),
            jax.ShapeDtypeStruct((rows, 9 * WINDOW), bf16),
        ),
        scratch_shapes=[pltpu.VMEM((BLOCK // 2, rows, PACK), f32)],
        compiler_params=params(24),
        cost_estimate=pl.CostEstimate(
            flops=2 * rows * 9 * WINDOW * GROUP, bytes_accessed=5 << 20, transcendentals=rows * GROUP
        ),
    )(before, own, after, band, *waits)


def shift_cells(field, step):
    if step == 0:
        return field
    column = lax.broadcasted_iota(jnp.int32, field.shape, 1)
    edge = LS - 1 if step > 0 else 0
    return jnp.where(column == edge, 0.0, pltpu.roll(field, (-step) % LS, 1))


def conv_two_kernel(planes, x_ref, w_ref, *refs):
    out_ref, lhs_ref, v_ref = refs[-3:]

    @pl.when(pl.program_id(0) == 0)
    def _():
        v_ref[:, :, 0] = jnp.zeros((3, 2, LS + 2, LS, PACK), f32)
        v_ref[:, :, planes + 1] = jnp.zeros((3, 2, LS + 2, LS, PACK), f32)
        edge = jnp.zeros((LS, PACK), f32)

        def spread(p, carry):
            x = x_ref[p].astype(f32)
            turned = pltpu.roll(x, C1, 1)
            for half, parts in enumerate(((x, turned), (turned, x))):
                cells = jnp.concatenate(parts, axis=0).reshape(LS, LS, PACK)
                for c in range(3):
                    v_ref[c, half, p + 1, 0] = edge
                    v_ref[c, half, p + 1, 1 : LS + 1] = shift_cells(cells, c - 1)
                    v_ref[c, half, p + 1, LS + 1] = edge
            return carry

        lax.fori_loop(0, planes, spread, 0)

        def gather(p, carry):
            rows = pl.ds(pl.multiple_of(p * CELLS, CELLS), CELLS)
            for m in range((TAPS + 1) // 2):
                t = 2 * m
                low = v_ref[t % 3, 0, p + t // 9, pl.ds((t // 3) % 3, LS)].reshape(CELLS, PACK)
                t = 2 * m + 1
                if t < TAPS:
                    high = v_ref[t % 3, 1, p + t // 9, pl.ds((t // 3) % 3, LS)].reshape(CELLS, PACK)
                    tile = jnp.where(low_lanes(low.shape), low, high)
                    lhs_ref[rows, m * PACK : (m + 1) * PACK] = tile.astype(bf16)
                else:
                    lhs_ref[rows, m * PACK : m * PACK + C1] = low[:, :C1].astype(bf16)
            return carry

        lax.fori_loop(0, planes, gather, 0)

    chunk = 4 * CELLS
    for m in range(planes * CELLS // chunk):
        rows = slice(m * chunk, (m + 1) * chunk)
        out_ref[rows] = jnp.dot(lhs_ref[rows], w_ref[...], preferred_element_type=f32).astype(bf16)


def conv_two(pieces, weight, after):
    planes = pieces.shape[0]
    cells = planes * CELLS
    block = 256
    return pl.pallas_call(
        lambda *refs: conv_two_kernel(planes, *refs),
        grid=(C2 // block,),
        in_specs=[
            pl.BlockSpec(pieces.shape, lambda n: (0, 0, 0)),
            pl.BlockSpec((TAPS * C1, block), lambda n: (0, n)),
        ]
        + [pl.BlockSpec(memory_space=pltpu.HBM)] * len(after),
        out_specs=pl.BlockSpec((cells, block), lambda n: (0, n)),
        out_shape=jax.ShapeDtypeStruct((cells, C2), bf16),
        scratch_shapes=[
            pltpu.VMEM((cells, TAPS * C1), bf16),
            pltpu.VMEM((3, 2, planes + 2, LS + 2, LS, PACK), f32),
        ],
        compiler_params=params(56),
        cost_estimate=pl.CostEstimate(
            flops=2 * cells * TAPS * C1 * C2, bytes_accessed=10 << 20, transcendentals=0
        ),
    )(pieces, weight, *after)


def join_kernel(count, *refs):
    out_ref, first = refs[-1], 0
    for ref in refs[:count]:
        rows = ref.shape[0]
        out_ref[first : first + rows] = ref[...]
        first += rows


def joined(values, after=()):
    rows = sum(value.shape[0] for value in values)
    columns = values[0].shape[1]
    return pl.pallas_call(
        lambda *refs: join_kernel(len(values), *refs),
        grid=(1,),
        in_specs=[pl.BlockSpec(value.shape, lambda n: (0, 0)) for value in values]
        + [pl.BlockSpec(memory_space=pl.ANY)] * len(after),
        out_specs=pl.BlockSpec((rows, columns), lambda n: (0, 0)),
        out_shape=jax.ShapeDtypeStruct((rows, columns), values[0].dtype),
        compiler_params=params(32),
        cost_estimate=pl.CostEstimate(flops=0, bytes_accessed=4 * rows * columns, transcendentals=0),
    )(*values, *after)


def plane_copies(device, pieces, refs, target_ref, base, sems):
    copies = []
    for differences, ref in zip(pieces, refs):
        for k, difference in enumerate(differences):
            row = pl.multiple_of(base + (device ^ difference) * CELLS, CELLS)
            source = ref.at[pl.ds(k * CELLS, CELLS), :]
            target = target_ref.at[pl.ds(row, CELLS), :]
            copies.append(pltpu.make_async_copy(source, target, sems.at[len(copies)]))
    return copies


def back_two_kernel(planes, pieces, device_ref, *refs):
    cot_refs = refs[: len(pieces)]
    w_ref, out_ref, cot_ref, sum_ref, sems = refs[len(pieces)], *refs[-4:]
    b = pl.program_id(0)
    cells = planes * CELLS

    @pl.when(b == 0)
    def _():
        copies = plane_copies(device_ref[0], pieces, cot_refs, cot_ref, CELLS, sems)
        for copy in copies:
            copy.start()
        cot_ref[:CELLS] = jnp.zeros((CELLS, C2), bf16)
        cot_ref[cells + CELLS :] = jnp.zeros((CELLS, C2), bf16)
        sum_ref[...] = jnp.zeros(sum_ref.shape, f32)
        for copy in copies:
            copy.wait()

    total = None
    for a in range(3):
        term = lax.dot_general(
            cot_ref[(2 - a) * CELLS : (2 - a) * CELLS + cells],
            w_ref[a],
            (((1,), (1,)), ((), ())),
            preferred_element_type=f32,
        )
        total = term if total is None else total + term
    rows = pl.ds(b, LS)
    first = total[:, :PACK].reshape(planes, LS, LS, PACK)
    sum_ref[0, :, rows] = sum_ref[0, :, rows] + first
    last = jnp.concatenate([total[:, PACK:], jnp.zeros((cells, C1), f32)], axis=1)
    sum_ref[1, :, rows] = sum_ref[1, :, rows] + last.reshape(planes, LS, LS, PACK)

    @pl.when(b == 2)
    def _():
        def finish(p, carry):
            pair = sum_ref[0, p, 1 : LS + 1]
            single = sum_ref[1, p, 1 : LS + 1]
            total = shift_cells(pair, 1) + shift_cells(single, -1)
            total = total.reshape(CELLS, PACK) + pltpu.roll(pair.reshape(CELLS, PACK), C1, 1)
            top, bottom = total[: CELLS // 2], total[CELLS // 2 :]
            out_ref[p] = jnp.where(low_lanes(top.shape), top, pltpu.roll(bottom, C1, 1)).astype(bf16)
            return carry

        lax.fori_loop(0, planes, finish, 0)


def back_two(device, pieces, cots, weight, after):
    planes = sum(len(piece) for piece in pieces)
    return pl.pallas_call(
        lambda *refs: back_two_kernel(planes, pieces, *refs),
        grid_spec=pltpu.PrefetchScalarGridSpec(
            num_scalar_prefetch=1,
            grid=(3,),
            in_specs=[pl.BlockSpec(memory_space=pltpu.HBM)] * len(cots)
            + [pl.BlockSpec((3, 3 * C1, C2), lambda n, s: (0, n, 0))]
            + [pl.BlockSpec(memory_space=pltpu.HBM)] * len(after),
            out_specs=pl.BlockSpec((planes, CELLS // 2, PACK), lambda n, s: (0, 0, 0)),
            scratch_shapes=[
                pltpu.VMEM(((planes + 2) * CELLS, C2), bf16),
                pltpu.VMEM((2, planes, LS + 2, LS, PACK), f32),
                pltpu.SemaphoreType.DMA((planes,)),
            ],
        ),
        out_shape=jax.ShapeDtypeStruct((planes, CELLS // 2, PACK), bf16),
        compiler_params=params(56),
        cost_estimate=pl.CostEstimate(
            flops=2 * planes * CELLS * TAPS * C1 * C2, bytes_accessed=6 << 20, transcendentals=0
        ),
    )(device, *cots, weight.reshape(3, 9 * C1, C2), *after)


def weight_two_kernel(planes, pieces, scale, device_ref, *refs):
    samples = len(pieces)
    field_refs, cot_refs = refs[:samples], refs[samples:]
    out_ref, token_ref, cot_ref, flat_ref, lhs_ref, sems = refs[-6:]
    cells = planes * CELLS
    a = pl.program_id(0)

    @pl.when(a == 0)
    def _():
        copies, first = [], 0
        for s in range(samples):
            refs_here = cot_refs[first : first + len(pieces[s])]
            copies += plane_copies(device_ref[0], pieces[s], refs_here, cot_ref.at[s], CELLS, sems.at[s])
            first += len(pieces[s])
        for copy in copies:
            copy.start()
        for s in range(samples):
            cot_ref[s, :CELLS] = jnp.zeros((CELLS, C2), bf16)
            cot_ref[s, cells + CELLS :] = jnp.zeros((CELLS, C2), bf16)

            def cells_of(p):
                x = field_refs[s][p].astype(f32)
                return jnp.concatenate([x, pltpu.roll(x, C1, 1)], axis=0)

            for j in range(planes // 2):
                pair = jnp.concatenate([cells_of(2 * j), cells_of(2 * j + 1)], axis=0)
                flat_ref[s, :, j * PACK : (j + 1) * PACK] = pair.T[:C1]

        lane = lax.broadcasted_iota(jnp.int32, (1, cells), 1)
        row, column = (lane // LS) % LS, lane % LS
        for b in range(3):
            for c in range(3):
                inside = (row + b >= 1) & (row + b <= LS) & (column + c >= 1) & (column + c <= LS)
                mask = inside.astype(f32)
                shift = (-(LS * (b - 1) + c - 1)) % cells
                t = 3 * b + c
                for s in range(samples):
                    value = flat_ref[s]
                    if shift:
                        value = pltpu.roll(value, shift, 1) * mask
                    lhs_ref[s, t * C1 : (t + 1) * C1] = value.astype(bf16)
        for copy in copies:
            copy.wait()

    rows = pl.ds(pl.multiple_of((2 - a) * CELLS, CELLS), cells)
    total = None
    for s in range(samples):
        term = jnp.dot(lhs_ref[s], cot_ref[s, rows], preferred_element_type=f32)
        total = term if total is None else total + term
    out_ref[...] = total * scale
    token_ref[...] = jnp.zeros(token_ref.shape, f32)


def weight_two(device, fields, pieces, cots, scale, after):
    samples = len(fields)
    planes = fields[0].shape[0]
    cells = planes * CELLS
    block = 9 * C1
    flat = [value for sample in cots for value in sample]
    return pl.pallas_call(
        lambda *refs: weight_two_kernel(planes, pieces, scale, *refs),
        grid_spec=pltpu.PrefetchScalarGridSpec(
            num_scalar_prefetch=1,
            grid=(3,),
            in_specs=[pl.BlockSpec(field.shape, lambda n, s: (0, 0, 0)) for field in fields]
            + [pl.BlockSpec(memory_space=pltpu.HBM)] * (len(flat) + len(after)),
            out_specs=(
                pl.BlockSpec((block, C2), lambda n, s: (n, 0)),
                pl.BlockSpec((8, PACK), lambda n, s: (0, 0)),
            ),
            scratch_shapes=[
                pltpu.VMEM((samples, (planes + 2) * CELLS, C2), bf16),
                pltpu.VMEM((samples, C1, cells), f32),
                pltpu.VMEM((samples, block, cells), bf16),
                pltpu.SemaphoreType.DMA((samples, planes)),
            ],
        ),
        out_shape=(
            jax.ShapeDtypeStruct((TAPS * C1, C2), f32),
            jax.ShapeDtypeStruct((8, PACK), f32),
        ),
        compiler_params=params(60),
        cost_estimate=pl.CostEstimate(
            flops=2 * samples * cells * TAPS * C1 * C2, bytes_accessed=18 << 20, transcendentals=0
        ),
    )(device, *fields, *flat, *after)


def grad_pre_kernel(pieces_ref, slope_ref, lhs_ref, *refs):
    grad_ref, partial_ref, spread_ref, packed_ref = refs[-4:]
    for r in range(BLOCK):
        for u in range(BLOCK // 2):
            piece = r * BLOCK + 2 * u
            first = pieces_ref[piece].astype(f32)
            second = pieces_ref[piece + 1].astype(f32)
            low = low_lanes(first.shape)
            top = jnp.where(low, first, pltpu.roll(second, C1, 1))
            bottom = jnp.where(low, pltpu.roll(first, C1, 1), second)
            for i in range(LS):
                source = top if i < LS // 2 else bottom
                start = (i % (LS // 2)) * LS
                spread_ref[u, pl.ds(BLOCK * i + r, LS, stride=LAT), :] = source[start : start + LS]
    grads = []
    for u in range(BLOCK // 2):
        lanes = slice(u * PACK, (u + 1) * PACK)
        value = (spread_ref[u] * slope_ref[:, lanes]).astype(bf16)
        grad_ref[:, lanes] = value
        grads.append(value)
    grad = jnp.concatenate(grads, axis=1)
    for lateral in range(9):
        window = lhs_ref[:, lateral * WINDOW : (lateral + 1) * WINDOW]
        product = lax.dot_general(window, grad, (((0,), (0,)), ((), ())), preferred_element_type=f32)
        for c in range(3):
            sums = []
            for parity in range(2):
                part = None
                for pair in range(BLOCK // 2):
                    column = 2 * pair + parity + c - 1
                    slot = column if column >= 0 else BLOCK + 1
                    term = product[slot * C1 : (slot + 1) * C1, pair * PACK : (pair + 1) * PACK]
                    part = term if part is None else part + term
                sums.append(part)
            total = sums[0] + pltpu.roll(sums[1], C1, 1)
            top, bottom = total[: C1 // 2], total[C1 // 2 :]
            t = 3 * lateral + c
            packed_ref[t * (C1 // 2) : (t + 1) * (C1 // 2)] = jnp.where(
                low_lanes(top.shape), top, pltpu.roll(bottom, C1, 1)
            )
    packed_ref[TAPS * (C1 // 2) :] = jnp.zeros(((32 - TAPS) * (C1 // 2), PACK), f32)
    for row in range(C1 // 2):
        entry = packed_ref[pl.ds(row, 32, stride=C1 // 2), :]
        partial_ref[row] = entry.astype(bf16)


def grad_pre_of(pieces, slope, lhs, after):
    rows = LS * LAT
    whole = pl.BlockSpec(memory_space=pltpu.VMEM)
    return pl.pallas_call(
        grad_pre_kernel,
        in_specs=[whole] * 3 + [pl.BlockSpec(memory_space=pltpu.HBM)] * len(after),
        out_shape=(
            jax.ShapeDtypeStruct((rows, GROUP), bf16),
            jax.ShapeDtypeStruct((C1 // 2, 32, PACK), bf16),
        ),
        scratch_shapes=[
            pltpu.VMEM((BLOCK // 2, rows, PACK), f32),
            pltpu.VMEM((32 * (C1 // 2), PACK), f32),
        ],
        compiler_params=params(24),
        cost_estimate=pl.CostEstimate(
            flops=2 * rows * 9 * WINDOW * GROUP, bytes_accessed=3 << 20, transcendentals=0
        ),
    )(pieces, slope, lhs, *after)


def back_one_kernel(before_ref, own_ref, after_ref, w_ref, out_ref, lhs_ref):
    for a, ref in enumerate((before_ref, own_ref, after_ref)):
        write_windows(lhs_ref, a, [ref[g * LAT : (g + 1) * LAT].astype(f32) for g in range(LS)])
    result = jnp.dot(lhs_ref[...], w_ref[...], preferred_element_type=f32)
    for g in range(LS):
        out_ref[:, g * GROUP : (g + 1) * GROUP] = result[g * LAT : (g + 1) * LAT].astype(bf16)


def back_one(before, own, after, band):
    rows = LS * LAT
    return pl.pallas_call(
        back_one_kernel,
        out_shape=jax.ShapeDtypeStruct((LAT, LAT * C1), bf16),
        scratch_shapes=[pltpu.VMEM((rows, 9 * WINDOW), bf16)],
        compiler_params=params(24),
        cost_estimate=pl.CostEstimate(
            flops=2 * rows * 9 * WINDOW * GROUP, bytes_accessed=3 << 20, transcendentals=0
        ),
    )(before, own, after, band)


def sum_kernel(scale, shares_ref, *refs):
    out_ref = refs[-1]
    total = jnp.sum(shares_ref[...].astype(f32), axis=0) * scale
    out_ref[...] = jnp.broadcast_to(total.astype(bf16)[None], out_ref.shape)


def sum_shares(shares, scale, after):
    whole = pl.BlockSpec(memory_space=pltpu.VMEM)
    return pl.pallas_call(
        lambda *refs: sum_kernel(scale, *refs),
        in_specs=[whole] + [pl.BlockSpec(memory_space=pltpu.HBM)] * len(after),
        out_shape=jax.ShapeDtypeStruct(shares.shape, bf16),
        compiler_params=params(16),
        cost_estimate=pl.CostEstimate(flops=0, bytes_accessed=1 << 20, transcendentals=0),
    )(shares, *after)


def unpack_kernel(packed_ref, *refs):
    out_ref, wide_ref = refs[-2:]
    wide_ref[...] = packed_ref[...].astype(f32).reshape(wide_ref.shape)
    for t in range(TAPS):
        entry = wide_ref[pl.ds(t, C1 // 2, stride=32), :]
        out_ref[t] = jnp.concatenate([entry[:, :C1], entry[:, C1:]], axis=0)


def unpack(packed, after):
    whole = pl.BlockSpec(memory_space=pltpu.VMEM)
    return pl.pallas_call(
        unpack_kernel,
        in_specs=[whole] + [pl.BlockSpec(memory_space=pltpu.HBM)] * len(after),
        out_shape=jax.ShapeDtypeStruct((TAPS, C1, C1), f32),
        scratch_shapes=[pltpu.VMEM((32 * (C1 // 2), PACK), f32)],
        compiler_params=params(16),
        cost_estimate=pl.CostEstimate(flops=0, bytes_accessed=1 << 20, transcendentals=0),
    )(packed, *after)


def neighbours(value, axis):
    count = lax.axis_size(axis)
    before = lax.ppermute(value, axis, [(i, i + 1) for i in range(count - 1)])
    after = lax.ppermute(value, axis, [(i + 1, i) for i in range(count - 1)])
    return before, after


def flipped(value, difference):
    count = lax.axis_size("depth")
    return lax.ppermute(value, "depth", [(i, i ^ difference) for i in range(count)])


def over_samples(value):
    count = lax.axis_size("sample")
    return [value] + [
        lax.ppermute(value, "sample", [(i, (i + shift) % count) for i in range(count)])
        for shift in range(1, count)
    ]


def on_device(volume, conv1_weight, conv2_weight, cotangent):
    samples = lax.axis_size("sample")
    shards = lax.axis_size("depth")
    flat_two = conv2_weight.reshape(TAPS * C1, C2)
    own = volume.reshape(LAT, LAT * C1)
    device = lax.axis_index("depth").astype(jnp.int32).reshape(1)
    cot = cotangent.reshape(CELLS, C2)

    core, chip = 1, 2
    outer = list(range(4, shards, 4))
    before, after = neighbours(own, "depth")
    far = [flipped(cot, difference) for difference in outer]
    cot_chip = flipped(cot, chip)

    back_weight = jnp.swapaxes(conv1_weight[::-1], 1, 2)
    band = banded(conv1_weight)
    back_band = banded(back_weight)

    moved, slope, windows = conv_one(before, own, after, band, far)
    fields = lax.all_to_all(moved, "depth", split_axis=0, concat_axis=0, tiled=True)

    far = joined(far, [before, after])
    first = joined([cot, cot_chip, far])
    last = flipped(far, chip)
    pieces = [[0, chip] + outer, [difference + chip for difference in outer]]
    pieces = pieces + [[difference + core for difference in piece] for piece in pieces]
    all_cots, all_fields = [], over_samples(fields)
    for value in zip(over_samples(first), over_samples(last)):
        all_cots.append(list(value) + [flipped(part, core) for part in value])
    all_pieces = [pieces] * samples
    crossed = [part for value in all_cots[1:] for part in value[:2]]
    swapped = [part for value in all_cots[1:] for part in value[2:]]

    partial = conv_two(fields, flat_two, [last])
    features = lax.psum_scatter(partial, "depth", scatter_dimension=0, tiled=True)

    grad_pieces = back_two(device, pieces, all_cots[0], flat_two, [partial] + crossed)
    grad_pieces = lax.all_to_all(grad_pieces, "depth", split_axis=0, concat_axis=0, tiled=True)
    grad_pre, partial_one = grad_pre_of(grad_pieces, slope, windows, swapped + all_fields[1:])
    grad_before, grad_after = neighbours(grad_pre, "depth")

    devices = samples * shards
    both = ("sample", "depth")
    scale_one = 1.0 / math.sqrt(samples * shards * LAT * LAT)
    shares = partial_one.reshape(devices, -1, PACK)
    shares = lax.all_to_all(shares, both, split_axis=0, concat_axis=0, tiled=True)
    scale_two = 1.0 / math.sqrt(samples * shards * CELLS)
    grad_conv2, token = weight_two(
        device, all_fields, all_pieces, all_cots, scale_two, [grad_pre]
    )
    summed = sum_shares(shares, scale_one, [token])
    shares = lax.all_to_all(summed, both, split_axis=0, concat_axis=0, tiled=True)
    grad_volume = back_one(grad_before, grad_pre, grad_after, back_band)
    grad_conv1 = unpack(shares.reshape(C1 // 2, 32, PACK), [])

    return (
        features.reshape(cotangent.shape),
        grad_volume.reshape(volume.shape),
        grad_conv1,
        grad_conv2.reshape(conv2_weight.shape),
    )


def solution(mesh):
    return jax.shard_map(
        on_device,
        mesh=mesh,
        in_specs=(
            P("sample", "depth", None, None),
            P(),
            P(None, "depth", None),
            P("sample", "depth", None, None, None),
        ),
        out_specs=(
            P("sample", "depth", None, None, None),
            P("sample", "depth", None, None),
            P(),
            P(None, "depth", None),
        ),
        check_vma=False,
    )
```

```python
import math

import jax
import jax.numpy as jnp
from jax import lax
from jax.experimental import pallas as pl
from jax.experimental.pallas import tpu as pltpu
from jax.sharding import PartitionSpec as P

C1 = 64
LAT = 32
BLOCK = 4
C2 = 1024
LS = 8
CELLS = LS * LS
GROUP = BLOCK * C1
WINDOW = GROUP + 2 * C1
TAPS = 27
PACK = 2 * C1

root_coef = 0.7978845608028654
cubic_coef = 0.044715

f32 = jnp.float32
bf16 = jnp.bfloat16


def params(mebibytes):
    return pltpu.CompilerParams(vmem_limit_bytes=mebibytes * 1024 * 1024)


def low_lanes(shape):
    return lax.broadcasted_iota(jnp.int32, shape, len(shape) - 1) < C1


def band_kernel(w_ref, out_ref):
    for lateral in range(9):
        for slot in range(BLOCK + 2):
            column = slot if slot <= BLOCK else -1
            for pair in range(BLOCK // 2):
                halves = []
                for own in (2 * pair, 2 * pair + 1):
                    c = column - own + 1
                    if 0 <= c <= 2:
                        halves.append(w_ref[3 * lateral + c])
                    else:
                        halves.append(jnp.zeros((C1, C1), bf16))
                start = lateral * WINDOW + slot * C1
                out_ref[start : start + C1, pair * PACK : (pair + 1) * PACK] = jnp.concatenate(halves, axis=1)


def banded(weight):
    return pl.pallas_call(
        band_kernel,
        out_shape=jax.ShapeDtypeStruct((9 * WINDOW, GROUP), bf16),
        compiler_params=params(16),
        cost_estimate=pl.CostEstimate(flops=0, bytes_accessed=4 << 20, transcendentals=0),
    )(weight)


def write_windows(lhs_ref, a, groups):
    field = jnp.concatenate(groups, axis=0)
    blank = jnp.zeros((LAT, PACK), f32)
    after = jnp.concatenate([g[:, :PACK] for g in groups[1:]] + [blank], axis=0)
    before = jnp.concatenate([blank] + [g[:, GROUP - PACK :] for g in groups[:-1]], axis=0)
    edge = jnp.where(low_lanes(after.shape), after, before)
    window = jnp.concatenate([field, edge], axis=1)
    rows = window.shape[0]
    row = lax.broadcasted_iota(jnp.int32, window.shape, 0) % LAT
    shifted = [
        jnp.where(row == 0, 0.0, pltpu.roll(window, 1, 0)),
        window,
        jnp.where(row == LAT - 1, 0.0, pltpu.roll(window, rows - 1, 0)),
    ]
    for b in range(3):
        start = (3 * a + b) * WINDOW
        lhs_ref[:, start : start + WINDOW] = shifted[b].astype(bf16)


def conv_one_kernel(before_ref, own_ref, after_ref, w_ref, *refs):
    moved_ref, slope_ref, lhs_ref, hid_ref = refs[-4:]
    for a, ref in enumerate((before_ref, own_ref, after_ref)):
        write_windows(lhs_ref, a, [ref[:, g * GROUP : (g + 1) * GROUP].astype(f32) for g in range(LS)])
    pre = jnp.dot(lhs_ref[...], w_ref[...], preferred_element_type=f32)
    tanh_val = jnp.tanh(root_coef * (pre + cubic_coef * pre * pre * pre))
    hidden = 0.5 * pre * (1.0 + tanh_val)
    slope_ref[...] = 0.5 * (1.0 + tanh_val) + 0.5 * pre * (1.0 - tanh_val * tanh_val) * root_coef * (
        1.0 + 3.0 * cubic_coef * pre * pre
    )
    for u in range(BLOCK // 2):
        hid_ref[u] = hidden[:, u * PACK : (u + 1) * PACK]
    for r in range(BLOCK):
        for u in range(BLOCK // 2):
            cells = jnp.concatenate(
                [hid_ref[u, pl.ds(BLOCK * i + r, LS, stride=LAT), :] for i in range(LS)], axis=0
            )
            top, bottom = cells[: CELLS // 2], cells[CELLS // 2 :]
            low = low_lanes(top.shape)
            piece = r * BLOCK + 2 * u
            moved_ref[piece] = jnp.where(low, top, pltpu.roll(bottom, C1, 1)).astype(bf16)
            moved_ref[piece + 1] = jnp.where(low, pltpu.roll(top, C1, 1), bottom).astype(bf16)


def conv_one(before, own, after, band, waits):
    rows = LS * LAT
    whole = pl.BlockSpec(memory_space=pltpu.VMEM)
    return pl.pallas_call(
        conv_one_kernel,
        in_specs=[whole] * 4 + [pl.BlockSpec(memory_space=pl.ANY)] * len(waits),
        out_shape=(
            jax.ShapeDtypeStruct((BLOCK * BLOCK, CELLS // 2, PACK), bf16),
            jax.ShapeDtypeStruct((rows, GROUP), f32),
            jax.ShapeDtypeStruct((rows, 9 * WINDOW), bf16),
        ),
        scratch_shapes=[pltpu.VMEM((BLOCK // 2, rows, PACK), f32)],
        compiler_params=params(24),
        cost_estimate=pl.CostEstimate(
            flops=2 * rows * 9 * WINDOW * GROUP, bytes_accessed=5 << 20, transcendentals=rows * GROUP
        ),
    )(before, own, after, band, *waits)


def shift_cells(field, step):
    if step == 0:
        return field
    column = lax.broadcasted_iota(jnp.int32, field.shape, 1)
    edge = LS - 1 if step > 0 else 0
    return jnp.where(column == edge, 0.0, pltpu.roll(field, (-step) % LS, 1))


def conv_two_kernel(planes, x_ref, w_ref, *refs):
    out_ref, lhs_ref, v_ref = refs[-3:]

    @pl.when(pl.program_id(0) == 0)
    def _():
        v_ref[:, :, 0] = jnp.zeros((3, 2, LS + 2, LS, PACK), f32)
        v_ref[:, :, planes + 1] = jnp.zeros((3, 2, LS + 2, LS, PACK), f32)
        edge = jnp.zeros((LS, PACK), f32)

        def spread(p, carry):
            x = x_ref[p].astype(f32)
            turned = pltpu.roll(x, C1, 1)
            for half, parts in enumerate(((x, turned), (turned, x))):
                cells = jnp.concatenate(parts, axis=0).reshape(LS, LS, PACK)
                for c in range(3):
                    v_ref[c, half, p + 1, 0] = edge
                    v_ref[c, half, p + 1, 1 : LS + 1] = shift_cells(cells, c - 1)
                    v_ref[c, half, p + 1, LS + 1] = edge
            return carry

        lax.fori_loop(0, planes, spread, 0)

        def gather(p, carry):
            rows = pl.ds(pl.multiple_of(p * CELLS, CELLS), CELLS)
            for m in range((TAPS + 1) // 2):
                t = 2 * m
                low = v_ref[t % 3, 0, p + t // 9, pl.ds((t // 3) % 3, LS)].reshape(CELLS, PACK)
                t = 2 * m + 1
                if t < TAPS:
                    high = v_ref[t % 3, 1, p + t // 9, pl.ds((t // 3) % 3, LS)].reshape(CELLS, PACK)
                    tile = jnp.where(low_lanes(low.shape), low, high)
                    lhs_ref[rows, m * PACK : (m + 1) * PACK] = tile.astype(bf16)
                else:
                    lhs_ref[rows, m * PACK : m * PACK + C1] = low[:, :C1].astype(bf16)
            return carry

        lax.fori_loop(0, planes, gather, 0)

    chunk = 4 * CELLS
    for m in range(planes * CELLS // chunk):
        rows = slice(m * chunk, (m + 1) * chunk)
        out_ref[rows] = jnp.dot(lhs_ref[rows], w_ref[...], preferred_element_type=f32).astype(bf16)


def conv_two(pieces, weight, after):
    planes = pieces.shape[0]
    cells = planes * CELLS
    block = 256
    return pl.pallas_call(
        lambda *refs: conv_two_kernel(planes, *refs),
        grid=(C2 // block,),
        in_specs=[
            pl.BlockSpec(pieces.shape, lambda n: (0, 0, 0)),
            pl.BlockSpec((TAPS * C1, block), lambda n: (0, n)),
        ]
        + [pl.BlockSpec(memory_space=pl.ANY)] * len(after),
        out_specs=pl.BlockSpec((cells, block), lambda n: (0, n)),
        out_shape=jax.ShapeDtypeStruct((cells, C2), bf16),
        scratch_shapes=[
            pltpu.VMEM((cells, TAPS * C1), bf16),
            pltpu.VMEM((3, 2, planes + 2, LS + 2, LS, PACK), f32),
        ],
        compiler_params=params(56),
        cost_estimate=pl.CostEstimate(
            flops=2 * cells * TAPS * C1 * C2, bytes_accessed=10 << 20, transcendentals=0
        ),
    )(pieces, weight, *after)


def plane_copies(device, pieces, refs, target_ref, base, sems):
    copies = []
    for differences, ref in zip(pieces, refs):
        for k, difference in enumerate(differences):
            row = pl.multiple_of(base + (device ^ difference) * CELLS, CELLS)
            source = ref.at[pl.ds(k * CELLS, CELLS), :]
            target = target_ref.at[pl.ds(row, CELLS), :]
            copies.append(pltpu.make_async_copy(source, target, sems.at[len(copies)]))
    return copies


def back_two_kernel(planes, pieces, device_ref, *refs):
    cot_refs = refs[: len(pieces)]
    w_ref, out_ref, cot_ref, sum_ref, sems = refs[len(pieces)], *refs[-4:]
    b = pl.program_id(0)
    cells = planes * CELLS

    @pl.when(b == 0)
    def _():
        copies = plane_copies(device_ref[0], pieces, cot_refs, cot_ref, CELLS, sems)
        for copy in copies:
            copy.start()
        cot_ref[:CELLS] = jnp.zeros((CELLS, C2), bf16)
        cot_ref[cells + CELLS :] = jnp.zeros((CELLS, C2), bf16)
        sum_ref[...] = jnp.zeros(sum_ref.shape, f32)
        for copy in copies:
            copy.wait()

    total = None
    for a in range(3):
        term = lax.dot_general(
            cot_ref[(2 - a) * CELLS : (2 - a) * CELLS + cells],
            w_ref[a],
            (((1,), (1,)), ((), ())),
            preferred_element_type=f32,
        )
        total = term if total is None else total + term
    rows = pl.ds(b, LS)
    first = total[:, :PACK].reshape(planes, LS, LS, PACK)
    sum_ref[0, :, rows] = sum_ref[0, :, rows] + first
    last = jnp.concatenate([total[:, PACK:], jnp.zeros((cells, C1), f32)], axis=1)
    sum_ref[1, :, rows] = sum_ref[1, :, rows] + last.reshape(planes, LS, LS, PACK)

    @pl.when(b == 2)
    def _():
        def finish(p, carry):
            pair = sum_ref[0, p, 1 : LS + 1]
            single = sum_ref[1, p, 1 : LS + 1]
            total = shift_cells(pair, 1) + shift_cells(single, -1)
            total = total.reshape(CELLS, PACK) + pltpu.roll(pair.reshape(CELLS, PACK), C1, 1)
            top, bottom = total[: CELLS // 2], total[CELLS // 2 :]
            out_ref[p] = jnp.where(low_lanes(top.shape), top, pltpu.roll(bottom, C1, 1)).astype(bf16)
            return carry

        lax.fori_loop(0, planes, finish, 0)


def back_two(device, pieces, cots, weight, after):
    planes = sum(len(piece) for piece in pieces)
    return pl.pallas_call(
        lambda *refs: back_two_kernel(planes, pieces, *refs),
        grid_spec=pltpu.PrefetchScalarGridSpec(
            num_scalar_prefetch=1,
            grid=(3,),
            in_specs=[pl.BlockSpec(memory_space=pl.ANY)] * len(cots)
            + [pl.BlockSpec((3, 3 * C1, C2), lambda n, s: (0, n, 0))]
            + [pl.BlockSpec(memory_space=pl.ANY)] * len(after),
            out_specs=pl.BlockSpec((planes, CELLS // 2, PACK), lambda n, s: (0, 0, 0)),
            scratch_shapes=[
                pltpu.VMEM(((planes + 2) * CELLS, C2), bf16),
                pltpu.VMEM((2, planes, LS + 2, LS, PACK), f32),
                pltpu.SemaphoreType.DMA((planes,)),
            ],
        ),
        out_shape=jax.ShapeDtypeStruct((planes, CELLS // 2, PACK), bf16),
        compiler_params=params(56),
        cost_estimate=pl.CostEstimate(
            flops=2 * planes * CELLS * TAPS * C1 * C2, bytes_accessed=6 << 20, transcendentals=0
        ),
    )(device, *cots, weight.reshape(3, 9 * C1, C2), *after)


def weight_two_kernel(planes, pieces, scale, device_ref, *refs):
    samples = len(pieces)
    field_refs, cot_refs = refs[:samples], refs[samples:]
    out_ref, token_ref, cot_ref, flat_ref, lhs_ref, sems = refs[-6:]
    cells = planes * CELLS
    a = pl.program_id(0)

    @pl.when(a == 0)
    def _():
        copies, first = [], 0
        for s in range(samples):
            refs_here = cot_refs[first : first + len(pieces[s])]
            copies += plane_copies(device_ref[0], pieces[s], refs_here, cot_ref.at[s], CELLS, sems.at[s])
            first += len(pieces[s])
        for copy in copies:
            copy.start()
        for s in range(samples):
            cot_ref[s, :CELLS] = jnp.zeros((CELLS, C2), bf16)
            cot_ref[s, cells + CELLS :] = jnp.zeros((CELLS, C2), bf16)

            def cells_of(p):
                x = field_refs[s][p].astype(f32)
                return jnp.concatenate([x, pltpu.roll(x, C1, 1)], axis=0)

            for j in range(planes // 2):
                pair = jnp.concatenate([cells_of(2 * j), cells_of(2 * j + 1)], axis=0)
                flat_ref[s, :, j * PACK : (j + 1) * PACK] = pair.T[:C1]

        lane = lax.broadcasted_iota(jnp.int32, (1, cells), 1)
        row, column = (lane // LS) % LS, lane % LS
        for b in range(3):
            for c in range(3):
                inside = (row + b >= 1) & (row + b <= LS) & (column + c >= 1) & (column + c <= LS)
                mask = inside.astype(f32)
                shift = (-(LS * (b - 1) + c - 1)) % cells
                t = 3 * b + c
                for s in range(samples):
                    value = flat_ref[s]
                    if shift:
                        value = pltpu.roll(value, shift, 1) * mask
                    lhs_ref[s, t * C1 : (t + 1) * C1] = value.astype(bf16)
        for copy in copies:
            copy.wait()

    rows = pl.ds(pl.multiple_of((2 - a) * CELLS, CELLS), cells)
    total = None
    for s in range(samples):
        term = jnp.dot(lhs_ref[s], cot_ref[s, rows], preferred_element_type=f32)
        total = term if total is None else total + term
    out_ref[...] = total * scale
    token_ref[...] = jnp.zeros(token_ref.shape, f32)


def weight_two(device, fields, pieces, cots, scale, after):
    samples = len(fields)
    planes = fields[0].shape[0]
    cells = planes * CELLS
    block = 9 * C1
    flat = [value for sample in cots for value in sample]
    return pl.pallas_call(
        lambda *refs: weight_two_kernel(planes, pieces, scale, *refs),
        grid_spec=pltpu.PrefetchScalarGridSpec(
            num_scalar_prefetch=1,
            grid=(3,),
            in_specs=[pl.BlockSpec(field.shape, lambda n, s: (0, 0, 0)) for field in fields]
            + [pl.BlockSpec(memory_space=pl.ANY)] * (len(flat) + len(after)),
            out_specs=(
                pl.BlockSpec((block, C2), lambda n, s: (n, 0)),
                pl.BlockSpec((8, PACK), lambda n, s: (0, 0)),
            ),
            scratch_shapes=[
                pltpu.VMEM((samples, (planes + 2) * CELLS, C2), bf16),
                pltpu.VMEM((samples, C1, cells), f32),
                pltpu.VMEM((samples, block, cells), bf16),
                pltpu.SemaphoreType.DMA((samples, planes)),
            ],
        ),
        out_shape=(
            jax.ShapeDtypeStruct((TAPS * C1, C2), f32),
            jax.ShapeDtypeStruct((8, PACK), f32),
        ),
        compiler_params=params(60),
        cost_estimate=pl.CostEstimate(
            flops=2 * samples * cells * TAPS * C1 * C2, bytes_accessed=18 << 20, transcendentals=0
        ),
    )(device, *fields, *flat, *after)


def grad_pre_kernel(pieces_ref, slope_ref, lhs_ref, *refs):
    grad_ref, partial_ref, spread_ref, packed_ref = refs[-4:]
    for r in range(BLOCK):
        for u in range(BLOCK // 2):
            piece = r * BLOCK + 2 * u
            first = pieces_ref[piece].astype(f32)
            second = pieces_ref[piece + 1].astype(f32)
            low = low_lanes(first.shape)
            top = jnp.where(low, first, pltpu.roll(second, C1, 1))
            bottom = jnp.where(low, pltpu.roll(first, C1, 1), second)
            for i in range(LS):
                source = top if i < LS // 2 else bottom
                start = (i % (LS // 2)) * LS
                spread_ref[u, pl.ds(BLOCK * i + r, LS, stride=LAT), :] = source[start : start + LS]
    grads = []
    for u in range(BLOCK // 2):
        lanes = slice(u * PACK, (u + 1) * PACK)
        value = (spread_ref[u] * slope_ref[:, lanes]).astype(bf16)
        grad_ref[:, lanes] = value
        grads.append(value)
    grad = jnp.concatenate(grads, axis=1)
    for lateral in range(9):
        window = lhs_ref[:, lateral * WINDOW : (lateral + 1) * WINDOW]
        product = lax.dot_general(window, grad, (((0,), (0,)), ((), ())), preferred_element_type=f32)
        for c in range(3):
            sums = []
            for parity in range(2):
                part = None
                for pair in range(BLOCK // 2):
                    column = 2 * pair + parity + c - 1
                    slot = column if column >= 0 else BLOCK + 1
                    term = product[slot * C1 : (slot + 1) * C1, pair * PACK : (pair + 1) * PACK]
                    part = term if part is None else part + term
                sums.append(part)
            total = sums[0] + pltpu.roll(sums[1], C1, 1)
            top, bottom = total[: C1 // 2], total[C1 // 2 :]
            t = 3 * lateral + c
            packed_ref[t * (C1 // 2) : (t + 1) * (C1 // 2)] = jnp.where(
                low_lanes(top.shape), top, pltpu.roll(bottom, C1, 1)
            )
    packed_ref[TAPS * (C1 // 2) :] = jnp.zeros(((32 - TAPS) * (C1 // 2), PACK), f32)
    for row in range(C1 // 2):
        entry = packed_ref[pl.ds(row, 32, stride=C1 // 2), :]
        partial_ref[row] = entry.astype(bf16)


def grad_pre_of(pieces, slope, lhs, after):
    rows = LS * LAT
    whole = pl.BlockSpec(memory_space=pltpu.VMEM)
    return pl.pallas_call(
        grad_pre_kernel,
        in_specs=[whole] * 3 + [pl.BlockSpec(memory_space=pl.ANY)] * len(after),
        out_shape=(
            jax.ShapeDtypeStruct((rows, GROUP), bf16),
            jax.ShapeDtypeStruct((C1 // 2, 32, PACK), bf16),
        ),
        scratch_shapes=[
            pltpu.VMEM((BLOCK // 2, rows, PACK), f32),
            pltpu.VMEM((32 * (C1 // 2), PACK), f32),
        ],
        compiler_params=params(24),
        cost_estimate=pl.CostEstimate(
            flops=2 * rows * 9 * WINDOW * GROUP, bytes_accessed=3 << 20, transcendentals=0
        ),
    )(pieces, slope, lhs, *after)


def back_one_kernel(before_ref, own_ref, after_ref, w_ref, out_ref, lhs_ref):
    for a, ref in enumerate((before_ref, own_ref, after_ref)):
        write_windows(lhs_ref, a, [ref[g * LAT : (g + 1) * LAT].astype(f32) for g in range(LS)])
    result = jnp.dot(lhs_ref[...], w_ref[...], preferred_element_type=f32)
    for g in range(LS):
        out_ref[:, g * GROUP : (g + 1) * GROUP] = result[g * LAT : (g + 1) * LAT].astype(bf16)


def back_one(before, own, after, band):
    rows = LS * LAT
    return pl.pallas_call(
        back_one_kernel,
        out_shape=jax.ShapeDtypeStruct((LAT, LAT * C1), bf16),
        scratch_shapes=[pltpu.VMEM((rows, 9 * WINDOW), bf16)],
        compiler_params=params(24),
        cost_estimate=pl.CostEstimate(
            flops=2 * rows * 9 * WINDOW * GROUP, bytes_accessed=3 << 20, transcendentals=0
        ),
    )(before, own, after, band)


def sum_kernel(scale, shares_ref, *refs):
    out_ref = refs[-1]
    total = jnp.sum(shares_ref[...].astype(f32), axis=0) * scale
    out_ref[...] = jnp.broadcast_to(total.astype(bf16)[None], out_ref.shape)


def sum_shares(shares, scale, after):
    whole = pl.BlockSpec(memory_space=pltpu.VMEM)
    return pl.pallas_call(
        lambda *refs: sum_kernel(scale, *refs),
        in_specs=[whole] + [pl.BlockSpec(memory_space=pl.ANY)] * len(after),
        out_shape=jax.ShapeDtypeStruct(shares.shape, bf16),
        compiler_params=params(16),
        cost_estimate=pl.CostEstimate(flops=0, bytes_accessed=1 << 20, transcendentals=0),
    )(shares, *after)


def unpack_kernel(packed_ref, *refs):
    out_ref, wide_ref = refs[-2:]
    wide_ref[...] = packed_ref[...].astype(f32).reshape(wide_ref.shape)
    for t in range(TAPS):
        entry = wide_ref[pl.ds(t, C1 // 2, stride=32), :]
        out_ref[t] = jnp.concatenate([entry[:, :C1], entry[:, C1:]], axis=0)


def unpack(packed, after):
    whole = pl.BlockSpec(memory_space=pltpu.VMEM)
    return pl.pallas_call(
        unpack_kernel,
        in_specs=[whole] + [pl.BlockSpec(memory_space=pl.ANY)] * len(after),
        out_shape=jax.ShapeDtypeStruct((TAPS, C1, C1), f32),
        scratch_shapes=[pltpu.VMEM((32 * (C1 // 2), PACK), f32)],
        compiler_params=params(16),
        cost_estimate=pl.CostEstimate(flops=0, bytes_accessed=1 << 20, transcendentals=0),
    )(packed, *after)


def neighbours(value, axis):
    count = lax.axis_size(axis)
    before = lax.ppermute(value, axis, [(i, i + 1) for i in range(count - 1)])
    after = lax.ppermute(value, axis, [(i + 1, i) for i in range(count - 1)])
    return before, after


def flipped(value, difference):
    count = lax.axis_size("depth")
    return lax.ppermute(value, "depth", [(i, i ^ difference) for i in range(count)])


def over_samples(value):
    count = lax.axis_size("sample")
    return [value] + [
        lax.ppermute(value, "sample", [(i, (i + shift) % count) for i in range(count)])
        for shift in range(1, count)
    ]


def on_device(volume, conv1_weight, conv2_weight, cotangent):
    samples = lax.axis_size("sample")
    shards = lax.axis_size("depth")
    flat_two = conv2_weight.reshape(TAPS * C1, C2)
    own = volume.reshape(LAT, LAT * C1)
    device = lax.axis_index("depth").astype(jnp.int32).reshape(1)
    cot = cotangent.reshape(CELLS, C2)

    core, chip = 1, 2
    outer = list(range(4, shards, 4))
    far = [flipped(cot, difference) for difference in outer]
    before, after = neighbours(own, "depth")
    cot_chip = flipped(cot, chip)

    back_weight = jnp.swapaxes(conv1_weight[::-1], 1, 2)
    band = banded(conv1_weight)
    back_band = banded(back_weight)

    moved, slope, windows = conv_one(before, own, after, band, [])
    fields = lax.all_to_all(moved, "depth", split_axis=0, concat_axis=0, tiled=True)

    near = jnp.concatenate([cot, cot_chip], axis=0)
    far = jnp.concatenate(far, axis=0)
    far_chip = flipped(far, chip)
    cots = [near, far, far_chip]
    pieces = [[0, chip], outer, [difference + chip for difference in outer]]
    pieces = pieces + [[difference + core for difference in piece] for piece in pieces]

    partial = conv_two(fields, flat_two, [])
    features = lax.psum_scatter(partial, "depth", scatter_dimension=0, tiled=True)

    own_cots = cots + [flipped(value, core) for value in cots]
    half = jnp.concatenate(cots, axis=0)
    halves = [[difference for piece in group for difference in piece] for group in (pieces[:3], pieces[3:])]
    all_pieces, all_cots = [pieces], [own_cots]
    for value in over_samples(half)[1:]:
        all_pieces.append(halves)
        all_cots.append([value, flipped(value, core)])
    all_fields = over_samples(fields)
    swapped = [value[1] for value in all_cots[1:]]

    grad_pieces = back_two(device, pieces, own_cots, flat_two, [partial])
    grad_pieces = lax.all_to_all(grad_pieces, "depth", split_axis=0, concat_axis=0, tiled=True)
    grad_pre, partial_one = grad_pre_of(grad_pieces, slope, windows, swapped)
    grad_before, grad_after = neighbours(grad_pre, "depth")

    devices = samples * shards
    both = ("sample", "depth")
    scale_one = 1.0 / math.sqrt(samples * shards * LAT * LAT)
    shares = partial_one.reshape(devices, -1, PACK)
    shares = lax.all_to_all(shares, both, split_axis=0, concat_axis=0, tiled=True)
    scale_two = 1.0 / math.sqrt(samples * shards * CELLS)
    grad_conv2, token = weight_two(
        device, all_fields, all_pieces, all_cots, scale_two, [grad_pre]
    )
    summed = sum_shares(shares, scale_one, [token])
    shares = lax.all_to_all(summed, both, split_axis=0, concat_axis=0, tiled=True)
    grad_volume = back_one(grad_before, grad_pre, grad_after, back_band)
    grad_conv1 = unpack(shares.reshape(C1 // 2, 32, PACK), [])

    return (
        features.reshape(cotangent.shape),
        grad_volume.reshape(volume.shape),
        grad_conv1,
        grad_conv2.reshape(conv2_weight.shape),
    )


def solution(mesh):
    return jax.shard_map(
        on_device,
        mesh=mesh,
        in_specs=(
            P("sample", "depth", None, None),
            P(),
            P(None, "depth", None),
            P("sample", "depth", None, None, None),
        ),
        out_specs=(
            P("sample", "depth", None, None, None),
            P("sample", "depth", None, None),
            P(),
            P(None, "depth", None),
        ),
        check_vma=False,
    )
```

```python
import math

import jax
import jax.numpy as jnp
from jax import lax
from jax.experimental import pallas as pl
from jax.experimental.pallas import tpu as pltpu
from jax.sharding import PartitionSpec as P

C1 = 64
LAT = 32
BLOCK = 4
C2 = 1024
LS = 8
CELLS = LS * LS
GROUP = BLOCK * C1
WINDOW = GROUP + 2 * C1
TAPS = 27
PACK = 2 * C1

root_coef = 0.7978845608028654
cubic_coef = 0.044715

f32 = jnp.float32
bf16 = jnp.bfloat16


def params(mebibytes):
    return pltpu.CompilerParams(vmem_limit_bytes=mebibytes * 1024 * 1024)


def low_lanes(shape):
    return lax.broadcasted_iota(jnp.int32, shape, len(shape) - 1) < C1


def band_kernel(w_ref, out_ref):
    for lateral in range(9):
        for slot in range(BLOCK + 2):
            column = slot if slot <= BLOCK else -1
            for pair in range(BLOCK // 2):
                halves = []
                for own in (2 * pair, 2 * pair + 1):
                    c = column - own + 1
                    if 0 <= c <= 2:
                        halves.append(w_ref[3 * lateral + c])
                    else:
                        halves.append(jnp.zeros((C1, C1), bf16))
                start = lateral * WINDOW + slot * C1
                out_ref[start : start + C1, pair * PACK : (pair + 1) * PACK] = jnp.concatenate(halves, axis=1)


def banded(weight):
    return pl.pallas_call(
        band_kernel,
        out_shape=jax.ShapeDtypeStruct((9 * WINDOW, GROUP), bf16),
        compiler_params=params(16),
        cost_estimate=pl.CostEstimate(flops=0, bytes_accessed=4 << 20, transcendentals=0),
    )(weight)


def write_windows(lhs_ref, a, groups):
    field = jnp.concatenate(groups, axis=0)
    blank = jnp.zeros((LAT, PACK), f32)
    after = jnp.concatenate([g[:, :PACK] for g in groups[1:]] + [blank], axis=0)
    before = jnp.concatenate([blank] + [g[:, GROUP - PACK :] for g in groups[:-1]], axis=0)
    edge = jnp.where(low_lanes(after.shape), after, before)
    window = jnp.concatenate([field, edge], axis=1)
    rows = window.shape[0]
    row = lax.broadcasted_iota(jnp.int32, window.shape, 0) % LAT
    shifted = [
        jnp.where(row == 0, 0.0, pltpu.roll(window, 1, 0)),
        window,
        jnp.where(row == LAT - 1, 0.0, pltpu.roll(window, rows - 1, 0)),
    ]
    for b in range(3):
        start = (3 * a + b) * WINDOW
        lhs_ref[:, start : start + WINDOW] = shifted[b].astype(bf16)


def conv_one_kernel(before_ref, own_ref, after_ref, w_ref, *refs):
    moved_ref, slope_ref, lhs_ref, hid_ref = refs[-4:]
    for a, ref in enumerate((before_ref, own_ref, after_ref)):
        write_windows(lhs_ref, a, [ref[:, g * GROUP : (g + 1) * GROUP].astype(f32) for g in range(LS)])
    pre = jnp.dot(lhs_ref[...], w_ref[...], preferred_element_type=f32)
    tanh_val = jnp.tanh(root_coef * (pre + cubic_coef * pre * pre * pre))
    hidden = 0.5 * pre * (1.0 + tanh_val)
    slope_ref[...] = 0.5 * (1.0 + tanh_val) + 0.5 * pre * (1.0 - tanh_val * tanh_val) * root_coef * (
        1.0 + 3.0 * cubic_coef * pre * pre
    )
    for u in range(BLOCK // 2):
        hid_ref[u] = hidden[:, u * PACK : (u + 1) * PACK]
    for r in range(BLOCK):
        for u in range(BLOCK // 2):
            cells = jnp.concatenate(
                [hid_ref[u, pl.ds(BLOCK * i + r, LS, stride=LAT), :] for i in range(LS)], axis=0
            )
            top, bottom = cells[: CELLS // 2], cells[CELLS // 2 :]
            low = low_lanes(top.shape)
            piece = r * BLOCK + 2 * u
            moved_ref[piece] = jnp.where(low, top, pltpu.roll(bottom, C1, 1)).astype(bf16)
            moved_ref[piece + 1] = jnp.where(low, pltpu.roll(top, C1, 1), bottom).astype(bf16)


def conv_one(before, own, after, band, waits):
    rows = LS * LAT
    whole = pl.BlockSpec(memory_space=pltpu.VMEM)
    return pl.pallas_call(
        conv_one_kernel,
        in_specs=[whole] * 4 + [pl.BlockSpec(memory_space=pl.ANY)] * len(waits),
        out_shape=(
            jax.ShapeDtypeStruct((BLOCK * BLOCK, CELLS // 2, PACK), bf16),
            jax.ShapeDtypeStruct((rows, GROUP), f32),
            jax.ShapeDtypeStruct((rows, 9 * WINDOW), bf16),
        ),
        scratch_shapes=[pltpu.VMEM((BLOCK // 2, rows, PACK), f32)],
        compiler_params=params(24),
        cost_estimate=pl.CostEstimate(
            flops=2 * rows * 9 * WINDOW * GROUP, bytes_accessed=5 << 20, transcendentals=rows * GROUP
        ),
    )(before, own, after, band, *waits)


def shift_cells(field, step):
    if step == 0:
        return field
    column = lax.broadcasted_iota(jnp.int32, field.shape, 1)
    edge = LS - 1 if step > 0 else 0
    return jnp.where(column == edge, 0.0, pltpu.roll(field, (-step) % LS, 1))


def conv_two_kernel(planes, x_ref, w_ref, *refs):
    out_ref, lhs_ref, v_ref = refs[-3:]

    @pl.when(pl.program_id(0) == 0)
    def _():
        v_ref[:, :, 0] = jnp.zeros((3, 2, LS + 2, LS, PACK), f32)
        v_ref[:, :, planes + 1] = jnp.zeros((3, 2, LS + 2, LS, PACK), f32)
        edge = jnp.zeros((LS, PACK), f32)

        def spread(p, carry):
            x = x_ref[p].astype(f32)
            turned = pltpu.roll(x, C1, 1)
            for half, parts in enumerate(((x, turned), (turned, x))):
                cells = jnp.concatenate(parts, axis=0).reshape(LS, LS, PACK)
                for c in range(3):
                    v_ref[c, half, p + 1, 0] = edge
                    v_ref[c, half, p + 1, 1 : LS + 1] = shift_cells(cells, c - 1)
                    v_ref[c, half, p + 1, LS + 1] = edge
            return carry

        lax.fori_loop(0, planes, spread, 0)

        def gather(p, carry):
            rows = pl.ds(pl.multiple_of(p * CELLS, CELLS), CELLS)
            for m in range((TAPS + 1) // 2):
                t = 2 * m
                low = v_ref[t % 3, 0, p + t // 9, pl.ds((t // 3) % 3, LS)].reshape(CELLS, PACK)
                t = 2 * m + 1
                if t < TAPS:
                    high = v_ref[t % 3, 1, p + t // 9, pl.ds((t // 3) % 3, LS)].reshape(CELLS, PACK)
                    tile = jnp.where(low_lanes(low.shape), low, high)
                    lhs_ref[rows, m * PACK : (m + 1) * PACK] = tile.astype(bf16)
                else:
                    lhs_ref[rows, m * PACK : m * PACK + C1] = low[:, :C1].astype(bf16)
            return carry

        lax.fori_loop(0, planes, gather, 0)

    chunk = 4 * CELLS
    for m in range(planes * CELLS // chunk):
        rows = slice(m * chunk, (m + 1) * chunk)
        out_ref[rows] = jnp.dot(lhs_ref[rows], w_ref[...], preferred_element_type=f32).astype(bf16)


def conv_two(pieces, weight, after):
    planes = pieces.shape[0]
    cells = planes * CELLS
    block = 256
    return pl.pallas_call(
        lambda *refs: conv_two_kernel(planes, *refs),
        grid=(C2 // block,),
        in_specs=[
            pl.BlockSpec(pieces.shape, lambda n: (0, 0, 0)),
            pl.BlockSpec((TAPS * C1, block), lambda n: (0, n)),
        ]
        + [pl.BlockSpec(memory_space=pl.ANY)] * len(after),
        out_specs=pl.BlockSpec((cells, block), lambda n: (0, n)),
        out_shape=jax.ShapeDtypeStruct((cells, C2), bf16),
        scratch_shapes=[
            pltpu.VMEM((cells, TAPS * C1), bf16),
            pltpu.VMEM((3, 2, planes + 2, LS + 2, LS, PACK), f32),
        ],
        compiler_params=params(56),
        cost_estimate=pl.CostEstimate(
            flops=2 * cells * TAPS * C1 * C2, bytes_accessed=10 << 20, transcendentals=0
        ),
    )(pieces, weight, *after)


def join_kernel(count, *refs):
    out_ref, first = refs[-1], 0
    for ref in refs[:count]:
        rows = ref.shape[0]
        out_ref[first : first + rows] = ref[...]
        first += rows


def joined(values, after=()):
    rows = sum(value.shape[0] for value in values)
    columns = values[0].shape[1]
    return pl.pallas_call(
        lambda *refs: join_kernel(len(values), *refs),
        grid=(1,),
        in_specs=[pl.BlockSpec(value.shape, lambda n: (0, 0)) for value in values]
        + [pl.BlockSpec(memory_space=pl.ANY)] * len(after),
        out_specs=pl.BlockSpec((rows, columns), lambda n: (0, 0)),
        out_shape=jax.ShapeDtypeStruct((rows, columns), values[0].dtype),
        compiler_params=params(32),
        cost_estimate=pl.CostEstimate(flops=0, bytes_accessed=4 * rows * columns, transcendentals=0),
    )(*values, *after)


def plane_copies(device, pieces, refs, target_ref, base, sems):
    copies = []
    for differences, ref in zip(pieces, refs):
        for k, difference in enumerate(differences):
            row = pl.multiple_of(base + (device ^ difference) * CELLS, CELLS)
            source = ref.at[pl.ds(k * CELLS, CELLS), :]
            target = target_ref.at[pl.ds(row, CELLS), :]
            copies.append(pltpu.make_async_copy(source, target, sems.at[len(copies)]))
    return copies


def back_two_kernel(planes, pieces, device_ref, *refs):
    cot_refs = refs[: len(pieces)]
    w_ref, out_ref, cot_ref, sum_ref, sems = refs[len(pieces)], *refs[-4:]
    b = pl.program_id(0)
    cells = planes * CELLS

    @pl.when(b == 0)
    def _():
        copies = plane_copies(device_ref[0], pieces, cot_refs, cot_ref, CELLS, sems)
        for copy in copies:
            copy.start()
        cot_ref[:CELLS] = jnp.zeros((CELLS, C2), bf16)
        cot_ref[cells + CELLS :] = jnp.zeros((CELLS, C2), bf16)
        sum_ref[...] = jnp.zeros(sum_ref.shape, f32)
        for copy in copies:
            copy.wait()

    total = None
    for a in range(3):
        term = lax.dot_general(
            cot_ref[(2 - a) * CELLS : (2 - a) * CELLS + cells],
            w_ref[a],
            (((1,), (1,)), ((), ())),
            preferred_element_type=f32,
        )
        total = term if total is None else total + term
    rows = pl.ds(b, LS)
    first = total[:, :PACK].reshape(planes, LS, LS, PACK)
    sum_ref[0, :, rows] = sum_ref[0, :, rows] + first
    last = jnp.concatenate([total[:, PACK:], jnp.zeros((cells, C1), f32)], axis=1)
    sum_ref[1, :, rows] = sum_ref[1, :, rows] + last.reshape(planes, LS, LS, PACK)

    @pl.when(b == 2)
    def _():
        def finish(p, carry):
            pair = sum_ref[0, p, 1 : LS + 1]
            single = sum_ref[1, p, 1 : LS + 1]
            total = shift_cells(pair, 1) + shift_cells(single, -1)
            total = total.reshape(CELLS, PACK) + pltpu.roll(pair.reshape(CELLS, PACK), C1, 1)
            top, bottom = total[: CELLS // 2], total[CELLS // 2 :]
            out_ref[p] = jnp.where(low_lanes(top.shape), top, pltpu.roll(bottom, C1, 1)).astype(bf16)
            return carry

        lax.fori_loop(0, planes, finish, 0)


def back_two(device, pieces, cots, weight, after):
    planes = sum(len(piece) for piece in pieces)
    return pl.pallas_call(
        lambda *refs: back_two_kernel(planes, pieces, *refs),
        grid_spec=pltpu.PrefetchScalarGridSpec(
            num_scalar_prefetch=1,
            grid=(3,),
            in_specs=[pl.BlockSpec(memory_space=pl.ANY)] * len(cots)
            + [pl.BlockSpec((3, 3 * C1, C2), lambda n, s: (0, n, 0))]
            + [pl.BlockSpec(memory_space=pl.ANY)] * len(after),
            out_specs=pl.BlockSpec((planes, CELLS // 2, PACK), lambda n, s: (0, 0, 0)),
            scratch_shapes=[
                pltpu.VMEM(((planes + 2) * CELLS, C2), bf16),
                pltpu.VMEM((2, planes, LS + 2, LS, PACK), f32),
                pltpu.SemaphoreType.DMA((planes,)),
            ],
        ),
        out_shape=jax.ShapeDtypeStruct((planes, CELLS // 2, PACK), bf16),
        compiler_params=params(56),
        cost_estimate=pl.CostEstimate(
            flops=2 * planes * CELLS * TAPS * C1 * C2, bytes_accessed=6 << 20, transcendentals=0
        ),
    )(device, *cots, weight.reshape(3, 9 * C1, C2), *after)


def weight_two_kernel(planes, pieces, scale, device_ref, *refs):
    samples = len(pieces)
    field_refs, cot_refs = refs[:samples], refs[samples:]
    out_ref, token_ref, cot_ref, flat_ref, lhs_ref, sems = refs[-6:]
    cells = planes * CELLS
    a = pl.program_id(0)

    @pl.when(a == 0)
    def _():
        copies, first = [], 0
        for s in range(samples):
            refs_here = cot_refs[first : first + len(pieces[s])]
            copies += plane_copies(device_ref[0], pieces[s], refs_here, cot_ref.at[s], CELLS, sems.at[s])
            first += len(pieces[s])
        for copy in copies:
            copy.start()
        for s in range(samples):
            cot_ref[s, :CELLS] = jnp.zeros((CELLS, C2), bf16)
            cot_ref[s, cells + CELLS :] = jnp.zeros((CELLS, C2), bf16)

            def cells_of(p):
                x = field_refs[s][p].astype(f32)
                return jnp.concatenate([x, pltpu.roll(x, C1, 1)], axis=0)

            for j in range(planes // 2):
                pair = jnp.concatenate([cells_of(2 * j), cells_of(2 * j + 1)], axis=0)
                flat_ref[s, :, j * PACK : (j + 1) * PACK] = pair.T[:C1]

        lane = lax.broadcasted_iota(jnp.int32, (1, cells), 1)
        row, column = (lane // LS) % LS, lane % LS
        for b in range(3):
            for c in range(3):
                inside = (row + b >= 1) & (row + b <= LS) & (column + c >= 1) & (column + c <= LS)
                mask = inside.astype(f32)
                shift = (-(LS * (b - 1) + c - 1)) % cells
                t = 3 * b + c
                for s in range(samples):
                    value = flat_ref[s]
                    if shift:
                        value = pltpu.roll(value, shift, 1) * mask
                    lhs_ref[s, t * C1 : (t + 1) * C1] = value.astype(bf16)
        for copy in copies:
            copy.wait()

    rows = pl.ds(pl.multiple_of((2 - a) * CELLS, CELLS), cells)
    total = None
    for s in range(samples):
        term = jnp.dot(lhs_ref[s], cot_ref[s, rows], preferred_element_type=f32)
        total = term if total is None else total + term
    out_ref[...] = total * scale
    token_ref[...] = jnp.zeros(token_ref.shape, f32)


def weight_two(device, fields, pieces, cots, scale, after):
    samples = len(fields)
    planes = fields[0].shape[0]
    cells = planes * CELLS
    block = 9 * C1
    flat = [value for sample in cots for value in sample]
    return pl.pallas_call(
        lambda *refs: weight_two_kernel(planes, pieces, scale, *refs),
        grid_spec=pltpu.PrefetchScalarGridSpec(
            num_scalar_prefetch=1,
            grid=(3,),
            in_specs=[pl.BlockSpec(field.shape, lambda n, s: (0, 0, 0)) for field in fields]
            + [pl.BlockSpec(memory_space=pl.ANY)] * (len(flat) + len(after)),
            out_specs=(
                pl.BlockSpec((block, C2), lambda n, s: (n, 0)),
                pl.BlockSpec((8, PACK), lambda n, s: (0, 0)),
            ),
            scratch_shapes=[
                pltpu.VMEM((samples, (planes + 2) * CELLS, C2), bf16),
                pltpu.VMEM((samples, C1, cells), f32),
                pltpu.VMEM((samples, block, cells), bf16),
                pltpu.SemaphoreType.DMA((samples, planes)),
            ],
        ),
        out_shape=(
            jax.ShapeDtypeStruct((TAPS * C1, C2), f32),
            jax.ShapeDtypeStruct((8, PACK), f32),
        ),
        compiler_params=params(60),
        cost_estimate=pl.CostEstimate(
            flops=2 * samples * cells * TAPS * C1 * C2, bytes_accessed=18 << 20, transcendentals=0
        ),
    )(device, *fields, *flat, *after)


def grad_pre_kernel(pieces_ref, slope_ref, lhs_ref, *refs):
    grad_ref, partial_ref, spread_ref, packed_ref = refs[-4:]
    for r in range(BLOCK):
        for u in range(BLOCK // 2):
            piece = r * BLOCK + 2 * u
            first = pieces_ref[piece].astype(f32)
            second = pieces_ref[piece + 1].astype(f32)
            low = low_lanes(first.shape)
            top = jnp.where(low, first, pltpu.roll(second, C1, 1))
            bottom = jnp.where(low, pltpu.roll(first, C1, 1), second)
            for i in range(LS):
                source = top if i < LS // 2 else bottom
                start = (i % (LS // 2)) * LS
                spread_ref[u, pl.ds(BLOCK * i + r, LS, stride=LAT), :] = source[start : start + LS]
    grads = []
    for u in range(BLOCK // 2):
        lanes = slice(u * PACK, (u + 1) * PACK)
        value = (spread_ref[u] * slope_ref[:, lanes]).astype(bf16)
        grad_ref[:, lanes] = value
        grads.append(value)
    grad = jnp.concatenate(grads, axis=1)
    for lateral in range(9):
        window = lhs_ref[:, lateral * WINDOW : (lateral + 1) * WINDOW]
        product = lax.dot_general(window, grad, (((0,), (0,)), ((), ())), preferred_element_type=f32)
        for c in range(3):
            sums = []
            for parity in range(2):
                part = None
                for pair in range(BLOCK // 2):
                    column = 2 * pair + parity + c - 1
                    slot = column if column >= 0 else BLOCK + 1
                    term = product[slot * C1 : (slot + 1) * C1, pair * PACK : (pair + 1) * PACK]
                    part = term if part is None else part + term
                sums.append(part)
            total = sums[0] + pltpu.roll(sums[1], C1, 1)
            top, bottom = total[: C1 // 2], total[C1 // 2 :]
            t = 3 * lateral + c
            packed_ref[t * (C1 // 2) : (t + 1) * (C1 // 2)] = jnp.where(
                low_lanes(top.shape), top, pltpu.roll(bottom, C1, 1)
            )
    packed_ref[TAPS * (C1 // 2) :] = jnp.zeros(((32 - TAPS) * (C1 // 2), PACK), f32)
    for row in range(C1 // 2):
        entry = packed_ref[pl.ds(row, 32, stride=C1 // 2), :]
        partial_ref[row] = entry.astype(bf16)


def grad_pre_of(pieces, slope, lhs, after):
    rows = LS * LAT
    whole = pl.BlockSpec(memory_space=pltpu.VMEM)
    return pl.pallas_call(
        grad_pre_kernel,
        in_specs=[whole] * 3 + [pl.BlockSpec(memory_space=pl.ANY)] * len(after),
        out_shape=(
            jax.ShapeDtypeStruct((rows, GROUP), bf16),
            jax.ShapeDtypeStruct((C1 // 2, 32, PACK), bf16),
        ),
        scratch_shapes=[
            pltpu.VMEM((BLOCK // 2, rows, PACK), f32),
            pltpu.VMEM((32 * (C1 // 2), PACK), f32),
        ],
        compiler_params=params(24),
        cost_estimate=pl.CostEstimate(
            flops=2 * rows * 9 * WINDOW * GROUP, bytes_accessed=3 << 20, transcendentals=0
        ),
    )(pieces, slope, lhs, *after)


def back_one_kernel(before_ref, own_ref, after_ref, w_ref, out_ref, lhs_ref):
    for a, ref in enumerate((before_ref, own_ref, after_ref)):
        write_windows(lhs_ref, a, [ref[g * LAT : (g + 1) * LAT].astype(f32) for g in range(LS)])
    result = jnp.dot(lhs_ref[...], w_ref[...], preferred_element_type=f32)
    for g in range(LS):
        out_ref[:, g * GROUP : (g + 1) * GROUP] = result[g * LAT : (g + 1) * LAT].astype(bf16)


def back_one(before, own, after, band):
    rows = LS * LAT
    return pl.pallas_call(
        back_one_kernel,
        out_shape=jax.ShapeDtypeStruct((LAT, LAT * C1), bf16),
        scratch_shapes=[pltpu.VMEM((rows, 9 * WINDOW), bf16)],
        compiler_params=params(24),
        cost_estimate=pl.CostEstimate(
            flops=2 * rows * 9 * WINDOW * GROUP, bytes_accessed=3 << 20, transcendentals=0
        ),
    )(before, own, after, band)


def sum_kernel(scale, shares_ref, *refs):
    out_ref = refs[-1]
    total = jnp.sum(shares_ref[...].astype(f32), axis=0) * scale
    out_ref[...] = jnp.broadcast_to(total.astype(bf16)[None], out_ref.shape)


def sum_shares(shares, scale, after):
    whole = pl.BlockSpec(memory_space=pltpu.VMEM)
    return pl.pallas_call(
        lambda *refs: sum_kernel(scale, *refs),
        in_specs=[whole] + [pl.BlockSpec(memory_space=pl.ANY)] * len(after),
        out_shape=jax.ShapeDtypeStruct(shares.shape, bf16),
        compiler_params=params(16),
        cost_estimate=pl.CostEstimate(flops=0, bytes_accessed=1 << 20, transcendentals=0),
    )(shares, *after)


def unpack_kernel(packed_ref, *refs):
    out_ref, wide_ref = refs[-2:]
    wide_ref[...] = packed_ref[...].astype(f32).reshape(wide_ref.shape)
    for t in range(TAPS):
        entry = wide_ref[pl.ds(t, C1 // 2, stride=32), :]
        out_ref[t] = jnp.concatenate([entry[:, :C1], entry[:, C1:]], axis=0)


def unpack(packed, after):
    whole = pl.BlockSpec(memory_space=pltpu.VMEM)
    return pl.pallas_call(
        unpack_kernel,
        in_specs=[whole] + [pl.BlockSpec(memory_space=pl.ANY)] * len(after),
        out_shape=jax.ShapeDtypeStruct((TAPS, C1, C1), f32),
        scratch_shapes=[pltpu.VMEM((32 * (C1 // 2), PACK), f32)],
        compiler_params=params(16),
        cost_estimate=pl.CostEstimate(flops=0, bytes_accessed=1 << 20, transcendentals=0),
    )(packed, *after)


def neighbours(value, axis):
    count = lax.axis_size(axis)
    before = lax.ppermute(value, axis, [(i, i + 1) for i in range(count - 1)])
    after = lax.ppermute(value, axis, [(i + 1, i) for i in range(count - 1)])
    return before, after


def flipped(value, difference):
    count = lax.axis_size("depth")
    return lax.ppermute(value, "depth", [(i, i ^ difference) for i in range(count)])


def over_samples(value):
    count = lax.axis_size("sample")
    return [value] + [
        lax.ppermute(value, "sample", [(i, (i + shift) % count) for i in range(count)])
        for shift in range(1, count)
    ]


def on_device(volume, conv1_weight, conv2_weight, cotangent):
    samples = lax.axis_size("sample")
    shards = lax.axis_size("depth")
    flat_two = conv2_weight.reshape(TAPS * C1, C2)
    own = volume.reshape(LAT, LAT * C1)
    device = lax.axis_index("depth").astype(jnp.int32).reshape(1)
    cot = cotangent.reshape(CELLS, C2)

    core, chip = 1, 2
    outer = list(range(4, shards, 4))
    far = [flipped(cot, difference) for difference in outer]
    before, after = neighbours(own, "depth")
    cot_chip = flipped(cot, chip)

    back_weight = jnp.swapaxes(conv1_weight[::-1], 1, 2)
    band = banded(conv1_weight)
    back_band = banded(back_weight)

    moved, slope, windows = conv_one(before, own, after, band, [])
    fields = lax.all_to_all(moved, "depth", split_axis=0, concat_axis=0, tiled=True)

    near = joined([cot, cot_chip], [fields])
    far = joined(far, [slope])
    far_chip = flipped(far, chip)
    cots = [near, far, far_chip]
    pieces = [[0, chip], outer, [difference + chip for difference in outer]]
    pieces = pieces + [[difference + core for difference in piece] for piece in pieces]

    near_core, far_core = flipped(near, core), flipped(far, core)
    partial = conv_two(fields, flat_two, [near_core, far_core])
    features = lax.psum_scatter(partial, "depth", scatter_dimension=0, tiled=True)

    own_cots = cots + [near_core, far_core, flipped(far_chip, core)]
    grad_pieces = back_two(device, pieces, own_cots, flat_two, [partial])
    returned = lax.all_to_all(grad_pieces, "depth", split_axis=0, concat_axis=0, tiled=True)
    half = joined(cots, [partial])
    halves = [[difference for piece in group for difference in piece] for group in (pieces[:3], pieces[3:])]
    all_pieces, all_cots = [pieces], [own_cots]
    for value in over_samples(half)[1:]:
        value = joined([value], [returned])
        all_pieces.append(halves)
        all_cots.append([value, flipped(value, core)])
    all_fields = over_samples(fields)

    grad_pre, partial_one = grad_pre_of(returned, slope, windows, [])
    grad_before, grad_after = neighbours(grad_pre, "depth")

    devices = samples * shards
    both = ("sample", "depth")
    scale_one = 1.0 / math.sqrt(samples * shards * LAT * LAT)
    shares = partial_one.reshape(devices, -1, PACK)
    shares = lax.all_to_all(shares, both, split_axis=0, concat_axis=0, tiled=True)
    scale_two = 1.0 / math.sqrt(samples * shards * CELLS)
    grad_conv2, token = weight_two(
        device, all_fields, all_pieces, all_cots, scale_two, [grad_pre]
    )
    summed = sum_shares(shares, scale_one, [token])
    shares = lax.all_to_all(summed, both, split_axis=0, concat_axis=0, tiled=True)
    grad_volume = back_one(grad_before, grad_pre, grad_after, back_band)
    grad_conv1 = unpack(shares.reshape(C1 // 2, 32, PACK), [])

    return (
        features.reshape(cotangent.shape),
        grad_volume.reshape(volume.shape),
        grad_conv1,
        grad_conv2.reshape(conv2_weight.shape),
    )


def solution(mesh):
    return jax.shard_map(
        on_device,
        mesh=mesh,
        in_specs=(
            P("sample", "depth", None, None),
            P(),
            P(None, "depth", None),
            P("sample", "depth", None, None, None),
        ),
        out_specs=(
            P("sample", "depth", None, None, None),
            P("sample", "depth", None, None),
            P(),
            P(None, "depth", None),
        ),
        check_vma=False,
    )
```

```python
import math

import jax
import jax.numpy as jnp
from jax import lax
from jax.experimental import pallas as pl
from jax.experimental.pallas import tpu as pltpu
from jax.sharding import PartitionSpec as P

C1 = 64
LAT = 32
BLOCK = 4
C2 = 1024
LS = 8
CELLS = LS * LS
GROUP = BLOCK * C1
WINDOW = GROUP + 2 * C1
TAPS = 27
PACK = 2 * C1

root_coef = 0.7978845608028654
cubic_coef = 0.044715

f32 = jnp.float32
bf16 = jnp.bfloat16


def params(mebibytes):
    return pltpu.CompilerParams(vmem_limit_bytes=mebibytes * 1024 * 1024)


def low_lanes(shape):
    return lax.broadcasted_iota(jnp.int32, shape, len(shape) - 1) < C1


def band_kernel(w_ref, out_ref):
    for lateral in range(9):
        for slot in range(BLOCK + 2):
            column = slot if slot <= BLOCK else -1
            for pair in range(BLOCK // 2):
                halves = []
                for own in (2 * pair, 2 * pair + 1):
                    c = column - own + 1
                    if 0 <= c <= 2:
                        halves.append(w_ref[3 * lateral + c])
                    else:
                        halves.append(jnp.zeros((C1, C1), bf16))
                start = lateral * WINDOW + slot * C1
                out_ref[start : start + C1, pair * PACK : (pair + 1) * PACK] = jnp.concatenate(halves, axis=1)


def banded(weight):
    return pl.pallas_call(
        band_kernel,
        out_shape=jax.ShapeDtypeStruct((9 * WINDOW, GROUP), bf16),
        compiler_params=params(16),
        cost_estimate=pl.CostEstimate(flops=0, bytes_accessed=4 << 20, transcendentals=0),
    )(weight)


def write_windows(lhs_ref, a, groups):
    field = jnp.concatenate(groups, axis=0)
    blank = jnp.zeros((LAT, PACK), f32)
    after = jnp.concatenate([g[:, :PACK] for g in groups[1:]] + [blank], axis=0)
    before = jnp.concatenate([blank] + [g[:, GROUP - PACK :] for g in groups[:-1]], axis=0)
    edge = jnp.where(low_lanes(after.shape), after, before)
    window = jnp.concatenate([field, edge], axis=1)
    rows = window.shape[0]
    row = lax.broadcasted_iota(jnp.int32, window.shape, 0) % LAT
    shifted = [
        jnp.where(row == 0, 0.0, pltpu.roll(window, 1, 0)),
        window,
        jnp.where(row == LAT - 1, 0.0, pltpu.roll(window, rows - 1, 0)),
    ]
    for b in range(3):
        start = (3 * a + b) * WINDOW
        lhs_ref[:, start : start + WINDOW] = shifted[b].astype(bf16)


def conv_one_kernel(before_ref, own_ref, after_ref, w_ref, *refs):
    moved_ref, slope_ref, lhs_ref, hid_ref = refs[-4:]
    for a, ref in enumerate((before_ref, own_ref, after_ref)):
        write_windows(lhs_ref, a, [ref[:, g * GROUP : (g + 1) * GROUP].astype(f32) for g in range(LS)])
    pre = jnp.dot(lhs_ref[...], w_ref[...], preferred_element_type=f32)
    tanh_val = jnp.tanh(root_coef * (pre + cubic_coef * pre * pre * pre))
    hidden = 0.5 * pre * (1.0 + tanh_val)
    slope_ref[...] = 0.5 * (1.0 + tanh_val) + 0.5 * pre * (1.0 - tanh_val * tanh_val) * root_coef * (
        1.0 + 3.0 * cubic_coef * pre * pre
    )
    for u in range(BLOCK // 2):
        hid_ref[u] = hidden[:, u * PACK : (u + 1) * PACK]
    for r in range(BLOCK):
        for u in range(BLOCK // 2):
            cells = jnp.concatenate(
                [hid_ref[u, pl.ds(BLOCK * i + r, LS, stride=LAT), :] for i in range(LS)], axis=0
            )
            top, bottom = cells[: CELLS // 2], cells[CELLS // 2 :]
            low = low_lanes(top.shape)
            piece = r * BLOCK + 2 * u
            moved_ref[piece] = jnp.where(low, top, pltpu.roll(bottom, C1, 1)).astype(bf16)
            moved_ref[piece + 1] = jnp.where(low, pltpu.roll(top, C1, 1), bottom).astype(bf16)


def conv_one(before, own, after, band, waits):
    rows = LS * LAT
    whole = pl.BlockSpec(memory_space=pltpu.VMEM)
    return pl.pallas_call(
        conv_one_kernel,
        in_specs=[whole] * 4 + [pl.BlockSpec(memory_space=pl.ANY)] * len(waits),
        out_shape=(
            jax.ShapeDtypeStruct((BLOCK * BLOCK, CELLS // 2, PACK), bf16),
            jax.ShapeDtypeStruct((rows, GROUP), f32),
            jax.ShapeDtypeStruct((rows, 9 * WINDOW), bf16),
        ),
        scratch_shapes=[pltpu.VMEM((BLOCK // 2, rows, PACK), f32)],
        compiler_params=params(24),
        cost_estimate=pl.CostEstimate(
            flops=2 * rows * 9 * WINDOW * GROUP, bytes_accessed=5 << 20, transcendentals=rows * GROUP
        ),
    )(before, own, after, band, *waits)


def shift_cells(field, step):
    if step == 0:
        return field
    column = lax.broadcasted_iota(jnp.int32, field.shape, 1)
    edge = LS - 1 if step > 0 else 0
    return jnp.where(column == edge, 0.0, pltpu.roll(field, (-step) % LS, 1))


def conv_two_kernel(planes, x_ref, w_ref, *refs):
    out_ref, token_ref, lhs_ref, v_ref = refs[-4:]
    token_ref[...] = jnp.zeros(token_ref.shape, f32)

    @pl.when(pl.program_id(0) == 0)
    def _():
        v_ref[:, :, 0] = jnp.zeros((3, 2, LS + 2, LS, PACK), f32)
        v_ref[:, :, planes + 1] = jnp.zeros((3, 2, LS + 2, LS, PACK), f32)
        edge = jnp.zeros((LS, PACK), f32)

        def spread(p, carry):
            x = x_ref[p].astype(f32)
            turned = pltpu.roll(x, C1, 1)
            for half, parts in enumerate(((x, turned), (turned, x))):
                cells = jnp.concatenate(parts, axis=0).reshape(LS, LS, PACK)
                for c in range(3):
                    v_ref[c, half, p + 1, 0] = edge
                    v_ref[c, half, p + 1, 1 : LS + 1] = shift_cells(cells, c - 1)
                    v_ref[c, half, p + 1, LS + 1] = edge
            return carry

        lax.fori_loop(0, planes, spread, 0)

        def gather(p, carry):
            rows = pl.ds(pl.multiple_of(p * CELLS, CELLS), CELLS)
            for m in range((TAPS + 1) // 2):
                t = 2 * m
                low = v_ref[t % 3, 0, p + t // 9, pl.ds((t // 3) % 3, LS)].reshape(CELLS, PACK)
                t = 2 * m + 1
                if t < TAPS:
                    high = v_ref[t % 3, 1, p + t // 9, pl.ds((t // 3) % 3, LS)].reshape(CELLS, PACK)
                    tile = jnp.where(low_lanes(low.shape), low, high)
                    lhs_ref[rows, m * PACK : (m + 1) * PACK] = tile.astype(bf16)
                else:
                    lhs_ref[rows, m * PACK : m * PACK + C1] = low[:, :C1].astype(bf16)
            return carry

        lax.fori_loop(0, planes, gather, 0)

    chunk = 4 * CELLS
    for m in range(planes * CELLS // chunk):
        rows = slice(m * chunk, (m + 1) * chunk)
        out_ref[rows] = jnp.dot(lhs_ref[rows], w_ref[...], preferred_element_type=f32).astype(bf16)


def conv_two(pieces, weight, after):
    planes = pieces.shape[0]
    cells = planes * CELLS
    block = 256
    return pl.pallas_call(
        lambda *refs: conv_two_kernel(planes, *refs),
        grid=(C2 // block,),
        in_specs=[
            pl.BlockSpec(pieces.shape, lambda n: (0, 0, 0)),
            pl.BlockSpec((TAPS * C1, block), lambda n: (0, n)),
        ]
        + [pl.BlockSpec(memory_space=pl.ANY)] * len(after),
        out_specs=(
            pl.BlockSpec((cells, block), lambda n: (0, n)),
            pl.BlockSpec((8, PACK), lambda n: (0, 0)),
        ),
        out_shape=(jax.ShapeDtypeStruct((cells, C2), bf16), jax.ShapeDtypeStruct((8, PACK), f32)),
        scratch_shapes=[
            pltpu.VMEM((cells, TAPS * C1), bf16),
            pltpu.VMEM((3, 2, planes + 2, LS + 2, LS, PACK), f32),
        ],
        compiler_params=params(56),
        cost_estimate=pl.CostEstimate(
            flops=2 * cells * TAPS * C1 * C2, bytes_accessed=10 << 20, transcendentals=0
        ),
    )(pieces, weight, *after)


def join_kernel(count, *refs):
    out_ref, first = refs[-1], 0
    for ref in refs[:count]:
        rows = ref.shape[0]
        out_ref[first : first + rows] = ref[...]
        first += rows


def joined(values, after=()):
    rows = sum(value.shape[0] for value in values)
    columns = values[0].shape[1]
    return pl.pallas_call(
        lambda *refs: join_kernel(len(values), *refs),
        grid=(1,),
        in_specs=[pl.BlockSpec(value.shape, lambda n: (0, 0)) for value in values]
        + [pl.BlockSpec(memory_space=pl.ANY)] * len(after),
        out_specs=pl.BlockSpec((rows, columns), lambda n: (0, 0)),
        out_shape=jax.ShapeDtypeStruct((rows, columns), values[0].dtype),
        compiler_params=params(32),
        cost_estimate=pl.CostEstimate(flops=0, bytes_accessed=4 * rows * columns, transcendentals=0),
    )(*values, *after)


def held_kernel(*refs):
    pass


def held(value, after):
    return pl.pallas_call(
        held_kernel,
        in_specs=[pl.BlockSpec(memory_space=pl.ANY)] * (1 + len(after)),
        out_specs=pl.BlockSpec(memory_space=pl.ANY),
        out_shape=jax.ShapeDtypeStruct(value.shape, value.dtype),
        input_output_aliases={0: 0},
        compiler_params=params(16),
    )(value, *after)


def plane_copies(device, pieces, refs, target_ref, base, sems):
    copies = []
    for differences, ref in zip(pieces, refs):
        for k, difference in enumerate(differences):
            row = pl.multiple_of(base + (device ^ difference) * CELLS, CELLS)
            source = ref.at[pl.ds(k * CELLS, CELLS), :]
            target = target_ref.at[pl.ds(row, CELLS), :]
            copies.append(pltpu.make_async_copy(source, target, sems.at[len(copies)]))
    return copies


def back_two_kernel(planes, pieces, device_ref, *refs):
    cot_refs = refs[: len(pieces)]
    w_ref, out_ref, cot_ref, sum_ref, sems = refs[len(pieces)], *refs[-4:]
    b = pl.program_id(0)
    cells = planes * CELLS

    @pl.when(b == 0)
    def _():
        copies = plane_copies(device_ref[0], pieces, cot_refs, cot_ref, CELLS, sems)
        for copy in copies:
            copy.start()
        cot_ref[:CELLS] = jnp.zeros((CELLS, C2), bf16)
        cot_ref[cells + CELLS :] = jnp.zeros((CELLS, C2), bf16)
        sum_ref[...] = jnp.zeros(sum_ref.shape, f32)
        for copy in copies:
            copy.wait()

    total = None
    for a in range(3):
        term = lax.dot_general(
            cot_ref[(2 - a) * CELLS : (2 - a) * CELLS + cells],
            w_ref[a],
            (((1,), (1,)), ((), ())),
            preferred_element_type=f32,
        )
        total = term if total is None else total + term
    rows = pl.ds(b, LS)
    first = total[:, :PACK].reshape(planes, LS, LS, PACK)
    sum_ref[0, :, rows] = sum_ref[0, :, rows] + first
    last = jnp.concatenate([total[:, PACK:], jnp.zeros((cells, C1), f32)], axis=1)
    sum_ref[1, :, rows] = sum_ref[1, :, rows] + last.reshape(planes, LS, LS, PACK)

    @pl.when(b == 2)
    def _():
        def finish(p, carry):
            pair = sum_ref[0, p, 1 : LS + 1]
            single = sum_ref[1, p, 1 : LS + 1]
            total = shift_cells(pair, 1) + shift_cells(single, -1)
            total = total.reshape(CELLS, PACK) + pltpu.roll(pair.reshape(CELLS, PACK), C1, 1)
            top, bottom = total[: CELLS // 2], total[CELLS // 2 :]
            out_ref[p] = jnp.where(low_lanes(top.shape), top, pltpu.roll(bottom, C1, 1)).astype(bf16)
            return carry

        lax.fori_loop(0, planes, finish, 0)


def back_two(device, pieces, cots, weight, after):
    planes = sum(len(piece) for piece in pieces)
    return pl.pallas_call(
        lambda *refs: back_two_kernel(planes, pieces, *refs),
        grid_spec=pltpu.PrefetchScalarGridSpec(
            num_scalar_prefetch=1,
            grid=(3,),
            in_specs=[pl.BlockSpec(memory_space=pl.ANY)] * len(cots)
            + [pl.BlockSpec((3, 3 * C1, C2), lambda n, s: (0, n, 0))]
            + [pl.BlockSpec(memory_space=pl.ANY)] * len(after),
            out_specs=pl.BlockSpec((planes, CELLS // 2, PACK), lambda n, s: (0, 0, 0)),
            scratch_shapes=[
                pltpu.VMEM(((planes + 2) * CELLS, C2), bf16),
                pltpu.VMEM((2, planes, LS + 2, LS, PACK), f32),
                pltpu.SemaphoreType.DMA((planes,)),
            ],
        ),
        out_shape=jax.ShapeDtypeStruct((planes, CELLS // 2, PACK), bf16),
        compiler_params=params(56),
        cost_estimate=pl.CostEstimate(
            flops=2 * planes * CELLS * TAPS * C1 * C2, bytes_accessed=6 << 20, transcendentals=0
        ),
    )(device, *cots, weight.reshape(3, 9 * C1, C2), *after)


def weight_two_kernel(planes, pieces, scale, device_ref, *refs):
    samples = len(pieces)
    field_refs, cot_refs = refs[:samples], refs[samples:]
    out_ref, token_ref, cot_ref, flat_ref, lhs_ref, sems = refs[-6:]
    cells = planes * CELLS
    a = pl.program_id(0)

    @pl.when(a == 0)
    def _():
        copies, first = [], 0
        for s in range(samples):
            refs_here = cot_refs[first : first + len(pieces[s])]
            copies += plane_copies(device_ref[0], pieces[s], refs_here, cot_ref.at[s], CELLS, sems.at[s])
            first += len(pieces[s])
        for copy in copies:
            copy.start()
        for s in range(samples):
            cot_ref[s, :CELLS] = jnp.zeros((CELLS, C2), bf16)
            cot_ref[s, cells + CELLS :] = jnp.zeros((CELLS, C2), bf16)

            def cells_of(p):
                x = field_refs[s][p].astype(f32)
                return jnp.concatenate([x, pltpu.roll(x, C1, 1)], axis=0)

            for j in range(planes // 2):
                pair = jnp.concatenate([cells_of(2 * j), cells_of(2 * j + 1)], axis=0)
                flat_ref[s, :, j * PACK : (j + 1) * PACK] = pair.T[:C1]

        lane = lax.broadcasted_iota(jnp.int32, (1, cells), 1)
        row, column = (lane // LS) % LS, lane % LS
        for b in range(3):
            for c in range(3):
                inside = (row + b >= 1) & (row + b <= LS) & (column + c >= 1) & (column + c <= LS)
                mask = inside.astype(f32)
                shift = (-(LS * (b - 1) + c - 1)) % cells
                t = 3 * b + c
                for s in range(samples):
                    value = flat_ref[s]
                    if shift:
                        value = pltpu.roll(value, shift, 1) * mask
                    lhs_ref[s, t * C1 : (t + 1) * C1] = value.astype(bf16)
        for copy in copies:
            copy.wait()

    rows = pl.ds(pl.multiple_of((2 - a) * CELLS, CELLS), cells)
    total = None
    for s in range(samples):
        term = jnp.dot(lhs_ref[s], cot_ref[s, rows], preferred_element_type=f32)
        total = term if total is None else total + term
    out_ref[...] = total * scale
    token_ref[...] = jnp.zeros(token_ref.shape, f32)


def weight_two(device, fields, pieces, cots, scale, after):
    samples = len(fields)
    planes = fields[0].shape[0]
    cells = planes * CELLS
    block = 9 * C1
    flat = [value for sample in cots for value in sample]
    return pl.pallas_call(
        lambda *refs: weight_two_kernel(planes, pieces, scale, *refs),
        grid_spec=pltpu.PrefetchScalarGridSpec(
            num_scalar_prefetch=1,
            grid=(3,),
            in_specs=[pl.BlockSpec(field.shape, lambda n, s: (0, 0, 0)) for field in fields]
            + [pl.BlockSpec(memory_space=pl.ANY)] * (len(flat) + len(after)),
            out_specs=(
                pl.BlockSpec((block, C2), lambda n, s: (n, 0)),
                pl.BlockSpec((8, PACK), lambda n, s: (0, 0)),
            ),
            scratch_shapes=[
                pltpu.VMEM((samples, (planes + 2) * CELLS, C2), bf16),
                pltpu.VMEM((samples, C1, cells), f32),
                pltpu.VMEM((samples, block, cells), bf16),
                pltpu.SemaphoreType.DMA((samples, planes)),
            ],
        ),
        out_shape=(
            jax.ShapeDtypeStruct((TAPS * C1, C2), f32),
            jax.ShapeDtypeStruct((8, PACK), f32),
        ),
        compiler_params=params(60),
        cost_estimate=pl.CostEstimate(
            flops=2 * samples * cells * TAPS * C1 * C2, bytes_accessed=18 << 20, transcendentals=0
        ),
    )(device, *fields, *flat, *after)


def grad_pre_kernel(pieces_ref, slope_ref, lhs_ref, *refs):
    grad_ref, partial_ref, spread_ref, packed_ref = refs[-4:]
    for r in range(BLOCK):
        for u in range(BLOCK // 2):
            piece = r * BLOCK + 2 * u
            first = pieces_ref[piece].astype(f32)
            second = pieces_ref[piece + 1].astype(f32)
            low = low_lanes(first.shape)
            top = jnp.where(low, first, pltpu.roll(second, C1, 1))
            bottom = jnp.where(low, pltpu.roll(first, C1, 1), second)
            for i in range(LS):
                source = top if i < LS // 2 else bottom
                start = (i % (LS // 2)) * LS
                spread_ref[u, pl.ds(BLOCK * i + r, LS, stride=LAT), :] = source[start : start + LS]
    grads = []
    for u in range(BLOCK // 2):
        lanes = slice(u * PACK, (u + 1) * PACK)
        value = (spread_ref[u] * slope_ref[:, lanes]).astype(bf16)
        grad_ref[:, lanes] = value
        grads.append(value)
    grad = jnp.concatenate(grads, axis=1)
    for lateral in range(9):
        window = lhs_ref[:, lateral * WINDOW : (lateral + 1) * WINDOW]
        product = lax.dot_general(window, grad, (((0,), (0,)), ((), ())), preferred_element_type=f32)
        for c in range(3):
            sums = []
            for parity in range(2):
                part = None
                for pair in range(BLOCK // 2):
                    column = 2 * pair + parity + c - 1
                    slot = column if column >= 0 else BLOCK + 1
                    term = product[slot * C1 : (slot + 1) * C1, pair * PACK : (pair + 1) * PACK]
                    part = term if part is None else part + term
                sums.append(part)
            total = sums[0] + pltpu.roll(sums[1], C1, 1)
            top, bottom = total[: C1 // 2], total[C1 // 2 :]
            t = 3 * lateral + c
            packed_ref[t * (C1 // 2) : (t + 1) * (C1 // 2)] = jnp.where(
                low_lanes(top.shape), top, pltpu.roll(bottom, C1, 1)
            )
    packed_ref[TAPS * (C1 // 2) :] = jnp.zeros(((32 - TAPS) * (C1 // 2), PACK), f32)
    for row in range(C1 // 2):
        entry = packed_ref[pl.ds(row, 32, stride=C1 // 2), :]
        partial_ref[row] = entry.astype(bf16)


def grad_pre_of(pieces, slope, lhs, after):
    rows = LS * LAT
    whole = pl.BlockSpec(memory_space=pltpu.VMEM)
    return pl.pallas_call(
        grad_pre_kernel,
        in_specs=[whole] * 3 + [pl.BlockSpec(memory_space=pl.ANY)] * len(after),
        out_shape=(
            jax.ShapeDtypeStruct((rows, GROUP), bf16),
            jax.ShapeDtypeStruct((C1 // 2, 32, PACK), bf16),
        ),
        scratch_shapes=[
            pltpu.VMEM((BLOCK // 2, rows, PACK), f32),
            pltpu.VMEM((32 * (C1 // 2), PACK), f32),
        ],
        compiler_params=params(24),
        cost_estimate=pl.CostEstimate(
            flops=2 * rows * 9 * WINDOW * GROUP, bytes_accessed=3 << 20, transcendentals=0
        ),
    )(pieces, slope, lhs, *after)


def back_one_kernel(before_ref, own_ref, after_ref, w_ref, out_ref, lhs_ref):
    for a, ref in enumerate((before_ref, own_ref, after_ref)):
        write_windows(lhs_ref, a, [ref[g * LAT : (g + 1) * LAT].astype(f32) for g in range(LS)])
    result = jnp.dot(lhs_ref[...], w_ref[...], preferred_element_type=f32)
    for g in range(LS):
        out_ref[:, g * GROUP : (g + 1) * GROUP] = result[g * LAT : (g + 1) * LAT].astype(bf16)


def back_one(before, own, after, band):
    rows = LS * LAT
    return pl.pallas_call(
        back_one_kernel,
        out_shape=jax.ShapeDtypeStruct((LAT, LAT * C1), bf16),
        scratch_shapes=[pltpu.VMEM((rows, 9 * WINDOW), bf16)],
        compiler_params=params(24),
        cost_estimate=pl.CostEstimate(
            flops=2 * rows * 9 * WINDOW * GROUP, bytes_accessed=3 << 20, transcendentals=0
        ),
    )(before, own, after, band)


def sum_kernel(scale, shares_ref, *refs):
    out_ref = refs[-1]
    total = jnp.sum(shares_ref[...].astype(f32), axis=0) * scale
    out_ref[...] = jnp.broadcast_to(total.astype(bf16)[None], out_ref.shape)


def sum_shares(shares, scale, after):
    whole = pl.BlockSpec(memory_space=pltpu.VMEM)
    return pl.pallas_call(
        lambda *refs: sum_kernel(scale, *refs),
        in_specs=[whole] + [pl.BlockSpec(memory_space=pl.ANY)] * len(after),
        out_shape=jax.ShapeDtypeStruct(shares.shape, bf16),
        compiler_params=params(16),
        cost_estimate=pl.CostEstimate(flops=0, bytes_accessed=1 << 20, transcendentals=0),
    )(shares, *after)


def unpack_kernel(packed_ref, *refs):
    out_ref, wide_ref = refs[-2:]
    wide_ref[...] = packed_ref[...].astype(f32).reshape(wide_ref.shape)
    for t in range(TAPS):
        entry = wide_ref[pl.ds(t, C1 // 2, stride=32), :]
        out_ref[t] = jnp.concatenate([entry[:, :C1], entry[:, C1:]], axis=0)


def unpack(packed, after):
    whole = pl.BlockSpec(memory_space=pltpu.VMEM)
    return pl.pallas_call(
        unpack_kernel,
        in_specs=[whole] + [pl.BlockSpec(memory_space=pl.ANY)] * len(after),
        out_shape=jax.ShapeDtypeStruct((TAPS, C1, C1), f32),
        scratch_shapes=[pltpu.VMEM((32 * (C1 // 2), PACK), f32)],
        compiler_params=params(16),
        cost_estimate=pl.CostEstimate(flops=0, bytes_accessed=1 << 20, transcendentals=0),
    )(packed, *after)


def neighbours(value, axis):
    count = lax.axis_size(axis)
    before = lax.ppermute(value, axis, [(i, i + 1) for i in range(count - 1)])
    after = lax.ppermute(value, axis, [(i + 1, i) for i in range(count - 1)])
    return before, after


def flipped(value, difference):
    count = lax.axis_size("depth")
    return lax.ppermute(value, "depth", [(i, i ^ difference) for i in range(count)])


def over_samples(value):
    count = lax.axis_size("sample")
    return [value] + [
        lax.ppermute(value, "sample", [(i, (i + shift) % count) for i in range(count)])
        for shift in range(1, count)
    ]


def on_device(volume, conv1_weight, conv2_weight, cotangent):
    samples = lax.axis_size("sample")
    shards = lax.axis_size("depth")
    flat_two = conv2_weight.reshape(TAPS * C1, C2)
    own = volume.reshape(LAT, LAT * C1)
    device = lax.axis_index("depth").astype(jnp.int32).reshape(1)
    cot = cotangent.reshape(CELLS, C2)

    core, chip = 1, 2
    outer = list(range(4, shards, 4))
    far = [flipped(cot, difference) for difference in outer]
    before, after = neighbours(own, "depth")
    cot_chip = flipped(cot, chip)

    back_weight = jnp.swapaxes(conv1_weight[::-1], 1, 2)
    band = banded(conv1_weight)
    back_band = banded(back_weight)

    moved, slope, windows = conv_one(before, own, after, band, [])
    fields = lax.all_to_all(moved, "depth", split_axis=0, concat_axis=0, tiled=True)

    near = joined([cot, cot_chip], [fields])
    far = joined(far, [slope, cot_chip])
    far_chip = flipped(far, chip)
    cots = [near, far, far_chip]
    pieces = [[0, chip], outer, [difference + chip for difference in outer]]
    pieces = pieces + [[difference + core for difference in piece] for piece in pieces]

    near_core, far_core = flipped(near, core), flipped(far, core)
    partial, done = conv_two(fields, flat_two, [near_core, far_core])
    features = lax.psum_scatter(partial, "depth", scatter_dimension=0, tiled=True)

    own_cots = cots + [near_core, far_core, flipped(far_chip, core)]
    grad_pieces = back_two(device, pieces, own_cots, flat_two, [done])
    returned = lax.all_to_all(grad_pieces, "depth", split_axis=0, concat_axis=0, tiled=True)
    half = joined(cots, [done])
    halves = [[difference for piece in group for difference in piece] for group in (pieces[:3], pieces[3:])]
    all_pieces, all_cots = [pieces], [own_cots]
    for value in over_samples(half)[1:]:
        value = held(value, [returned])
        all_pieces.append(halves)
        all_cots.append([value, flipped(value, core)])
    all_fields = over_samples(fields)

    grad_pre, partial_one = grad_pre_of(returned, slope, windows, [])
    grad_before, grad_after = neighbours(grad_pre, "depth")

    devices = samples * shards
    both = ("sample", "depth")
    scale_one = 1.0 / math.sqrt(samples * shards * LAT * LAT)
    shares = partial_one.reshape(devices, -1, PACK)
    shares = lax.all_to_all(shares, both, split_axis=0, concat_axis=0, tiled=True)
    scale_two = 1.0 / math.sqrt(samples * shards * CELLS)
    grad_conv2, token = weight_two(
        device, all_fields, all_pieces, all_cots, scale_two, [grad_pre]
    )
    summed = sum_shares(shares, scale_one, [token])
    shares = lax.all_to_all(summed, both, split_axis=0, concat_axis=0, tiled=True)
    grad_volume = back_one(grad_before, grad_pre, grad_after, back_band)
    grad_conv1 = unpack(shares.reshape(C1 // 2, 32, PACK), [])

    return (
        features.reshape(cotangent.shape),
        grad_volume.reshape(volume.shape),
        grad_conv1,
        grad_conv2.reshape(conv2_weight.shape),
    )


def solution(mesh):
    return jax.shard_map(
        on_device,
        mesh=mesh,
        in_specs=(
            P("sample", "depth", None, None),
            P(),
            P(None, "depth", None),
            P("sample", "depth", None, None, None),
        ),
        out_specs=(
            P("sample", "depth", None, None, None),
            P("sample", "depth", None, None),
            P(),
            P(None, "depth", None),
        ),
        check_vma=False,
    )
```

```python
import math

import jax
import jax.numpy as jnp
from jax import lax
from jax.experimental import pallas as pl
from jax.experimental.pallas import tpu as pltpu
from jax.sharding import PartitionSpec as P

C1 = 64
LAT = 32
BLOCK = 4
C2 = 1024
LS = 8
CELLS = LS * LS
GROUP = BLOCK * C1
WINDOW = GROUP + 2 * C1
TAPS = 27
PACK = 2 * C1

root_coef = 0.7978845608028654
cubic_coef = 0.044715

f32 = jnp.float32
bf16 = jnp.bfloat16


def params(mebibytes):
    return pltpu.CompilerParams(vmem_limit_bytes=mebibytes * 1024 * 1024)


def low_lanes(shape):
    return lax.broadcasted_iota(jnp.int32, shape, len(shape) - 1) < C1


def band_kernel(w_ref, out_ref):
    for lateral in range(9):
        for slot in range(BLOCK + 2):
            column = slot if slot <= BLOCK else -1
            for pair in range(BLOCK // 2):
                halves = []
                for own in (2 * pair, 2 * pair + 1):
                    c = column - own + 1
                    if 0 <= c <= 2:
                        halves.append(w_ref[3 * lateral + c])
                    else:
                        halves.append(jnp.zeros((C1, C1), bf16))
                start = lateral * WINDOW + slot * C1
                out_ref[start : start + C1, pair * PACK : (pair + 1) * PACK] = jnp.concatenate(halves, axis=1)


def banded(weight):
    return pl.pallas_call(
        band_kernel,
        out_shape=jax.ShapeDtypeStruct((9 * WINDOW, GROUP), bf16),
        compiler_params=params(16),
        cost_estimate=pl.CostEstimate(flops=0, bytes_accessed=4 << 20, transcendentals=0),
    )(weight)


def write_windows(lhs_ref, a, groups):
    field = jnp.concatenate(groups, axis=0)
    blank = jnp.zeros((LAT, PACK), f32)
    after = jnp.concatenate([g[:, :PACK] for g in groups[1:]] + [blank], axis=0)
    before = jnp.concatenate([blank] + [g[:, GROUP - PACK :] for g in groups[:-1]], axis=0)
    edge = jnp.where(low_lanes(after.shape), after, before)
    window = jnp.concatenate([field, edge], axis=1)
    rows = window.shape[0]
    row = lax.broadcasted_iota(jnp.int32, window.shape, 0) % LAT
    shifted = [
        jnp.where(row == 0, 0.0, pltpu.roll(window, 1, 0)),
        window,
        jnp.where(row == LAT - 1, 0.0, pltpu.roll(window, rows - 1, 0)),
    ]
    for b in range(3):
        start = (3 * a + b) * WINDOW
        lhs_ref[:, start : start + WINDOW] = shifted[b].astype(bf16)


def conv_one_kernel(before_ref, own_ref, after_ref, w_ref, *refs):
    moved_ref, slope_ref, lhs_ref, hid_ref = refs[-4:]
    for a, ref in enumerate((before_ref, own_ref, after_ref)):
        write_windows(lhs_ref, a, [ref[:, g * GROUP : (g + 1) * GROUP].astype(f32) for g in range(LS)])
    pre = jnp.dot(lhs_ref[...], w_ref[...], preferred_element_type=f32)
    tanh_val = jnp.tanh(root_coef * (pre + cubic_coef * pre * pre * pre))
    hidden = 0.5 * pre * (1.0 + tanh_val)
    slope_ref[...] = 0.5 * (1.0 + tanh_val) + 0.5 * pre * (1.0 - tanh_val * tanh_val) * root_coef * (
        1.0 + 3.0 * cubic_coef * pre * pre
    )
    for u in range(BLOCK // 2):
        hid_ref[u] = hidden[:, u * PACK : (u + 1) * PACK]
    for r in range(BLOCK):
        for u in range(BLOCK // 2):
            cells = jnp.concatenate(
                [hid_ref[u, pl.ds(BLOCK * i + r, LS, stride=LAT), :] for i in range(LS)], axis=0
            )
            top, bottom = cells[: CELLS // 2], cells[CELLS // 2 :]
            low = low_lanes(top.shape)
            piece = r * BLOCK + 2 * u
            moved_ref[piece] = jnp.where(low, top, pltpu.roll(bottom, C1, 1)).astype(bf16)
            moved_ref[piece + 1] = jnp.where(low, pltpu.roll(top, C1, 1), bottom).astype(bf16)


def conv_one(before, own, after, band, waits):
    rows = LS * LAT
    whole = pl.BlockSpec(memory_space=pltpu.VMEM)
    return pl.pallas_call(
        conv_one_kernel,
        in_specs=[whole] * 4 + [pl.BlockSpec(memory_space=pl.ANY)] * len(waits),
        out_shape=(
            jax.ShapeDtypeStruct((BLOCK * BLOCK, CELLS // 2, PACK), bf16),
            jax.ShapeDtypeStruct((rows, GROUP), f32),
            jax.ShapeDtypeStruct((rows, 9 * WINDOW), bf16),
        ),
        scratch_shapes=[pltpu.VMEM((BLOCK // 2, rows, PACK), f32)],
        compiler_params=params(24),
        cost_estimate=pl.CostEstimate(
            flops=2 * rows * 9 * WINDOW * GROUP, bytes_accessed=5 << 20, transcendentals=rows * GROUP
        ),
    )(before, own, after, band, *waits)


def shift_cells(field, step):
    if step == 0:
        return field
    column = lax.broadcasted_iota(jnp.int32, field.shape, 1)
    edge = LS - 1 if step > 0 else 0
    return jnp.where(column == edge, 0.0, pltpu.roll(field, (-step) % LS, 1))


def conv_two_kernel(planes, x_ref, w_ref, *refs):
    out_ref, token_ref, lhs_ref, v_ref = refs[-4:]
    token_ref[...] = jnp.zeros(token_ref.shape, f32)

    @pl.when(pl.program_id(0) == 0)
    def _():
        v_ref[:, :, 0] = jnp.zeros((3, 2, LS + 2, LS, PACK), f32)
        v_ref[:, :, planes + 1] = jnp.zeros((3, 2, LS + 2, LS, PACK), f32)
        edge = jnp.zeros((LS, PACK), f32)

        def spread(p, carry):
            x = x_ref[p].astype(f32)
            turned = pltpu.roll(x, C1, 1)
            for half, parts in enumerate(((x, turned), (turned, x))):
                cells = jnp.concatenate(parts, axis=0).reshape(LS, LS, PACK)
                for c in range(3):
                    v_ref[c, half, p + 1, 0] = edge
                    v_ref[c, half, p + 1, 1 : LS + 1] = shift_cells(cells, c - 1)
                    v_ref[c, half, p + 1, LS + 1] = edge
            return carry

        lax.fori_loop(0, planes, spread, 0)

        def gather(p, carry):
            rows = pl.ds(pl.multiple_of(p * CELLS, CELLS), CELLS)
            for m in range((TAPS + 1) // 2):
                t = 2 * m
                low = v_ref[t % 3, 0, p + t // 9, pl.ds((t // 3) % 3, LS)].reshape(CELLS, PACK)
                t = 2 * m + 1
                if t < TAPS:
                    high = v_ref[t % 3, 1, p + t // 9, pl.ds((t // 3) % 3, LS)].reshape(CELLS, PACK)
                    tile = jnp.where(low_lanes(low.shape), low, high)
                    lhs_ref[rows, m * PACK : (m + 1) * PACK] = tile.astype(bf16)
                else:
                    lhs_ref[rows, m * PACK : m * PACK + C1] = low[:, :C1].astype(bf16)
            return carry

        lax.fori_loop(0, planes, gather, 0)

    chunk = 4 * CELLS
    for m in range(planes * CELLS // chunk):
        rows = slice(m * chunk, (m + 1) * chunk)
        out_ref[rows] = jnp.dot(lhs_ref[rows], w_ref[...], preferred_element_type=f32).astype(bf16)


def conv_two(pieces, weight, after):
    planes = pieces.shape[0]
    cells = planes * CELLS
    block = 256
    return pl.pallas_call(
        lambda *refs: conv_two_kernel(planes, *refs),
        grid=(C2 // block,),
        in_specs=[
            pl.BlockSpec(pieces.shape, lambda n: (0, 0, 0)),
            pl.BlockSpec((TAPS * C1, block), lambda n: (0, n)),
        ]
        + [pl.BlockSpec(memory_space=pl.ANY)] * len(after),
        out_specs=(
            pl.BlockSpec((cells, block), lambda n: (0, n)),
            pl.BlockSpec((8, PACK), lambda n: (0, 0)),
        ),
        out_shape=(jax.ShapeDtypeStruct((cells, C2), bf16), jax.ShapeDtypeStruct((8, PACK), f32)),
        scratch_shapes=[
            pltpu.VMEM((cells, TAPS * C1), bf16),
            pltpu.VMEM((3, 2, planes + 2, LS + 2, LS, PACK), f32),
        ],
        compiler_params=params(56),
        cost_estimate=pl.CostEstimate(
            flops=2 * cells * TAPS * C1 * C2, bytes_accessed=10 << 20, transcendentals=0
        ),
    )(pieces, weight, *after)


def join_kernel(count, *refs):
    out_ref, first = refs[-1], 0
    for ref in refs[:count]:
        rows = ref.shape[0]
        out_ref[first : first + rows] = ref[...]
        first += rows


def joined(values, after=()):
    rows = sum(value.shape[0] for value in values)
    columns = values[0].shape[1]
    return pl.pallas_call(
        lambda *refs: join_kernel(len(values), *refs),
        grid=(1,),
        in_specs=[pl.BlockSpec(value.shape, lambda n: (0, 0)) for value in values]
        + [pl.BlockSpec(memory_space=pl.ANY)] * len(after),
        out_specs=pl.BlockSpec((rows, columns), lambda n: (0, 0)),
        out_shape=jax.ShapeDtypeStruct((rows, columns), values[0].dtype),
        compiler_params=params(32),
        cost_estimate=pl.CostEstimate(flops=0, bytes_accessed=4 * rows * columns, transcendentals=0),
    )(*values, *after)


def held_kernel(*refs):
    pass


def held(value, after):
    return pl.pallas_call(
        held_kernel,
        in_specs=[pl.BlockSpec(memory_space=pl.ANY)] * (1 + len(after)),
        out_specs=pl.BlockSpec(memory_space=pl.ANY),
        out_shape=jax.ShapeDtypeStruct(value.shape, value.dtype),
        input_output_aliases={0: 0},
        compiler_params=params(16),
    )(value, *after)


def plane_copies(device, pieces, refs, target_ref, base, sems):
    copies = []
    for differences, ref in zip(pieces, refs):
        for k, difference in enumerate(differences):
            row = pl.multiple_of(base + (device ^ difference) * CELLS, CELLS)
            source = ref.at[pl.ds(k * CELLS, CELLS), :]
            target = target_ref.at[pl.ds(row, CELLS), :]
            copies.append(pltpu.make_async_copy(source, target, sems.at[len(copies)]))
    return copies


def back_two_kernel(planes, pieces, device_ref, *refs):
    cot_refs = refs[: len(pieces)]
    w_ref, out_ref, cot_ref, sum_ref, sems = refs[len(pieces)], *refs[-4:]
    b = pl.program_id(0)
    cells = planes * CELLS

    @pl.when(b == 0)
    def _():
        copies = plane_copies(device_ref[0], pieces, cot_refs, cot_ref, CELLS, sems)
        for copy in copies:
            copy.start()
        cot_ref[:CELLS] = jnp.zeros((CELLS, C2), bf16)
        cot_ref[cells + CELLS :] = jnp.zeros((CELLS, C2), bf16)
        sum_ref[...] = jnp.zeros(sum_ref.shape, f32)
        for copy in copies:
            copy.wait()

    total = None
    for a in range(3):
        term = lax.dot_general(
            cot_ref[(2 - a) * CELLS : (2 - a) * CELLS + cells],
            w_ref[a],
            (((1,), (1,)), ((), ())),
            preferred_element_type=f32,
        )
        total = term if total is None else total + term
    rows = pl.ds(b, LS)
    first = total[:, :PACK].reshape(planes, LS, LS, PACK)
    sum_ref[0, :, rows] = sum_ref[0, :, rows] + first
    last = jnp.concatenate([total[:, PACK:], jnp.zeros((cells, C1), f32)], axis=1)
    sum_ref[1, :, rows] = sum_ref[1, :, rows] + last.reshape(planes, LS, LS, PACK)

    @pl.when(b == 2)
    def _():
        def finish(p, carry):
            pair = sum_ref[0, p, 1 : LS + 1]
            single = sum_ref[1, p, 1 : LS + 1]
            total = shift_cells(pair, 1) + shift_cells(single, -1)
            total = total.reshape(CELLS, PACK) + pltpu.roll(pair.reshape(CELLS, PACK), C1, 1)
            top, bottom = total[: CELLS // 2], total[CELLS // 2 :]
            out_ref[p] = jnp.where(low_lanes(top.shape), top, pltpu.roll(bottom, C1, 1)).astype(bf16)
            return carry

        lax.fori_loop(0, planes, finish, 0)


def back_two(device, pieces, cots, weight, after):
    planes = sum(len(piece) for piece in pieces)
    return pl.pallas_call(
        lambda *refs: back_two_kernel(planes, pieces, *refs),
        grid_spec=pltpu.PrefetchScalarGridSpec(
            num_scalar_prefetch=1,
            grid=(3,),
            in_specs=[pl.BlockSpec(memory_space=pl.ANY)] * len(cots)
            + [pl.BlockSpec((3, 3 * C1, C2), lambda n, s: (0, n, 0))]
            + [pl.BlockSpec(memory_space=pl.ANY)] * len(after),
            out_specs=pl.BlockSpec((planes, CELLS // 2, PACK), lambda n, s: (0, 0, 0)),
            scratch_shapes=[
                pltpu.VMEM(((planes + 2) * CELLS, C2), bf16),
                pltpu.VMEM((2, planes, LS + 2, LS, PACK), f32),
                pltpu.SemaphoreType.DMA((planes,)),
            ],
        ),
        out_shape=jax.ShapeDtypeStruct((planes, CELLS // 2, PACK), bf16),
        compiler_params=params(56),
        cost_estimate=pl.CostEstimate(
            flops=2 * planes * CELLS * TAPS * C1 * C2, bytes_accessed=6 << 20, transcendentals=0
        ),
    )(device, *cots, weight.reshape(3, 9 * C1, C2), *after)


def weight_two_kernel(planes, pieces, scale, based, device_ref, field_ref, *refs):
    cot_refs = refs[: len(pieces)]
    base_ref = refs[len(pieces)]
    out_ref, token_ref, cot_ref, flat_ref, lhs_ref, sems = refs[-6:]
    cells = planes * CELLS
    a = pl.program_id(0)

    @pl.when(a == 0)
    def _():
        copies = plane_copies(device_ref[0], pieces, cot_refs, cot_ref, CELLS, sems)
        for copy in copies:
            copy.start()
        cot_ref[:CELLS] = jnp.zeros((CELLS, C2), bf16)
        cot_ref[cells + CELLS :] = jnp.zeros((CELLS, C2), bf16)

        def cells_of(p):
            x = field_ref[p].astype(f32)
            return jnp.concatenate([x, pltpu.roll(x, C1, 1)], axis=0)

        for j in range(planes // 2):
            pair = jnp.concatenate([cells_of(2 * j), cells_of(2 * j + 1)], axis=0)
            flat_ref[:, j * PACK : (j + 1) * PACK] = pair.T[:C1]

        lane = lax.broadcasted_iota(jnp.int32, (1, cells), 1)
        row, column = (lane // LS) % LS, lane % LS
        for b in range(3):
            for c in range(3):
                inside = (row + b >= 1) & (row + b <= LS) & (column + c >= 1) & (column + c <= LS)
                mask = inside.astype(f32)
                shift = (-(LS * (b - 1) + c - 1)) % cells
                t = 3 * b + c
                value = flat_ref[...]
                if shift:
                    value = pltpu.roll(value, shift, 1) * mask
                lhs_ref[t * C1 : (t + 1) * C1] = value.astype(bf16)
        for copy in copies:
            copy.wait()

    rows = pl.ds(pl.multiple_of((2 - a) * CELLS, CELLS), cells)
    total = jnp.dot(lhs_ref[...], cot_ref[rows], preferred_element_type=f32) * scale
    out_ref[...] = total + base_ref[...] if based else total
    token_ref[...] = jnp.zeros(token_ref.shape, f32)


def weight_two(device, field, pieces, cots, scale, base, after):
    planes = field.shape[0]
    cells = planes * CELLS
    block = 9 * C1
    extra = ([] if base is None else [base]) + list(after)
    extra_specs = [pl.BlockSpec(memory_space=pl.ANY)] * len(after)
    if base is not None:
        extra_specs = [pl.BlockSpec((block, C2), lambda n, s: (n, 0))] + extra_specs
    return pl.pallas_call(
        lambda *refs: weight_two_kernel(planes, pieces, scale, base is not None, *refs),
        grid_spec=pltpu.PrefetchScalarGridSpec(
            num_scalar_prefetch=1,
            grid=(3,),
            in_specs=[pl.BlockSpec(field.shape, lambda n, s: (0, 0, 0))]
            + [pl.BlockSpec(memory_space=pl.ANY)] * len(cots)
            + extra_specs,
            out_specs=(
                pl.BlockSpec((block, C2), lambda n, s: (n, 0)),
                pl.BlockSpec((8, PACK), lambda n, s: (0, 0)),
            ),
            scratch_shapes=[
                pltpu.VMEM(((planes + 2) * CELLS, C2), bf16),
                pltpu.VMEM((C1, cells), f32),
                pltpu.VMEM((block, cells), bf16),
                pltpu.SemaphoreType.DMA((planes,)),
            ],
        ),
        out_shape=(
            jax.ShapeDtypeStruct((TAPS * C1, C2), f32),
            jax.ShapeDtypeStruct((8, PACK), f32),
        ),
        input_output_aliases={} if base is None else {2 + len(cots): 0},
        compiler_params=params(60),
        cost_estimate=pl.CostEstimate(
            flops=2 * cells * TAPS * C1 * C2, bytes_accessed=12 << 20, transcendentals=0
        ),
    )(device, field, *cots, *extra)


def grad_pre_kernel(pieces_ref, slope_ref, lhs_ref, *refs):
    grad_ref, partial_ref, spread_ref, packed_ref = refs[-4:]
    for r in range(BLOCK):
        for u in range(BLOCK // 2):
            piece = r * BLOCK + 2 * u
            first = pieces_ref[piece].astype(f32)
            second = pieces_ref[piece + 1].astype(f32)
            low = low_lanes(first.shape)
            top = jnp.where(low, first, pltpu.roll(second, C1, 1))
            bottom = jnp.where(low, pltpu.roll(first, C1, 1), second)
            for i in range(LS):
                source = top if i < LS // 2 else bottom
                start = (i % (LS // 2)) * LS
                spread_ref[u, pl.ds(BLOCK * i + r, LS, stride=LAT), :] = source[start : start + LS]
    grads = []
    for u in range(BLOCK // 2):
        lanes = slice(u * PACK, (u + 1) * PACK)
        value = (spread_ref[u] * slope_ref[:, lanes]).astype(bf16)
        grad_ref[:, lanes] = value
        grads.append(value)
    grad = jnp.concatenate(grads, axis=1)
    for lateral in range(9):
        window = lhs_ref[:, lateral * WINDOW : (lateral + 1) * WINDOW]
        product = lax.dot_general(window, grad, (((0,), (0,)), ((), ())), preferred_element_type=f32)
        for c in range(3):
            sums = []
            for parity in range(2):
                part = None
                for pair in range(BLOCK // 2):
                    column = 2 * pair + parity + c - 1
                    slot = column if column >= 0 else BLOCK + 1
                    term = product[slot * C1 : (slot + 1) * C1, pair * PACK : (pair + 1) * PACK]
                    part = term if part is None else part + term
                sums.append(part)
            total = sums[0] + pltpu.roll(sums[1], C1, 1)
            top, bottom = total[: C1 // 2], total[C1 // 2 :]
            t = 3 * lateral + c
            packed_ref[t * (C1 // 2) : (t + 1) * (C1 // 2)] = jnp.where(
                low_lanes(top.shape), top, pltpu.roll(bottom, C1, 1)
            )
    packed_ref[TAPS * (C1 // 2) :] = jnp.zeros(((32 - TAPS) * (C1 // 2), PACK), f32)
    for row in range(C1 // 2):
        entry = packed_ref[pl.ds(row, 32, stride=C1 // 2), :]
        partial_ref[row] = entry.astype(bf16)


def grad_pre_of(pieces, slope, lhs, after):
    rows = LS * LAT
    whole = pl.BlockSpec(memory_space=pltpu.VMEM)
    return pl.pallas_call(
        grad_pre_kernel,
        in_specs=[whole] * 3 + [pl.BlockSpec(memory_space=pl.ANY)] * len(after),
        out_shape=(
            jax.ShapeDtypeStruct((rows, GROUP), bf16),
            jax.ShapeDtypeStruct((C1 // 2, 32, PACK), bf16),
        ),
        scratch_shapes=[
            pltpu.VMEM((BLOCK // 2, rows, PACK), f32),
            pltpu.VMEM((32 * (C1 // 2), PACK), f32),
        ],
        compiler_params=params(24),
        cost_estimate=pl.CostEstimate(
            flops=2 * rows * 9 * WINDOW * GROUP, bytes_accessed=3 << 20, transcendentals=0
        ),
    )(pieces, slope, lhs, *after)


def back_one_kernel(before_ref, own_ref, after_ref, w_ref, out_ref, lhs_ref):
    for a, ref in enumerate((before_ref, own_ref, after_ref)):
        write_windows(lhs_ref, a, [ref[g * LAT : (g + 1) * LAT].astype(f32) for g in range(LS)])
    result = jnp.dot(lhs_ref[...], w_ref[...], preferred_element_type=f32)
    for g in range(LS):
        out_ref[:, g * GROUP : (g + 1) * GROUP] = result[g * LAT : (g + 1) * LAT].astype(bf16)


def back_one(before, own, after, band):
    rows = LS * LAT
    return pl.pallas_call(
        back_one_kernel,
        out_shape=jax.ShapeDtypeStruct((LAT, LAT * C1), bf16),
        scratch_shapes=[pltpu.VMEM((rows, 9 * WINDOW), bf16)],
        compiler_params=params(24),
        cost_estimate=pl.CostEstimate(
            flops=2 * rows * 9 * WINDOW * GROUP, bytes_accessed=3 << 20, transcendentals=0
        ),
    )(before, own, after, band)


def sum_kernel(scale, shares_ref, *refs):
    out_ref = refs[-1]
    total = jnp.sum(shares_ref[...].astype(f32), axis=0) * scale
    out_ref[...] = jnp.broadcast_to(total.astype(bf16)[None], out_ref.shape)


def sum_shares(shares, scale, after):
    whole = pl.BlockSpec(memory_space=pltpu.VMEM)
    return pl.pallas_call(
        lambda *refs: sum_kernel(scale, *refs),
        in_specs=[whole] + [pl.BlockSpec(memory_space=pl.ANY)] * len(after),
        out_shape=jax.ShapeDtypeStruct(shares.shape, bf16),
        compiler_params=params(16),
        cost_estimate=pl.CostEstimate(flops=0, bytes_accessed=1 << 20, transcendentals=0),
    )(shares, *after)


def unpack_kernel(packed_ref, *refs):
    out_ref, wide_ref = refs[-2:]
    wide_ref[...] = packed_ref[...].astype(f32).reshape(wide_ref.shape)
    for t in range(TAPS):
        entry = wide_ref[pl.ds(t, C1 // 2, stride=32), :]
        out_ref[t] = jnp.concatenate([entry[:, :C1], entry[:, C1:]], axis=0)


def unpack(packed, after):
    whole = pl.BlockSpec(memory_space=pltpu.VMEM)
    return pl.pallas_call(
        unpack_kernel,
        in_specs=[whole] + [pl.BlockSpec(memory_space=pl.ANY)] * len(after),
        out_shape=jax.ShapeDtypeStruct((TAPS, C1, C1), f32),
        scratch_shapes=[pltpu.VMEM((32 * (C1 // 2), PACK), f32)],
        compiler_params=params(16),
        cost_estimate=pl.CostEstimate(flops=0, bytes_accessed=1 << 20, transcendentals=0),
    )(packed, *after)


def neighbours(value, axis):
    count = lax.axis_size(axis)
    before = lax.ppermute(value, axis, [(i, i + 1) for i in range(count - 1)])
    after = lax.ppermute(value, axis, [(i + 1, i) for i in range(count - 1)])
    return before, after


def flipped(value, difference):
    count = lax.axis_size("depth")
    return lax.ppermute(value, "depth", [(i, i ^ difference) for i in range(count)])


def over_samples(value):
    count = lax.axis_size("sample")
    return [value] + [
        lax.ppermute(value, "sample", [(i, (i + shift) % count) for i in range(count)])
        for shift in range(1, count)
    ]


def on_device(volume, conv1_weight, conv2_weight, cotangent):
    samples = lax.axis_size("sample")
    shards = lax.axis_size("depth")
    flat_two = conv2_weight.reshape(TAPS * C1, C2)
    own = volume.reshape(LAT, LAT * C1)
    device = lax.axis_index("depth").astype(jnp.int32).reshape(1)
    cot = cotangent.reshape(CELLS, C2)

    core, chip = 1, 2
    outer = list(range(4, shards, 4))
    far = [flipped(cot, difference) for difference in outer]
    before, after = neighbours(own, "depth")
    cot_chip = flipped(cot, chip)

    back_weight = jnp.swapaxes(conv1_weight[::-1], 1, 2)
    band = banded(conv1_weight)
    back_band = banded(back_weight)

    moved, slope, windows = conv_one(before, own, after, band, [])
    fields = lax.all_to_all(moved, "depth", split_axis=0, concat_axis=0, tiled=True)

    near = joined([cot, cot_chip], [fields])
    far = joined(far, [slope, cot_chip])
    far_chip = flipped(far, chip)
    cots = [near, far, far_chip]
    pieces = [[0, chip], outer, [difference + chip for difference in outer]]
    pieces = pieces + [[difference + core for difference in piece] for piece in pieces]

    near_core, far_core = flipped(near, core), flipped(far, core)
    partial, done = conv_two(fields, flat_two, [near_core, far_core])
    features = lax.psum_scatter(partial, "depth", scatter_dimension=0, tiled=True)

    own_cots = cots + [near_core, far_core, flipped(far_chip, core)]
    grad_pieces = back_two(device, pieces, own_cots, flat_two, [done])
    returned = lax.all_to_all(grad_pieces, "depth", split_axis=0, concat_axis=0, tiled=True)
    scale_two = 1.0 / math.sqrt(samples * shards * CELLS)
    grad_conv2, token = weight_two(
        device, fields, pieces, own_cots, scale_two, None, [grad_pieces]
    )
    all_fields = over_samples(fields)
    grad_pre, partial_one = grad_pre_of(returned, slope, windows, [token] + all_fields[1:])
    half = joined(cots, [done])
    halves = [[difference for piece in group for difference in piece] for group in (pieces[:3], pieces[3:])]
    all_pieces, all_cots = [pieces], [own_cots]
    for value in over_samples(half)[1:]:
        value = held(value, [grad_pre])
        all_pieces.append(halves)
        all_cots.append([value, flipped(value, core)])

    grad_before, grad_after = neighbours(grad_pre, "depth")

    devices = samples * shards
    both = ("sample", "depth")
    scale_one = 1.0 / math.sqrt(samples * shards * LAT * LAT)
    shares = partial_one.reshape(devices, -1, PACK)
    shares = lax.all_to_all(shares, both, split_axis=0, concat_axis=0, tiled=True)
    for k in range(1, samples):
        grad_conv2, token = weight_two(
            device, all_fields[k], all_pieces[k], all_cots[k], scale_two, grad_conv2, [grad_pre]
        )
    summed = sum_shares(shares, scale_one, [token])
    shares = lax.all_to_all(summed, both, split_axis=0, concat_axis=0, tiled=True)
    grad_volume = back_one(grad_before, grad_pre, grad_after, back_band)
    grad_conv1 = unpack(shares.reshape(C1 // 2, 32, PACK), [])

    return (
        features.reshape(cotangent.shape),
        grad_volume.reshape(volume.shape),
        grad_conv1,
        grad_conv2.reshape(conv2_weight.shape),
    )


def solution(mesh):
    return jax.shard_map(
        on_device,
        mesh=mesh,
        in_specs=(
            P("sample", "depth", None, None),
            P(),
            P(None, "depth", None),
            P("sample", "depth", None, None, None),
        ),
        out_specs=(
            P("sample", "depth", None, None, None),
            P("sample", "depth", None, None),
            P(),
            P(None, "depth", None),
        ),
        check_vma=False,
    )
```

```python
import math

import jax
import jax.numpy as jnp
from jax import lax
from jax.experimental import pallas as pl
from jax.experimental.pallas import tpu as pltpu
from jax.sharding import PartitionSpec as P

C1 = 64
LAT = 32
BLOCK = 4
C2 = 1024
LS = 8
CELLS = LS * LS
GROUP = BLOCK * C1
WINDOW = GROUP + 2 * C1
TAPS = 27
PACK = 2 * C1

root_coef = 0.7978845608028654
cubic_coef = 0.044715

f32 = jnp.float32
bf16 = jnp.bfloat16


def params(mebibytes):
    return pltpu.CompilerParams(vmem_limit_bytes=mebibytes * 1024 * 1024)


def low_lanes(shape):
    return lax.broadcasted_iota(jnp.int32, shape, len(shape) - 1) < C1


def band_kernel(w_ref, out_ref):
    for lateral in range(9):
        for slot in range(BLOCK + 2):
            column = slot if slot <= BLOCK else -1
            for pair in range(BLOCK // 2):
                halves = []
                for own in (2 * pair, 2 * pair + 1):
                    c = column - own + 1
                    if 0 <= c <= 2:
                        halves.append(w_ref[3 * lateral + c])
                    else:
                        halves.append(jnp.zeros((C1, C1), bf16))
                start = lateral * WINDOW + slot * C1
                out_ref[start : start + C1, pair * PACK : (pair + 1) * PACK] = jnp.concatenate(halves, axis=1)


def banded(weight):
    return pl.pallas_call(
        band_kernel,
        out_shape=jax.ShapeDtypeStruct((9 * WINDOW, GROUP), bf16),
        compiler_params=params(16),
        cost_estimate=pl.CostEstimate(flops=0, bytes_accessed=4 << 20, transcendentals=0),
    )(weight)


def write_windows(lhs_ref, a, groups):
    field = jnp.concatenate(groups, axis=0)
    blank = jnp.zeros((LAT, PACK), f32)
    after = jnp.concatenate([g[:, :PACK] for g in groups[1:]] + [blank], axis=0)
    before = jnp.concatenate([blank] + [g[:, GROUP - PACK :] for g in groups[:-1]], axis=0)
    edge = jnp.where(low_lanes(after.shape), after, before)
    window = jnp.concatenate([field, edge], axis=1)
    rows = window.shape[0]
    row = lax.broadcasted_iota(jnp.int32, window.shape, 0) % LAT
    shifted = [
        jnp.where(row == 0, 0.0, pltpu.roll(window, 1, 0)),
        window,
        jnp.where(row == LAT - 1, 0.0, pltpu.roll(window, rows - 1, 0)),
    ]
    for b in range(3):
        start = (3 * a + b) * WINDOW
        lhs_ref[:, start : start + WINDOW] = shifted[b].astype(bf16)


def conv_one_kernel(before_ref, own_ref, after_ref, w_ref, *refs):
    moved_ref, slope_ref, lhs_ref, hid_ref = refs[-4:]
    for a, ref in enumerate((before_ref, own_ref, after_ref)):
        write_windows(lhs_ref, a, [ref[:, g * GROUP : (g + 1) * GROUP].astype(f32) for g in range(LS)])
    pre = jnp.dot(lhs_ref[...], w_ref[...], preferred_element_type=f32)
    tanh_val = jnp.tanh(root_coef * (pre + cubic_coef * pre * pre * pre))
    hidden = 0.5 * pre * (1.0 + tanh_val)
    slope_ref[...] = 0.5 * (1.0 + tanh_val) + 0.5 * pre * (1.0 - tanh_val * tanh_val) * root_coef * (
        1.0 + 3.0 * cubic_coef * pre * pre
    )
    for u in range(BLOCK // 2):
        hid_ref[u] = hidden[:, u * PACK : (u + 1) * PACK]
    for r in range(BLOCK):
        for u in range(BLOCK // 2):
            cells = jnp.concatenate(
                [hid_ref[u, pl.ds(BLOCK * i + r, LS, stride=LAT), :] for i in range(LS)], axis=0
            )
            top, bottom = cells[: CELLS // 2], cells[CELLS // 2 :]
            low = low_lanes(top.shape)
            piece = r * BLOCK + 2 * u
            moved_ref[piece] = jnp.where(low, top, pltpu.roll(bottom, C1, 1)).astype(bf16)
            moved_ref[piece + 1] = jnp.where(low, pltpu.roll(top, C1, 1), bottom).astype(bf16)


def conv_one(before, own, after, band, waits):
    rows = LS * LAT
    whole = pl.BlockSpec(memory_space=pltpu.VMEM)
    return pl.pallas_call(
        conv_one_kernel,
        in_specs=[whole] * 4 + [pl.BlockSpec(memory_space=pl.ANY)] * len(waits),
        out_shape=(
            jax.ShapeDtypeStruct((BLOCK * BLOCK, CELLS // 2, PACK), bf16),
            jax.ShapeDtypeStruct((rows, GROUP), f32),
            jax.ShapeDtypeStruct((rows, 9 * WINDOW), bf16),
        ),
        scratch_shapes=[pltpu.VMEM((BLOCK // 2, rows, PACK), f32)],
        compiler_params=params(24),
        cost_estimate=pl.CostEstimate(
            flops=2 * rows * 9 * WINDOW * GROUP, bytes_accessed=5 << 20, transcendentals=rows * GROUP
        ),
    )(before, own, after, band, *waits)


def shift_cells(field, step):
    if step == 0:
        return field
    column = lax.broadcasted_iota(jnp.int32, field.shape, 1)
    edge = LS - 1 if step > 0 else 0
    return jnp.where(column == edge, 0.0, pltpu.roll(field, (-step) % LS, 1))


def conv_two_kernel(planes, x_ref, w_ref, *refs):
    out_ref, token_ref, lhs_ref, v_ref = refs[-4:]
    token_ref[...] = jnp.zeros(token_ref.shape, f32)

    @pl.when(pl.program_id(0) == 0)
    def _():
        v_ref[:, :, 0] = jnp.zeros((3, 2, LS + 2, LS, PACK), f32)
        v_ref[:, :, planes + 1] = jnp.zeros((3, 2, LS + 2, LS, PACK), f32)
        edge = jnp.zeros((LS, PACK), f32)

        def spread(p, carry):
            x = x_ref[p].astype(f32)
            turned = pltpu.roll(x, C1, 1)
            for half, parts in enumerate(((x, turned), (turned, x))):
                cells = jnp.concatenate(parts, axis=0).reshape(LS, LS, PACK)
                for c in range(3):
                    v_ref[c, half, p + 1, 0] = edge
                    v_ref[c, half, p + 1, 1 : LS + 1] = shift_cells(cells, c - 1)
                    v_ref[c, half, p + 1, LS + 1] = edge
            return carry

        lax.fori_loop(0, planes, spread, 0)

        def gather(p, carry):
            rows = pl.ds(pl.multiple_of(p * CELLS, CELLS), CELLS)
            for m in range((TAPS + 1) // 2):
                t = 2 * m
                low = v_ref[t % 3, 0, p + t // 9, pl.ds((t // 3) % 3, LS)].reshape(CELLS, PACK)
                t = 2 * m + 1
                if t < TAPS:
                    high = v_ref[t % 3, 1, p + t // 9, pl.ds((t // 3) % 3, LS)].reshape(CELLS, PACK)
                    tile = jnp.where(low_lanes(low.shape), low, high)
                    lhs_ref[rows, m * PACK : (m + 1) * PACK] = tile.astype(bf16)
                else:
                    lhs_ref[rows, m * PACK : m * PACK + C1] = low[:, :C1].astype(bf16)
            return carry

        lax.fori_loop(0, planes, gather, 0)

    chunk = 4 * CELLS
    for m in range(planes * CELLS // chunk):
        rows = slice(m * chunk, (m + 1) * chunk)
        out_ref[rows] = jnp.dot(lhs_ref[rows], w_ref[...], preferred_element_type=f32).astype(bf16)


def conv_two(pieces, weight, after):
    planes = pieces.shape[0]
    cells = planes * CELLS
    block = 256
    return pl.pallas_call(
        lambda *refs: conv_two_kernel(planes, *refs),
        grid=(C2 // block,),
        in_specs=[
            pl.BlockSpec(pieces.shape, lambda n: (0, 0, 0)),
            pl.BlockSpec((TAPS * C1, block), lambda n: (0, n)),
        ]
        + [pl.BlockSpec(memory_space=pl.ANY)] * len(after),
        out_specs=(
            pl.BlockSpec((cells, block), lambda n: (0, n)),
            pl.BlockSpec((8, PACK), lambda n: (0, 0)),
        ),
        out_shape=(jax.ShapeDtypeStruct((cells, C2), bf16), jax.ShapeDtypeStruct((8, PACK), f32)),
        scratch_shapes=[
            pltpu.VMEM((cells, TAPS * C1), bf16),
            pltpu.VMEM((3, 2, planes + 2, LS + 2, LS, PACK), f32),
        ],
        compiler_params=params(56),
        cost_estimate=pl.CostEstimate(
            flops=2 * cells * TAPS * C1 * C2, bytes_accessed=10 << 20, transcendentals=0
        ),
    )(pieces, weight, *after)


def join_kernel(count, *refs):
    out_ref, first = refs[-1], 0
    for ref in refs[:count]:
        rows = ref.shape[0]
        out_ref[first : first + rows] = ref[...]
        first += rows


def joined(values, after=()):
    rows = sum(value.shape[0] for value in values)
    columns = values[0].shape[1]
    return pl.pallas_call(
        lambda *refs: join_kernel(len(values), *refs),
        grid=(1,),
        in_specs=[pl.BlockSpec(value.shape, lambda n: (0, 0)) for value in values]
        + [pl.BlockSpec(memory_space=pl.ANY)] * len(after),
        out_specs=pl.BlockSpec((rows, columns), lambda n: (0, 0)),
        out_shape=jax.ShapeDtypeStruct((rows, columns), values[0].dtype),
        compiler_params=params(32),
        cost_estimate=pl.CostEstimate(flops=0, bytes_accessed=4 * rows * columns, transcendentals=0),
    )(*values, *after)


def held_kernel(*refs):
    pass


def held(value, after):
    return pl.pallas_call(
        held_kernel,
        in_specs=[pl.BlockSpec(memory_space=pl.ANY)] * (1 + len(after)),
        out_specs=pl.BlockSpec(memory_space=pl.ANY),
        out_shape=jax.ShapeDtypeStruct(value.shape, value.dtype),
        input_output_aliases={0: 0},
        compiler_params=params(16),
    )(value, *after)


def plane_copies(device, pieces, refs, target_ref, base, sems):
    copies = []
    for differences, ref in zip(pieces, refs):
        for k, difference in enumerate(differences):
            row = pl.multiple_of(base + (device ^ difference) * CELLS, CELLS)
            source = ref.at[pl.ds(k * CELLS, CELLS), :]
            target = target_ref.at[pl.ds(row, CELLS), :]
            copies.append(pltpu.make_async_copy(source, target, sems.at[len(copies)]))
    return copies


def back_two_kernel(planes, pieces, device_ref, *refs):
    cot_refs = refs[: len(pieces)]
    w_ref, out_ref, cot_ref, sum_ref, sems = refs[len(pieces)], *refs[-4:]
    b = pl.program_id(0)
    cells = planes * CELLS

    @pl.when(b == 0)
    def _():
        copies = plane_copies(device_ref[0], pieces, cot_refs, cot_ref, CELLS, sems)
        for copy in copies:
            copy.start()
        cot_ref[:CELLS] = jnp.zeros((CELLS, C2), bf16)
        cot_ref[cells + CELLS :] = jnp.zeros((CELLS, C2), bf16)
        sum_ref[...] = jnp.zeros(sum_ref.shape, f32)
        for copy in copies:
            copy.wait()

    total = None
    for a in range(3):
        term = lax.dot_general(
            cot_ref[(2 - a) * CELLS : (2 - a) * CELLS + cells],
            w_ref[a],
            (((1,), (1,)), ((), ())),
            preferred_element_type=f32,
        )
        total = term if total is None else total + term
    rows = pl.ds(b, LS)
    first = total[:, :PACK].reshape(planes, LS, LS, PACK)
    sum_ref[0, :, rows] = sum_ref[0, :, rows] + first
    last = jnp.concatenate([total[:, PACK:], jnp.zeros((cells, C1), f32)], axis=1)
    sum_ref[1, :, rows] = sum_ref[1, :, rows] + last.reshape(planes, LS, LS, PACK)

    @pl.when(b == 2)
    def _():
        def finish(p, carry):
            pair = sum_ref[0, p, 1 : LS + 1]
            single = sum_ref[1, p, 1 : LS + 1]
            total = shift_cells(pair, 1) + shift_cells(single, -1)
            total = total.reshape(CELLS, PACK) + pltpu.roll(pair.reshape(CELLS, PACK), C1, 1)
            top, bottom = total[: CELLS // 2], total[CELLS // 2 :]
            out_ref[p] = jnp.where(low_lanes(top.shape), top, pltpu.roll(bottom, C1, 1)).astype(bf16)
            return carry

        lax.fori_loop(0, planes, finish, 0)


def back_two(device, pieces, cots, weight, after):
    planes = sum(len(piece) for piece in pieces)
    return pl.pallas_call(
        lambda *refs: back_two_kernel(planes, pieces, *refs),
        grid_spec=pltpu.PrefetchScalarGridSpec(
            num_scalar_prefetch=1,
            grid=(3,),
            in_specs=[pl.BlockSpec(memory_space=pl.ANY)] * len(cots)
            + [pl.BlockSpec((3, 3 * C1, C2), lambda n, s: (0, n, 0))]
            + [pl.BlockSpec(memory_space=pl.ANY)] * len(after),
            out_specs=pl.BlockSpec((planes, CELLS // 2, PACK), lambda n, s: (0, 0, 0)),
            scratch_shapes=[
                pltpu.VMEM(((planes + 2) * CELLS, C2), bf16),
                pltpu.VMEM((2, planes, LS + 2, LS, PACK), f32),
                pltpu.SemaphoreType.DMA((planes,)),
            ],
        ),
        out_shape=jax.ShapeDtypeStruct((planes, CELLS // 2, PACK), bf16),
        compiler_params=params(56),
        cost_estimate=pl.CostEstimate(
            flops=2 * planes * CELLS * TAPS * C1 * C2, bytes_accessed=6 << 20, transcendentals=0
        ),
    )(device, *cots, weight.reshape(3, 9 * C1, C2), *after)


def weight_two_kernel(planes, pieces, scale, based, device_ref, field_ref, *refs):
    cot_refs = refs[: len(pieces)]
    base_ref = refs[len(pieces)]
    out_ref, token_ref, cot_ref, flat_ref, lhs_ref, sems = refs[-6:]
    cells = planes * CELLS
    a = pl.program_id(0)

    @pl.when(a == 0)
    def _():
        copies = plane_copies(device_ref[0], pieces, cot_refs, cot_ref, CELLS, sems)
        for copy in copies:
            copy.start()
        cot_ref[:CELLS] = jnp.zeros((CELLS, C2), bf16)
        cot_ref[cells + CELLS :] = jnp.zeros((CELLS, C2), bf16)

        def cells_of(p):
            x = field_ref[p].astype(f32)
            return jnp.concatenate([x, pltpu.roll(x, C1, 1)], axis=0)

        for j in range(planes // 2):
            pair = jnp.concatenate([cells_of(2 * j), cells_of(2 * j + 1)], axis=0)
            flat_ref[:, j * PACK : (j + 1) * PACK] = pair.T[:C1]

        lane = lax.broadcasted_iota(jnp.int32, (1, cells), 1)
        row, column = (lane // LS) % LS, lane % LS
        for b in range(3):
            for c in range(3):
                inside = (row + b >= 1) & (row + b <= LS) & (column + c >= 1) & (column + c <= LS)
                mask = inside.astype(f32)
                shift = (-(LS * (b - 1) + c - 1)) % cells
                t = 3 * b + c
                value = flat_ref[...]
                if shift:
                    value = pltpu.roll(value, shift, 1) * mask
                lhs_ref[t * C1 : (t + 1) * C1] = value.astype(bf16)
        for copy in copies:
            copy.wait()

    rows = pl.ds(pl.multiple_of((2 - a) * CELLS, CELLS), cells)
    total = jnp.dot(lhs_ref[...], cot_ref[rows], preferred_element_type=f32) * scale
    out_ref[...] = total + base_ref[...] if based else total
    token_ref[...] = jnp.zeros(token_ref.shape, f32)


def weight_two(device, field, pieces, cots, scale, base, after):
    planes = field.shape[0]
    cells = planes * CELLS
    block = 9 * C1
    extra = ([] if base is None else [base]) + list(after)
    extra_specs = [pl.BlockSpec(memory_space=pl.ANY)] * len(after)
    if base is not None:
        extra_specs = [pl.BlockSpec((block, C2), lambda n, s: (n, 0))] + extra_specs
    return pl.pallas_call(
        lambda *refs: weight_two_kernel(planes, pieces, scale, base is not None, *refs),
        grid_spec=pltpu.PrefetchScalarGridSpec(
            num_scalar_prefetch=1,
            grid=(3,),
            in_specs=[pl.BlockSpec(field.shape, lambda n, s: (0, 0, 0))]
            + [pl.BlockSpec(memory_space=pl.ANY)] * len(cots)
            + extra_specs,
            out_specs=(
                pl.BlockSpec((block, C2), lambda n, s: (n, 0)),
                pl.BlockSpec((8, PACK), lambda n, s: (0, 0)),
            ),
            scratch_shapes=[
                pltpu.VMEM(((planes + 2) * CELLS, C2), bf16),
                pltpu.VMEM((C1, cells), f32),
                pltpu.VMEM((block, cells), bf16),
                pltpu.SemaphoreType.DMA((planes,)),
            ],
        ),
        out_shape=(
            jax.ShapeDtypeStruct((TAPS * C1, C2), f32),
            jax.ShapeDtypeStruct((8, PACK), f32),
        ),
        input_output_aliases={} if base is None else {2 + len(cots): 0},
        compiler_params=params(60 if base is None else 48),
        cost_estimate=pl.CostEstimate(
            flops=2 * cells * TAPS * C1 * C2, bytes_accessed=12 << 20, transcendentals=0
        ),
    )(device, field, *cots, *extra)


def grad_pre_kernel(pieces_ref, slope_ref, lhs_ref, *refs):
    grad_ref, partial_ref, spread_ref, packed_ref = refs[-4:]
    for r in range(BLOCK):
        for u in range(BLOCK // 2):
            piece = r * BLOCK + 2 * u
            first = pieces_ref[piece].astype(f32)
            second = pieces_ref[piece + 1].astype(f32)
            low = low_lanes(first.shape)
            top = jnp.where(low, first, pltpu.roll(second, C1, 1))
            bottom = jnp.where(low, pltpu.roll(first, C1, 1), second)
            for i in range(LS):
                source = top if i < LS // 2 else bottom
                start = (i % (LS // 2)) * LS
                spread_ref[u, pl.ds(BLOCK * i + r, LS, stride=LAT), :] = source[start : start + LS]
    grads = []
    for u in range(BLOCK // 2):
        lanes = slice(u * PACK, (u + 1) * PACK)
        value = (spread_ref[u] * slope_ref[:, lanes]).astype(bf16)
        grad_ref[:, lanes] = value
        grads.append(value)
    grad = jnp.concatenate(grads, axis=1)
    for lateral in range(9):
        window = lhs_ref[:, lateral * WINDOW : (lateral + 1) * WINDOW]
        product = lax.dot_general(window, grad, (((0,), (0,)), ((), ())), preferred_element_type=f32)
        for c in range(3):
            sums = []
            for parity in range(2):
                part = None
                for pair in range(BLOCK // 2):
                    column = 2 * pair + parity + c - 1
                    slot = column if column >= 0 else BLOCK + 1
                    term = product[slot * C1 : (slot + 1) * C1, pair * PACK : (pair + 1) * PACK]
                    part = term if part is None else part + term
                sums.append(part)
            total = sums[0] + pltpu.roll(sums[1], C1, 1)
            top, bottom = total[: C1 // 2], total[C1 // 2 :]
            t = 3 * lateral + c
            packed_ref[t * (C1 // 2) : (t + 1) * (C1 // 2)] = jnp.where(
                low_lanes(top.shape), top, pltpu.roll(bottom, C1, 1)
            )
    packed_ref[TAPS * (C1 // 2) :] = jnp.zeros(((32 - TAPS) * (C1 // 2), PACK), f32)
    for row in range(C1 // 2):
        entry = packed_ref[pl.ds(row, 32, stride=C1 // 2), :]
        partial_ref[row] = entry.astype(bf16)


def grad_pre_of(pieces, slope, lhs, after):
    rows = LS * LAT
    whole = pl.BlockSpec(memory_space=pltpu.VMEM)
    return pl.pallas_call(
        grad_pre_kernel,
        in_specs=[whole] * 3 + [pl.BlockSpec(memory_space=pl.ANY)] * len(after),
        out_shape=(
            jax.ShapeDtypeStruct((rows, GROUP), bf16),
            jax.ShapeDtypeStruct((C1 // 2, 32, PACK), bf16),
        ),
        scratch_shapes=[
            pltpu.VMEM((BLOCK // 2, rows, PACK), f32),
            pltpu.VMEM((32 * (C1 // 2), PACK), f32),
        ],
        compiler_params=params(24),
        cost_estimate=pl.CostEstimate(
            flops=2 * rows * 9 * WINDOW * GROUP, bytes_accessed=3 << 20, transcendentals=0
        ),
    )(pieces, slope, lhs, *after)


def back_one_kernel(before_ref, own_ref, after_ref, w_ref, out_ref, lhs_ref):
    for a, ref in enumerate((before_ref, own_ref, after_ref)):
        write_windows(lhs_ref, a, [ref[g * LAT : (g + 1) * LAT].astype(f32) for g in range(LS)])
    result = jnp.dot(lhs_ref[...], w_ref[...], preferred_element_type=f32)
    for g in range(LS):
        out_ref[:, g * GROUP : (g + 1) * GROUP] = result[g * LAT : (g + 1) * LAT].astype(bf16)


def back_one(before, own, after, band):
    rows = LS * LAT
    return pl.pallas_call(
        back_one_kernel,
        out_shape=jax.ShapeDtypeStruct((LAT, LAT * C1), bf16),
        scratch_shapes=[pltpu.VMEM((rows, 9 * WINDOW), bf16)],
        compiler_params=params(24),
        cost_estimate=pl.CostEstimate(
            flops=2 * rows * 9 * WINDOW * GROUP, bytes_accessed=3 << 20, transcendentals=0
        ),
    )(before, own, after, band)


def sum_kernel(scale, shares_ref, *refs):
    out_ref = refs[-1]
    total = jnp.sum(shares_ref[...].astype(f32), axis=0) * scale
    out_ref[...] = jnp.broadcast_to(total.astype(bf16)[None], out_ref.shape)


def sum_shares(shares, scale, after):
    whole = pl.BlockSpec(memory_space=pltpu.VMEM)
    return pl.pallas_call(
        lambda *refs: sum_kernel(scale, *refs),
        in_specs=[whole] + [pl.BlockSpec(memory_space=pl.ANY)] * len(after),
        out_shape=jax.ShapeDtypeStruct(shares.shape, bf16),
        compiler_params=params(16),
        cost_estimate=pl.CostEstimate(flops=0, bytes_accessed=1 << 20, transcendentals=0),
    )(shares, *after)


def unpack_kernel(packed_ref, *refs):
    out_ref, wide_ref = refs[-2:]
    wide_ref[...] = packed_ref[...].astype(f32).reshape(wide_ref.shape)
    for t in range(TAPS):
        entry = wide_ref[pl.ds(t, C1 // 2, stride=32), :]
        out_ref[t] = jnp.concatenate([entry[:, :C1], entry[:, C1:]], axis=0)


def unpack(packed, after):
    whole = pl.BlockSpec(memory_space=pltpu.VMEM)
    return pl.pallas_call(
        unpack_kernel,
        in_specs=[whole] + [pl.BlockSpec(memory_space=pl.ANY)] * len(after),
        out_shape=jax.ShapeDtypeStruct((TAPS, C1, C1), f32),
        scratch_shapes=[pltpu.VMEM((32 * (C1 // 2), PACK), f32)],
        compiler_params=params(16),
        cost_estimate=pl.CostEstimate(flops=0, bytes_accessed=1 << 20, transcendentals=0),
    )(packed, *after)


def neighbours(value, axis):
    count = lax.axis_size(axis)
    before = lax.ppermute(value, axis, [(i, i + 1) for i in range(count - 1)])
    after = lax.ppermute(value, axis, [(i + 1, i) for i in range(count - 1)])
    return before, after


def flipped(value, difference):
    count = lax.axis_size("depth")
    return lax.ppermute(value, "depth", [(i, i ^ difference) for i in range(count)])


def over_samples(value):
    count = lax.axis_size("sample")
    return [value] + [
        lax.ppermute(value, "sample", [(i, (i + shift) % count) for i in range(count)])
        for shift in range(1, count)
    ]


def on_device(volume, conv1_weight, conv2_weight, cotangent):
    samples = lax.axis_size("sample")
    shards = lax.axis_size("depth")
    flat_two = conv2_weight.reshape(TAPS * C1, C2)
    own = volume.reshape(LAT, LAT * C1)
    device = lax.axis_index("depth").astype(jnp.int32).reshape(1)
    cot = cotangent.reshape(CELLS, C2)

    core, chip = 1, 2
    outer = list(range(4, shards, 4))
    far = [flipped(cot, difference) for difference in outer]
    before, after = neighbours(own, "depth")
    cot_chip = flipped(cot, chip)

    back_weight = jnp.swapaxes(conv1_weight[::-1], 1, 2)
    band = banded(conv1_weight)
    back_band = banded(back_weight)

    moved, slope, windows = conv_one(before, own, after, band, [])
    fields = lax.all_to_all(moved, "depth", split_axis=0, concat_axis=0, tiled=True)

    near = joined([cot, cot_chip], [fields])
    far = joined(far, [slope, cot_chip])
    far_chip = flipped(far, chip)
    cots = [near, far, far_chip]
    pieces = [[0, chip], outer, [difference + chip for difference in outer]]
    pieces = pieces + [[difference + core for difference in piece] for piece in pieces]

    near_core, far_core = flipped(near, core), flipped(far, core)
    partial, done = conv_two(fields, flat_two, [near_core, far_core])
    features = lax.psum_scatter(partial, "depth", scatter_dimension=0, tiled=True)

    own_cots = cots + [near_core, far_core, flipped(far_chip, core)]
    grad_pieces = back_two(device, pieces, own_cots, flat_two, [done])
    returned = lax.all_to_all(grad_pieces, "depth", split_axis=0, concat_axis=0, tiled=True)
    scale_two = 1.0 / math.sqrt(samples * shards * CELLS)
    grad_conv2, token = weight_two(
        device, fields, pieces, own_cots, scale_two, None, [grad_pieces]
    )
    all_fields = over_samples(fields)
    grad_pre, partial_one = grad_pre_of(returned, slope, windows, [token] + all_fields[1:])
    half = joined(cots, [done])
    halves = [[difference for piece in group for difference in piece] for group in (pieces[:3], pieces[3:])]
    all_pieces, all_cots = [pieces], [own_cots]
    for value in over_samples(half)[1:]:
        value = held(value, [grad_pre])
        all_pieces.append(halves)
        all_cots.append([value, flipped(value, core)])

    grad_before, grad_after = neighbours(grad_pre, "depth")

    devices = samples * shards
    both = ("sample", "depth")
    scale_one = 1.0 / math.sqrt(samples * shards * LAT * LAT)
    shares = partial_one.reshape(devices, -1, PACK)
    shares = lax.all_to_all(shares, both, split_axis=0, concat_axis=0, tiled=True)
    for k in range(1, samples):
        grad_conv2, token = weight_two(
            device, all_fields[k], all_pieces[k], all_cots[k], scale_two, grad_conv2, [grad_pre]
        )
    summed = sum_shares(shares, scale_one, [token])
    shares = lax.all_to_all(summed, both, split_axis=0, concat_axis=0, tiled=True)
    grad_volume = back_one(grad_before, grad_pre, grad_after, back_band)
    grad_conv1 = unpack(shares.reshape(C1 // 2, 32, PACK), [])

    return (
        features.reshape(cotangent.shape),
        grad_volume.reshape(volume.shape),
        grad_conv1,
        grad_conv2.reshape(conv2_weight.shape),
    )


def solution(mesh):
    return jax.shard_map(
        on_device,
        mesh=mesh,
        in_specs=(
            P("sample", "depth", None, None),
            P(),
            P(None, "depth", None),
            P("sample", "depth", None, None, None),
        ),
        out_specs=(
            P("sample", "depth", None, None, None),
            P("sample", "depth", None, None),
            P(),
            P(None, "depth", None),
        ),
        check_vma=False,
    )
```
